32 devices in a mesh: lon: 2 (over x), lat: 4 (over z), head: 4 (over y, core).
Axes of the slice: x: 2, y: 2, z: 4, core: 2. Of those that a mesh axis runs over, the one named last changes fastest.
Arguments:
- tokens: bfloat16 [2, 24, 48, 1024], P(None, 'lat', 'lon'), may hold values from -6 to 6
- norm_gain: float32 [1024], replicated, may hold values from 0.5 to 1.5
- w_qkv: bfloat16 [1024, 3072], P(None, 'head'), may hold values from -0.1875 to 0.1875
- w_out: bfloat16 [1024, 1024], P('head'), may hold values from -0.1875 to 0.1875
- bias_table: float32 [759, 16], P(None, 'head'), may hold values from -3 to 300
- cotangent: bfloat16 [2, 24, 48, 1024], P(None, 'lat', 'lon'), may hold values from -6 to 6
Outputs:
- layer_out: bfloat16 [2, 24, 48, 1024], P(None, 'lat', 'lon')
- grad_tokens: bfloat16 [2, 24, 48, 1024], P(None, 'lat', 'lon')
- grad_qkv: float32 [1024, 3072], P(('lon', 'lat'), 'head')
- grad_out: float32 [1024, 1024], P('head', ('lon', 'lat'))
The draws below stay inside these ranges and needn't reach their ends.
All inputs are finite; a program needn't handle non-finite values.
Results may differ from the reference program's by a relative error of at most 0.013.
Values may be sent and summed in bfloat16 or wider, within the bound.
No kernel may reach another device: no remote copies, remote signals or barrier semaphores. Data moves between devices by JAX's collectives and lax.ppermute only.
A program may use at most 64 MiB of HBM per device.

```python
import jax
import jax.numpy as jnp
from jax import lax

D = 1024
HEADS = 16
HEAD_DIM = 64
LEV = 2
WLAT = 6
WLON = 12
NLAT = 24
NLON = 48
NREL = 759
N_HEAD = 4


def draw_bias_table(key, part):
    key = jax.random.fold_in(key, 7)
    table_shape = (NREL, HEADS)
    values = jnp.clip(jax.random.normal(key, table_shape, jnp.float32), -3.0, 3.0)
    return values


def strengthened(values, rng, source, target, parts, factor):
    def block_of(position):
        return (jnp.arange(values.shape[position]) // (values.shape[position] // parts)).reshape((-1,) + (1,) * (values.ndim - 1 - position))

    first = jax.random.permutation(rng, parts)[block_of(target)]
    far = (block_of(target) + parts // 2) % parts
    return jnp.where((block_of(source) == first) | (block_of(source) == far), factor * values, values)


def block_levels(key, extent, cuts, smallest, largest):
    level = 1.0
    for dim, parts in cuts:
        steps = jax.random.uniform(jax.random.fold_in(jax.random.fold_in(key, 6), dim), (parts,), jnp.float32, smallest / len(cuts), largest / len(cuts))
        level = level * jnp.repeat(jnp.exp(steps), extent[dim] // parts).reshape((-1,) + (1,) * (len(extent) - 1 - dim))
    return level


def gaussian(key, shape, spread, limit, shards=(), kind=jnp.bfloat16):
    drawn = spread * jax.random.normal(key, shape, jnp.float32)
    if shards:
        drawn = drawn * block_levels(key, shape, shards, -0.22, 0.18)
    return jnp.clip(drawn, -limit, limit).astype(kind)


def noise_with(own_key, extent, spread, limit, pieces, heavy, held_as=jnp.bfloat16):
    array = spread * jax.random.normal(own_key, extent, jnp.float32)
    if pieces:
        array = array * block_levels(own_key, extent, pieces, -0.22, 0.18)
    return jnp.clip(strengthened(array, jax.random.fold_in(own_key, 3), *heavy), -limit, limit).astype(held_as)


def setup_inputs(seed: int = 0) -> dict:
    streams_of = jax.random.split(jax.random.key(seed), 7)
    tokens = gaussian(streams_of[0], (LEV, NLAT, NLON, D), 1.0, 6.0, ((1, 4), (2, 2)))
    norm_gain = jnp.clip(1.0 + 0.1 * jax.random.normal(streams_of[1], (D,), jnp.float32), 0.5, 1.5)
    w_qkv = gaussian(streams_of[2], (D, 3 * D), D ** -0.5, 0.1875, ((1, 4),))
    w_out = gaussian(streams_of[3], (D, D), D ** -0.5, 0.1875, ((0, 4),))
    bias_table = draw_bias_table(jax.random.fold_in(streams_of[6], 71), 0)
    cotangent = noise_with(streams_of[5], (LEV, NLAT, NLON, D), 1.0, 6.0, ((1, 4), (2, 2)), (2, 3, 2, 2.0))
    return {"tokens": tokens, "norm_gain": norm_gain, "w_qkv": w_qkv, "w_out": w_out, "bias_table": bias_table, "cotangent": cotangent}


EPSILON = 1e-05
NEG_FILL = -1e+30

def normalize(values, norm_gain):
    floats = values.astype(jnp.float32)
    center = floats - lax.optimization_barrier(jnp.mean(floats, axis=-1, keepdims=True))
    inverse = lax.rsqrt(lax.optimization_barrier(jnp.mean(center * center, axis=-1, keepdims=True)) + EPSILON)
    scaled = center * inverse
    return ((scaled * norm_gain).astype(jnp.bfloat16), scaled, inverse)

def relative_index():
    window_size = LEV * WLAT * WLON
    cell_idx = jnp.arange(window_size, dtype=jnp.int32)
    level_pos = cell_idx // (WLAT * WLON)
    lat_pos = cell_idx // WLON % WLAT
    lon_pos = cell_idx % WLON
    span_lat = 2 * WLAT - 1
    span_lon = 2 * WLON - 1
    return ((level_pos[:, None] - level_pos[None, :] + LEV - 1) * span_lat * span_lon + (lat_pos[:, None] - lat_pos[None, :] + WLAT - 1) * span_lon + lon_pos[:, None] - lon_pos[None, :] + WLON - 1).astype(jnp.int32)

def to_windows(field):
    level_count, lat_count, lon_count, channels = field.shape
    split = field.reshape(level_count, lat_count // WLAT, WLAT, lon_count // WLON, WLON, channels)
    return split.transpose(1, 3, 0, 2, 4, 5).reshape(lat_count // WLAT, lon_count // WLON, level_count * WLAT * WLON, channels)

def from_windows(blocks, level_count):
    lat_blocks, lon_blocks, window_size, channels = blocks.shape
    split = blocks.reshape(lat_blocks, lon_blocks, level_count, WLAT, WLON, channels)
    return split.transpose(2, 0, 3, 1, 4, 5).reshape(level_count, lat_blocks * WLAT, lon_blocks * WLON, channels)

def attend(query_part, key_part, value_part, grad_part, rel_bias, allowed):
    scale = HEAD_DIM ** (-0.5)
    query_f = query_part.astype(jnp.float32)
    key_f = key_part.astype(jnp.float32)
    value_f = value_part.astype(jnp.float32)
    grad_f = grad_part.astype(jnp.float32)
    scores = jnp.einsum('wqhe,wkhe->whqk', query_f, key_f) * scale + rel_bias[None]
    scores = jnp.where(allowed[:, None], scores, NEG_FILL)
    peak = lax.optimization_barrier(jnp.max(scores, axis=-1, keepdims=True))
    raised = jnp.exp(scores - peak)
    prob_full = raised / lax.optimization_barrier(jnp.sum(raised, axis=-1, keepdims=True))
    prob_half = prob_full.astype(jnp.bfloat16)
    prob_back = prob_half.astype(jnp.float32)
    attended = jnp.einsum('whqk,wkhe->wqhe', prob_back, value_f).astype(jnp.bfloat16)
    grad_prob = jnp.einsum('wqhe,wkhe->whqk', grad_f, value_f)
    row_term = lax.optimization_barrier(jnp.sum(prob_full * grad_prob, axis=-1, keepdims=True))
    grad_score = (prob_full * (grad_prob - row_term) * scale).astype(jnp.bfloat16).astype(jnp.float32)
    grad_query = jnp.einsum('whqk,wkhe->wqhe', grad_score, key_f)
    grad_key = jnp.einsum('whqk,wqhe->wkhe', grad_score, query_f)
    grad_value = jnp.einsum('whqk,wqhe->wkhe', prob_back, grad_f)
    return (attended, jnp.stack([grad_query, grad_key, grad_value], axis=3).astype(jnp.bfloat16))

def rounded(values):
    return lax.optimization_barrier(values.astype(jnp.bfloat16)).astype(jnp.float32)

def reference(tokens, norm_gain, w_qkv, w_out, bias_table, cotangent):
    cells = LEV * NLAT * NLON
    shift_lat = WLAT // 2
    shift_lon = WLON // 2
    window_size = LEV * WLAT * WLON
    flat_tokens = tokens.reshape(cells, D)
    flat_grad = cotangent.reshape(cells, D)
    normed, scaled, inverse = normalize(flat_tokens, norm_gain)
    projected = jnp.dot(normed, w_qkv, preferred_element_type=jnp.float32).astype(jnp.bfloat16)
    d_attended = jnp.dot(flat_grad, w_out.T, preferred_element_type=jnp.float32).astype(jnp.bfloat16)
    joined = jnp.concatenate([projected, d_attended], axis=1).reshape(LEV, NLAT, NLON, 4 * D)
    rolled = jnp.roll(joined, (-shift_lat, -shift_lon), axis=(1, 2))
    blocks = to_windows(rolled)
    rel_bias = jnp.transpose(bias_table[relative_index()], (2, 0, 1))
    lat_pos = jnp.arange(window_size, dtype=jnp.int32) // WLON % WLAT

    def one_row(inputs):
        row_idx, row_blocks = inputs
        initial = (row_idx * WLAT + lat_pos + shift_lat) % NLAT
        allowed = jnp.abs(initial[:, None] - initial[None, :]) < WLAT
        lon_count = row_blocks.shape[0]
        qkv_part = row_blocks[:, :, :3 * D].reshape(lon_count, window_size, HEADS, 3, HEAD_DIM)
        grad_part = row_blocks[:, :, 3 * D:].reshape(lon_count, window_size, HEADS, HEAD_DIM)
        attended, dstack = attend(qkv_part[:, :, :, 0], qkv_part[:, :, :, 1], qkv_part[:, :, :, 2], grad_part, rel_bias, allowed[None])
        return jnp.concatenate([attended.reshape(lon_count, window_size, D), dstack.reshape(lon_count, window_size, 3 * D)], axis=2)
    results = lax.map(one_row, (jnp.arange(NLAT // WLAT, dtype=jnp.int32), blocks))
    restored = jnp.roll(from_windows(results, LEV), (shift_lat, shift_lon), axis=(1, 2)).reshape(cells, 4 * D)
    attended = restored[:, :D]
    dqkv = restored[:, D:]
    group_width = D // N_HEAD
    attn_total = jnp.zeros((cells, D), jnp.float32)
    dnormed = jnp.zeros((cells, D), jnp.float32)
    for group_idx in range(N_HEAD):
        first_col = group_idx * group_width
        out_term = jnp.dot(attended[:, first_col:first_col + group_width], w_out[first_col:first_col + group_width], preferred_element_type=jnp.float32)
        attn_total = attn_total + rounded(out_term)
        wide_first = 3 * first_col
        in_term = jnp.dot(dqkv[:, wide_first:wide_first + 3 * group_width], w_qkv[:, wide_first:wide_first + 3 * group_width].T, preferred_element_type=jnp.float32)
        dnormed = dnormed + rounded(in_term)
    layer_out = (flat_tokens.astype(jnp.float32) + attn_total).astype(jnp.bfloat16)
    grad_qkv = jnp.dot(normed.T, dqkv, preferred_element_type=jnp.float32)
    grad_out = jnp.dot(attended.T, flat_grad, preferred_element_type=jnp.float32)
    scaled_grad = dnormed * norm_gain
    mean_grad = lax.optimization_barrier(jnp.mean(scaled_grad, axis=-1, keepdims=True))
    mean_mixed = lax.optimization_barrier(jnp.mean(scaled_grad * scaled, axis=-1, keepdims=True))
    grad_tokens = (flat_grad.astype(jnp.float32) + (scaled_grad - mean_grad - scaled * mean_mixed) * inverse).astype(jnp.bfloat16)
    return (layer_out.reshape(LEV, NLAT, NLON, D), grad_tokens.reshape(LEV, NLAT, NLON, D), grad_qkv, grad_out)
```

```python
import functools

import jax
import jax.numpy as jnp
import numpy as np
from jax import lax
from jax.experimental import pallas as pl
from jax.experimental.pallas import tpu as pltpu
from jax.sharding import PartitionSpec as P

HEAD_DIM = 64
LEV = 2
WLAT = 6
WLON = 12
TILE_LON = 24
WINDOW = LEV * WLAT * WLON
WINDOWS = TILE_LON // WLON
CELLS = WINDOWS * WINDOW
QUARTERS = 4
PART = 80
MID_LAT = WLAT // 2
MID_LON = WLON // 2
SPAN_LAT = 2 * WLAT - 1
SPAN_LON = 2 * WLON - 1
EPSILON = 1e-05
NEG_FILL = -1e30
F32 = jnp.float32
BF16 = jnp.bfloat16

RIM_Z, RIM_X, RIM_D = 112, 48, 48
RIM = RIM_Z + RIM_X + RIM_D
OUT_OWN, OUT_Z, OUT_X, OUT_D = 32, 32, 16, 16
OUT_STARTS = (0, 32, 64, 80)
OUT_ROWS = 96


def own_row(level, lat, lon):
    return (level * WLAT + lat) * TILE_LON + lon


def rim_source():
    rows = np.full(RIM, -1)
    z_width = TILE_LON - MID_LON
    for level in range(LEV):
        for lat in range(MID_LAT):
            for lon in range(z_width):
                rows[(level * MID_LAT + lat) * z_width + lon] = own_row(level, lat, lon + MID_LON)
            for lon in range(MID_LON):
                at = (level * MID_LAT + lat) * MID_LON + lon
                rows[RIM_Z + at] = own_row(level, lat + MID_LAT, lon)
                rows[RIM_Z + RIM_X + at] = own_row(level, lat, lon)
    return rows


def window_cells():
    cells = []
    for window in range(WINDOWS):
        for quarter in range(QUARTERS):
            for lat in range(WLAT):
                for half in range(2):
                    for third in range(3):
                        lon = half * MID_LON + (quarter % 2) * 3 + third
                        cells.append((window, quarter // 2, lat, lon))
    return cells


CELL_LIST = window_cells()
CELL_AT = {cell: at for at, cell in enumerate(CELL_LIST)}


def shifted_source():
    z_width = TILE_LON - MID_LON
    rows = []
    for window, level, lat, lon in CELL_LIST:
        column = window * WLON + lon + MID_LON
        if lat < MID_LAT and column < TILE_LON:
            rows.append(own_row(level, lat + MID_LAT, column))
        elif column < TILE_LON:
            rows.append(CELLS + (level * MID_LAT + lat - MID_LAT) * z_width + column - MID_LON)
        else:
            base = CELLS + RIM_Z + (RIM_X if lat >= MID_LAT else 0)
            rows.append(base + (level * MID_LAT + lat % MID_LAT) * MID_LON + column - TILE_LON)
    return np.array(rows)


def quarter_cells(quarter):
    groups = [[], [], [], []]
    for cell in CELL_LIST:
        window, level, lat, lon = cell
        if level != quarter // 2 or lon % MID_LON // 3 != quarter % 2:
            continue
        beyond = window * WLON + lon + MID_LON >= TILE_LON
        groups[2 * beyond + (lat >= MID_LAT)].append(cell)
    return groups


def one_hot(rows, count):
    picked = np.zeros((len(rows), count), np.float32)
    for at, row in enumerate(rows):
        if row >= 0:
            picked[at, row] = 1.0
    return picked.astype(BF16)


def quarter_pick():
    rows = []
    for quarter in range(QUARTERS):
        cells = sum(quarter_cells(quarter), [])
        rows += [CELL_AT[cell] for cell in cells] + [-1] * (PART - len(cells))
    return one_hot(rows, CELLS)


def group_pick():
    rows = []
    start = 0
    for group, padded in zip(quarter_cells(0), (OUT_OWN, OUT_Z, OUT_X, OUT_D)):
        rows += list(range(start, start + len(group))) + [-1] * (padded - len(group))
        start += len(group)
    return one_hot(rows, PART)


def own_pick():
    place = {}
    for quarter in range(QUARTERS):
        for start, group in zip(OUT_STARTS, quarter_cells(quarter)):
            for at, (window, level, lat, lon) in enumerate(group):
                column = (window * WLON + lon + MID_LON) % TILE_LON
                row = own_row(level, (lat + MID_LAT) % WLAT, column)
                place[row] = quarter * OUT_ROWS + start + at
    return one_hot([place[row] for row in range(CELLS)], QUARTERS * OUT_ROWS)


def bias_rows():
    rows = []
    for window, level, lat, lon in CELL_LIST[:WINDOW]:
        rows.append((level * WLAT + lat) * 16 + WLON - 1 - lon)
    single = one_hot(rows, LEV * WLAT * 16)
    return np.concatenate([single] * 3, axis=1)


def bias_columns():
    return np.array(
        [
            [
                SPAN_LAT * SPAN_LON * (LEV - 1 - level)
                + SPAN_LON * (WLAT - 1 - lat)
                + 2 * (WLON - 1)
                - lon
                for _, level, lat, lon in CELL_LIST[:WINDOW]
            ]
        ],
        np.int32,
    )


def pole_mask():
    side = np.array([lat < MID_LAT for _, _, lat, _ in CELL_LIST[:WINDOW]])
    return np.where(side[:, None] == side[None, :], 0.0, NEG_FILL).astype(np.float32)


def dot(left, right):
    return lax.dot_general(left, right, (((1,), (0,)), ((), ())), preferred_element_type=F32)


def dot_rows(left, right):
    return lax.dot_general(left, right, (((1,), (1,)), ((), ())), preferred_element_type=F32)


def dot_columns(left, right):
    return lax.dot_general(left, right, (((0,), (0,)), ((), ())), preferred_element_type=F32)


def call(kernel, outs, scratch=(), cost=None, name=None):
    return pl.pallas_call(
        kernel,
        out_shape=outs,
        scratch_shapes=scratch,
        name=name,
        cost_estimate=cost,
        compiler_params=pltpu.CompilerParams(vmem_limit_bytes=48 * 1024 * 1024),
    )


def cost(flops, moved):
    return pl.CostEstimate(flops=flops, bytes_accessed=moved, transcendentals=0)


def pack_kernel(pick, tokens, cotangent, rim_z, rim_x, rim_d):
    core = lax.rem(lax.axis_index("head"), 2)
    source = jnp.where(core == 0, tokens[...], cotangent[...])
    rim = dot(pick[...], source).astype(BF16)
    rim_z[...] = rim[:RIM_Z]
    rim_x[...] = rim[RIM_Z : RIM_Z + RIM_X]
    rim_d[...] = rim[RIM_Z + RIM_X :]


def bias_kernel(table, columns, rows, mask, bias, shifted, parts):
    heads = bias.shape[0]
    width = shifted.shape[1]
    for head in range(heads):
        spread = jnp.broadcast_to(table[head : head + 1, :], (16, table.shape[1]))
        rolled = pltpu.roll(spread, 0, 1, stride=1, stride_axis=0)[:, :width]
        high = rolled.astype(BF16)
        rest = rolled - high.astype(F32)
        middle = rest.astype(BF16)
        low = (rest - middle.astype(F32)).astype(BF16)
        for split, value in enumerate((high, middle, low)):
            shifted[(head * 3 + split) * 16 : (head * 3 + split + 1) * 16, :] = value
    place = lax.broadcasted_iota(jnp.int32, (width, WINDOW), 0)
    count = LEV * WLAT * 16
    for level in range(LEV):
        for lat in range(WLAT):
            offset = SPAN_LAT * SPAN_LON * level + SPAN_LON * lat
            wanted = (place == columns[...] + offset).astype(F32).astype(BF16)
            block = dot(shifted[...], wanted).astype(BF16)
            start = (level * WLAT + lat) * 16
            for head in range(heads):
                for split in range(3):
                    first = (head * 3 + split) * 16
                    parts[head, split * count + start : split * count + start + 16, :] = block[
                        first : first + 16
                    ]
    last = lax.axis_index("lat") == lax.axis_size("lat") - 1
    added = jnp.where(last, mask[...], 0.0)
    for head in range(heads):
        bias[head] = dot(rows[...], parts[head]) + added


def scaled_rows(values):
    floats = values.astype(F32)
    center = floats - jnp.mean(floats, axis=-1, keepdims=True)
    inverse = lax.rsqrt(jnp.mean(center * center, axis=-1, keepdims=True) + EPSILON)
    return center * inverse, inverse


def layer_kernel(
    lon_count,
    tokens,
    cotangent,
    rim_here,
    rim_there,
    gain,
    w_qkv,
    w_out,
    bias,
    shift_pick,
    quarter,
    *refs,
):
    grads = refs[:lon_count]
    parts = refs[lon_count : lon_count + QUARTERS]
    part_tokens, part_cotangent = refs[lon_count + QUARTERS : lon_count + QUARTERS + 2]
    source, near_tokens, near_grad, normed, projected, d_attended, merged, terms, whole = refs[
        lon_count + QUARTERS + 2 :
    ]
    head_index = lax.axis_index("head")
    core = lax.rem(head_index, 2)
    heads = bias.shape[0]
    group = heads * HEAD_DIM
    source[CELLS:, :] = jnp.where(core == 0, rim_here[...], rim_there[...])
    source[:CELLS, :] = tokens[...]
    near_tokens[...] = dot(shift_pick[...], source[...]).astype(BF16)
    source[CELLS:, :] = jnp.where(core == 0, rim_there[...], rim_here[...])
    source[:CELLS, :] = cotangent[...]
    near_grad[...] = dot(shift_pick[...], source[...]).astype(BF16)
    scaled, _ = scaled_rows(near_tokens[...])
    normed[...] = (scaled * gain[...]).astype(BF16)
    projected[...] = dot(normed[...], w_qkv[...]).astype(BF16)
    d_attended[...] = dot_rows(near_grad[...], w_out[...]).astype(BF16)
    scale = HEAD_DIM**-0.5
    for window in range(WINDOWS):
        cells = slice(window * WINDOW, (window + 1) * WINDOW)
        for head in range(heads):
            first = 3 * HEAD_DIM * head
            query = projected[cells, first : first + HEAD_DIM]
            key = projected[cells, first + HEAD_DIM : first + 2 * HEAD_DIM]
            value = projected[cells, first + 2 * HEAD_DIM : first + 3 * HEAD_DIM]
            grad = d_attended[cells, HEAD_DIM * head : HEAD_DIM * (head + 1)]
            scores = dot_rows(query, key) * scale + bias[head]
            raised = jnp.exp(scores - jnp.max(scores, axis=-1, keepdims=True))
            prob = raised / jnp.sum(raised, axis=-1, keepdims=True)
            half = prob.astype(BF16)
            grad_prob = dot_rows(grad, value)
            row_term = jnp.sum(prob * grad_prob, axis=-1, keepdims=True)
            grad_score = (prob * (grad_prob - row_term) * scale).astype(BF16)
            attended = dot(half, value)
            grad_query = dot(grad_score, key)
            grad_key = dot_columns(grad_score, query)
            grad_value = dot_columns(half, grad)
            merged[cells, HEAD_DIM * head : HEAD_DIM * (head + 1)] = attended.astype(BF16)
            merged[cells, group + first : group + first + 3 * HEAD_DIM] = jnp.concatenate(
                [grad_query, grad_key, grad_value], axis=1
            ).astype(BF16)
    here = lax.axis_index("lon")
    rows = grads[0].shape[0]
    if rows % 128:
        whole[:, : 3 * group] = dot_columns(normed[...], merged[:, group:]).astype(BF16)
        whole[:, 3 * group :] = dot_columns(near_grad[...], merged[:, :group]).astype(BF16)
    for step in range(lon_count):
        there = lax.rem(here + step, lon_count)
        part = pl.ds(pl.multiple_of(there * rows, rows), rows)
        if rows % 128:
            grads[step][...] = whole[part, :]
            continue
        grads[step][:, : 3 * group] = dot_columns(normed[:, part], merged[:, group:]).astype(BF16)
        grads[step][:, 3 * group :] = dot_columns(near_grad[:, part], merged[:, :group]).astype(BF16)
    ordered = dot(quarter[...], merged[...]).astype(BF16)
    terms[0] = dot(ordered[:, :group], w_out[...]).astype(BF16)
    terms[1] = dot_rows(ordered[:, group:], w_qkv[...]).astype(BF16)
    for step in range(QUARTERS):
        there = lax.rem(head_index + step, QUARTERS)
        parts[step][...] = terms[:, pl.ds(pl.multiple_of(there * PART, 16), PART), :]
    mine = quarter[pl.ds(pl.multiple_of(head_index * PART, 16), PART), :]
    part_tokens[...] = dot(mine, near_tokens[...]).astype(BF16)
    part_cotangent[...] = dot(mine, near_grad[...]).astype(BF16)


def regroup_kernel(lat_count, *refs):
    count = len(refs) - lat_count
    arrived, blocks = refs[:count], refs[count:]
    here = lax.axis_index("lat")
    rows = blocks[0].shape[0]
    for step in range(lat_count):
        there = lax.rem(here + step, lat_count)
        part = pl.ds(pl.multiple_of(there * rows, rows), rows)
        total = arrived[0][part, :].astype(F32)
        for other in arrived[1:]:
            total = total + other[part, :].astype(F32)
        blocks[step][...] = total.astype(blocks[step].dtype)


def finish_kernel(group, flip, *refs):
    arrived, (grad_qkv, grad_out) = refs[:-2], refs[-2:]
    total = arrived[0][...]
    for other in arrived[1:]:
        total = total + other[...].astype(F32)
    grad_qkv[...] = total[:, : 3 * group]
    out = total[:, 3 * group :]
    grad_out[...] = out.T if flip else out


def norm_kernel(part_tokens, part_cotangent, gain, pick, first, second, third, fourth, *outs):
    layer = part_tokens[...].astype(F32)
    attn = first[0].astype(F32)
    d_normed = first[1].astype(F32)
    for other in (second, third, fourth):
        attn = attn + other[0].astype(F32)
        d_normed = d_normed + other[1].astype(F32)
    scaled, inverse = scaled_rows(part_tokens[...])
    grad = d_normed * gain[...]
    mean_grad = jnp.mean(grad, axis=-1, keepdims=True)
    mean_mixed = jnp.mean(grad * scaled, axis=-1, keepdims=True)
    moved = (grad - mean_grad - scaled * mean_mixed) * inverse
    for at, value in enumerate((layer + attn, part_cotangent[...].astype(F32) + moved)):
        rows = dot(pick[...], value.astype(BF16)).astype(BF16)
        for start, out in zip(OUT_STARTS, outs):
            out[at] = rows[start : start + out.shape[1]]


def join_kernel(own, z_rows, x_rows, d_rows, joined):
    for start, piece in zip(OUT_STARTS, (own, z_rows, x_rows, d_rows)):
        joined[:, start : start + piece.shape[1], :] = piece[...]


def spread_kernel(pick, first, second, third, fourth, layer_out, grad_tokens, gathered):
    head_index = lax.axis_index("head")
    for step, piece in enumerate((first, second, third, fourth)):
        owner = lax.rem(head_index + QUARTERS - step, QUARTERS)
        at = pl.ds(pl.multiple_of(owner * OUT_ROWS, 16), OUT_ROWS)
        gathered[:, at, :] = piece[...]
    layer_out[...] = dot(pick[...], gathered[0]).astype(BF16)
    grad_tokens[...] = dot(pick[...], gathered[1]).astype(BF16)


def shaped(*shape, dtype=BF16):
    return jax.ShapeDtypeStruct(shape, dtype)


def rotated(value, axis, step):
    count = lax.axis_size(axis)
    return lax.ppermute(value, axis, [(i, (i + step) % count) for i in range(count)])


def moved(value, lat_step, lon_step):
    lon_count, lat_count = lax.axis_size("lon"), lax.axis_size("lat")
    pairs = []
    for lon in range(lon_count):
        for lat in range(lat_count):
            target = (lon + lon_step) % lon_count * lat_count + (lat + lat_step) % lat_count
            pairs.append((lon * lat_count + lat, target))
    return lax.ppermute(value, ("lon", "lat"), pairs)


def body(tokens, norm_gain, w_qkv, w_out, bias_table, cotangent):
    level_count, lat_cells, lon_cells, width = tokens.shape
    heads = bias_table.shape[1]
    group = w_out.shape[0]
    lon_count, lat_count = lax.axis_size("lon"), lax.axis_size("lat")
    flat_tokens = tokens.reshape(CELLS, width)
    flat_grad = cotangent.reshape(CELLS, width)
    gain = norm_gain.reshape(1, width)
    rims = call(
        pack_kernel,
        [shaped(RIM_Z, width), shaped(RIM_X, width), shaped(RIM_D, width)],
        cost=cost(2 * RIM * CELLS * width, 4 * CELLS * width),
        name="pack_rims",
    )(one_hot(rim_source(), CELLS), flat_tokens, flat_grad)
    arrived = [moved(rims[0], -1, 0), moved(rims[1], 0, -1), moved(rims[2], -1, -1)]
    rim_here = jnp.concatenate(arrived, axis=0)
    pairs = [(i, i ^ 1) for i in range(lax.axis_size("head"))]
    rim_there = lax.ppermute(rim_here, "head", pairs)
    table = jnp.pad(bias_table.T, ((0, 0), (0, 1024 - bias_table.shape[0])))
    bias = call(
        bias_kernel,
        shaped(heads, WINDOW, WINDOW, dtype=F32),
        [pltpu.VMEM((heads * 48, 768), BF16), pltpu.VMEM((heads, 576, WINDOW), BF16)],
        cost=cost(2 * 192 * 768 * 144 * 12 * 2, 1000000),
        name="window_bias",
    )(table, bias_columns(), bias_rows(), pole_mask())
    lon_rows = width // lon_count
    results = call(
        functools.partial(layer_kernel, lon_count),
        [shaped(lon_rows, 4 * group)] * lon_count
        + [shaped(2, PART, width)] * QUARTERS
        + [shaped(PART, width)] * 2,
        [
            pltpu.VMEM((CELLS + RIM, width), BF16),
            pltpu.VMEM((CELLS, width), BF16),
            pltpu.VMEM((CELLS, width), BF16),
            pltpu.VMEM((CELLS, width), BF16),
            pltpu.VMEM((CELLS, 3 * group), BF16),
            pltpu.VMEM((CELLS, group), BF16),
            pltpu.VMEM((CELLS, 4 * group), BF16),
            pltpu.VMEM((2, QUARTERS * PART, width), BF16),
            pltpu.VMEM((width, 4 * group), BF16),
        ],
        cost=cost(3 * 2 * CELLS * width * width, 12000000),
        name="window_layer",
    )(
        flat_tokens,
        flat_grad,
        rim_here,
        rim_there,
        gain,
        w_qkv,
        w_out,
        bias,
        one_hot(shifted_source(), CELLS + RIM),
        quarter_pick(),
    )
    grads = results[:lon_count]
    parts = results[lon_count : lon_count + QUARTERS]
    part_tokens, part_cotangent = results[lon_count + QUARTERS :]
    from_lon = [grads[0]] + [rotated(grads[step], "lon", step) for step in range(1, lon_count)]
    from_head = [parts[0]] + [rotated(parts[step], "head", step) for step in range(1, QUARTERS)]
    rows = lon_rows // lat_count
    blocks = call(
        functools.partial(regroup_kernel, lat_count),
        [shaped(rows, 4 * group, dtype=F32)] + [shaped(rows, 4 * group)] * (lat_count - 1),
        cost=cost(4 * lon_rows * 4 * group, 6 * lon_rows * 4 * group),
        name="sum_over_lon",
    )(*from_lon)
    from_lat = [blocks[0]] + [rotated(blocks[step], "lat", step) for step in range(1, lat_count)]
    pieces = call(
        norm_kernel,
        [shaped(2, count, width) for count in (OUT_OWN, OUT_Z, OUT_X, OUT_D)],
        cost=cost(2 * 2 * OUT_ROWS * PART * width, 12 * PART * width),
        name="sum_over_heads",
    )(part_tokens, part_cotangent, gain, group_pick(), *from_head)
    home = [pieces[0], moved(pieces[1], 1, 0), moved(pieces[2], 0, 1), moved(pieces[3], 1, 1)]
    joined = call(
        join_kernel,
        shaped(2, OUT_ROWS, width),
        cost=cost(0, 8 * OUT_ROWS * width),
        name="join_home",
    )(*home)
    gathered = [joined] + [rotated(joined, "head", step) for step in range(1, QUARTERS)]
    layer_out, grad_tokens = call(
        spread_kernel,
        [shaped(CELLS, width)] * 2,
        [pltpu.VMEM((2, QUARTERS * OUT_ROWS, width), BF16)],
        cost=cost(2 * 2 * CELLS * CELLS * width, 8 * CELLS * width),
        name="spread_outputs",
    )(own_pick(), *gathered)
    flip = rows % 128 == 0
    grad_qkv, grad_out = call(
        functools.partial(finish_kernel, group, flip),
        [
            shaped(rows, 3 * group, dtype=F32),
            shaped(*((group, rows) if flip else (rows, group)), dtype=F32),
        ],
        cost=cost(4 * rows * 4 * group, 16 * rows * 4 * group),
        name="sum_over_lat",
    )(*from_lat)
    return (
        layer_out.reshape(tokens.shape),
        grad_tokens.reshape(tokens.shape),
        grad_qkv,
        grad_out if flip else grad_out.T,
    )


def solution(mesh):
    in_specs = (
        P(None, "lat", "lon", None),
        P(),
        P(None, "head"),
        P("head", None),
        P(None, "head"),
        P(None, "lat", "lon", None),
    )
    out_specs = (
        P(None, "lat", "lon", None),
        P(None, "lat", "lon", None),
        P(("lon", "lat"), "head"),
        P("head", ("lon", "lat")),
    )
    return jax.shard_map(body, mesh=mesh, in_specs=in_specs, out_specs=out_specs, check_vma=False)
```

```python
import functools

import jax
import jax.numpy as jnp
import numpy as np
from jax import lax
from jax.experimental import pallas as pl
from jax.experimental.pallas import tpu as pltpu
from jax.sharding import PartitionSpec as P

HEAD_DIM = 64
LEV = 2
WLAT = 6
WLON = 12
TILE_LON = 24
WINDOW = LEV * WLAT * WLON
WINDOWS = TILE_LON // WLON
CELLS = WINDOWS * WINDOW
QUARTERS = 4
PART = 80
MID_LAT = WLAT // 2
MID_LON = WLON // 2
SPAN_LAT = 2 * WLAT - 1
SPAN_LON = 2 * WLON - 1
EPSILON = 1e-05
NEG_FILL = -1e30
F32 = jnp.float32
BF16 = jnp.bfloat16

RIM_Z, RIM_X, RIM_D = 112, 48, 48
RIM = RIM_Z + RIM_X + RIM_D
OUT_OWN, OUT_Z, OUT_X, OUT_D = 32, 32, 16, 16
OUT_STARTS = (0, 32, 64, 80)
OUT_ROWS = 96


def own_row(level, lat, lon):
    return (level * WLAT + lat) * TILE_LON + lon


def rim_source():
    rows = np.full(RIM, -1)
    z_width = TILE_LON - MID_LON
    for level in range(LEV):
        for lat in range(MID_LAT):
            for lon in range(z_width):
                rows[(level * MID_LAT + lat) * z_width + lon] = own_row(level, lat, lon + MID_LON)
            for lon in range(MID_LON):
                at = (level * MID_LAT + lat) * MID_LON + lon
                rows[RIM_Z + at] = own_row(level, lat + MID_LAT, lon)
                rows[RIM_Z + RIM_X + at] = own_row(level, lat, lon)
    return rows


def window_cells():
    cells = []
    for window in range(WINDOWS):
        for quarter in range(QUARTERS):
            for lat in range(WLAT):
                for half in range(2):
                    for third in range(3):
                        lon = half * MID_LON + (quarter % 2) * 3 + third
                        cells.append((window, quarter // 2, lat, lon))
    return cells


CELL_LIST = window_cells()
CELL_AT = {cell: at for at, cell in enumerate(CELL_LIST)}


def shifted_source():
    z_width = TILE_LON - MID_LON
    rows = []
    for window, level, lat, lon in CELL_LIST:
        column = window * WLON + lon + MID_LON
        if lat < MID_LAT and column < TILE_LON:
            rows.append(own_row(level, lat + MID_LAT, column))
        elif column < TILE_LON:
            rows.append(CELLS + (level * MID_LAT + lat - MID_LAT) * z_width + column - MID_LON)
        else:
            base = CELLS + RIM_Z + (RIM_X if lat >= MID_LAT else 0)
            rows.append(base + (level * MID_LAT + lat % MID_LAT) * MID_LON + column - TILE_LON)
    return np.array(rows)


def quarter_cells(quarter):
    groups = [[], [], [], []]
    for cell in CELL_LIST:
        window, level, lat, lon = cell
        if level != quarter // 2 or lon % MID_LON // 3 != quarter % 2:
            continue
        beyond = window * WLON + lon + MID_LON >= TILE_LON
        groups[2 * beyond + (lat >= MID_LAT)].append(cell)
    return groups


def one_hot(rows, count):
    picked = np.zeros((len(rows), count), np.float32)
    for at, row in enumerate(rows):
        if row >= 0:
            picked[at, row] = 1.0
    return picked.astype(BF16)


def quarter_pick():
    rows = []
    for quarter in range(QUARTERS):
        cells = sum(quarter_cells(quarter), [])
        rows += [CELL_AT[cell] for cell in cells] + [-1] * (PART - len(cells))
    return one_hot(rows, CELLS)


def group_pick():
    rows = []
    start = 0
    for group, padded in zip(quarter_cells(0), (OUT_OWN, OUT_Z, OUT_X, OUT_D)):
        rows += list(range(start, start + len(group))) + [-1] * (padded - len(group))
        start += len(group)
    return one_hot(rows, PART)


def own_pick():
    place = {}
    for quarter in range(QUARTERS):
        for at, (window, level, lat, lon) in enumerate(sum(quarter_cells(quarter), [])):
            column = (window * WLON + lon + MID_LON) % TILE_LON
            row = own_row(level, (lat + MID_LAT) % WLAT, column)
            place[row] = quarter * PART + at
    return one_hot([place[row] for row in range(CELLS)], QUARTERS * PART)


def bias_rows():
    rows = []
    for window, level, lat, lon in CELL_LIST[:WINDOW]:
        rows.append((level * WLAT + lat) * 16 + WLON - 1 - lon)
    single = one_hot(rows, LEV * WLAT * 16)
    return np.concatenate([single] * 3, axis=1)


def bias_columns():
    return np.array(
        [
            [
                SPAN_LAT * SPAN_LON * (LEV - 1 - level)
                + SPAN_LON * (WLAT - 1 - lat)
                + 2 * (WLON - 1)
                - lon
                for _, level, lat, lon in CELL_LIST[:WINDOW]
            ]
        ],
        np.int32,
    )


def pole_mask():
    side = np.array([lat < MID_LAT for _, _, lat, _ in CELL_LIST[:WINDOW]])
    return np.where(side[:, None] == side[None, :], 0.0, NEG_FILL).astype(np.float32)


def dot(left, right):
    return lax.dot_general(left, right, (((1,), (0,)), ((), ())), preferred_element_type=F32)


def dot_rows(left, right):
    return lax.dot_general(left, right, (((1,), (1,)), ((), ())), preferred_element_type=F32)


def dot_columns(left, right):
    return lax.dot_general(left, right, (((0,), (0,)), ((), ())), preferred_element_type=F32)


def call(kernel, outs, scratch=(), cost=None, name=None):
    return pl.pallas_call(
        kernel,
        out_shape=outs,
        scratch_shapes=scratch,
        name=name,
        cost_estimate=cost,
        compiler_params=pltpu.CompilerParams(vmem_limit_bytes=48 * 1024 * 1024),
    )


def cost(flops, moved):
    return pl.CostEstimate(flops=flops, bytes_accessed=moved, transcendentals=0)


def pack_kernel(pick, tokens, cotangent, rim_z, rim_x, rim_d):
    core = lax.rem(lax.axis_index("head"), 2)
    source = jnp.where(core == 0, tokens[...], cotangent[...])
    rim = dot(pick[...], source).astype(BF16)
    rim_z[...] = rim[:RIM_Z]
    rim_x[...] = rim[RIM_Z : RIM_Z + RIM_X]
    rim_d[...] = rim[RIM_Z + RIM_X :]


def bias_kernel(table, columns, rows, mask, bias, shifted, parts):
    heads = bias.shape[0]
    width = shifted.shape[1]
    for head in range(heads):
        spread = jnp.broadcast_to(table[head : head + 1, :], (16, table.shape[1]))
        rolled = pltpu.roll(spread, 0, 1, stride=1, stride_axis=0)[:, :width]
        high = rolled.astype(BF16)
        rest = rolled - high.astype(F32)
        middle = rest.astype(BF16)
        low = (rest - middle.astype(F32)).astype(BF16)
        for split, value in enumerate((high, middle, low)):
            shifted[(head * 3 + split) * 16 : (head * 3 + split + 1) * 16, :] = value
    place = lax.broadcasted_iota(jnp.int32, (width, WINDOW), 0)
    count = LEV * WLAT * 16
    for level in range(LEV):
        for lat in range(WLAT):
            offset = SPAN_LAT * SPAN_LON * level + SPAN_LON * lat
            wanted = (place == columns[...] + offset).astype(F32).astype(BF16)
            block = dot(shifted[...], wanted).astype(BF16)
            start = (level * WLAT + lat) * 16
            for head in range(heads):
                for split in range(3):
                    first = (head * 3 + split) * 16
                    parts[head, split * count + start : split * count + start + 16, :] = block[
                        first : first + 16
                    ]
    last = lax.axis_index("lat") == lax.axis_size("lat") - 1
    added = jnp.where(last, mask[...], 0.0)
    for head in range(heads):
        bias[head] = dot(rows[...], parts[head]) + added


def scaled_rows(values):
    floats = values.astype(F32)
    center = floats - jnp.mean(floats, axis=-1, keepdims=True)
    inverse = lax.rsqrt(jnp.mean(center * center, axis=-1, keepdims=True) + EPSILON)
    return center * inverse, inverse


def attend(window, head, offset, projected, d_attended, bias, merged, group):
    cells = slice(window * WINDOW, (window + 1) * WINDOW)
    scale = HEAD_DIM**-0.5
    at = head - offset
    first = 3 * HEAD_DIM * at
    query = projected[cells, first : first + HEAD_DIM]
    key = projected[cells, first + HEAD_DIM : first + 2 * HEAD_DIM]
    value = projected[cells, first + 2 * HEAD_DIM : first + 3 * HEAD_DIM]
    grad = d_attended[cells, HEAD_DIM * at : HEAD_DIM * (at + 1)]
    scores = dot_rows(query, key) * scale + bias[head]
    raised = jnp.exp(scores - jnp.max(scores, axis=-1, keepdims=True))
    prob = raised / jnp.sum(raised, axis=-1, keepdims=True)
    half = prob.astype(BF16)
    grad_prob = dot_rows(grad, value)
    row_term = jnp.sum(prob * grad_prob, axis=-1, keepdims=True)
    grad_score = (prob * (grad_prob - row_term) * scale).astype(BF16)
    attended = dot(half, value)
    grad_query = dot(grad_score, key)
    grad_key = dot_columns(grad_score, query)
    grad_value = dot_columns(half, grad)
    merged[cells, HEAD_DIM * at : HEAD_DIM * (at + 1)] = attended.astype(BF16)
    merged[cells, group + first : group + first + 3 * HEAD_DIM] = jnp.concatenate(
        [grad_query, grad_key, grad_value], axis=1
    ).astype(BF16)


def weight_terms(lon_count, normed, near_grad, merged, group, grads, whole):
    here = lax.axis_index("lon")
    rows = grads[0].shape[0]
    if rows % 128:
        whole[:, : 3 * group] = dot_columns(normed[...], merged[:, group:]).astype(BF16)
        whole[:, 3 * group :] = dot_columns(near_grad[...], merged[:, :group]).astype(BF16)
    for step in range(lon_count):
        there = lax.rem(here + step, lon_count)
        part = pl.ds(pl.multiple_of(there * rows, rows), rows)
        if rows % 128:
            grads[step][...] = whole[part, :]
            continue
        grads[step][:, : 3 * group] = dot_columns(normed[:, part], merged[:, group:]).astype(BF16)
        grads[step][:, 3 * group :] = dot_columns(near_grad[:, part], merged[:, :group]).astype(BF16)


def first_kernel(
    lon_count,
    tokens,
    cotangent,
    rim_here,
    rim_there,
    gain,
    w_qkv,
    w_out,
    bias,
    shift_pick,
    *refs,
):
    grads = refs[:lon_count]
    near_tokens, near_grad, normed, projected, d_attended, merged = refs[lon_count : lon_count + 6]
    source, whole, project, d_attend = refs[lon_count + 6 :]
    core = lax.rem(lax.axis_index("head"), 2)
    heads = bias.shape[0] // 2
    group = heads * HEAD_DIM
    source[CELLS:, :] = jnp.where(core == 0, rim_here[...], rim_there[...])
    source[:CELLS, :] = tokens[...]
    near_tokens[...] = dot(shift_pick[...], source[...]).astype(BF16)
    source[CELLS:, :] = jnp.where(core == 0, rim_there[...], rim_here[...])
    source[:CELLS, :] = cotangent[...]
    near_grad[...] = dot(shift_pick[...], source[...]).astype(BF16)
    scaled, _ = scaled_rows(near_tokens[...])
    normed[...] = (scaled * gain[...]).astype(BF16)
    project[...] = dot(normed[...], w_qkv[...]).astype(BF16)
    d_attend[...] = dot_rows(near_grad[...], w_out[...]).astype(BF16)
    projected[...] = project[:, 3 * group :]
    d_attended[...] = d_attend[:, group:]
    for window in range(WINDOWS):
        for head in range(heads):
            attend(window, head, 0, project, d_attend, bias, merged, group)
    weight_terms(lon_count, normed, near_grad, merged, group, grads, whole)


def second_kernel(
    lon_count,
    near_tokens,
    near_grad,
    normed,
    projected,
    d_attended,
    merged_first,
    w_qkv,
    w_out,
    bias,
    quarter,
    *refs,
):
    grads = refs[:lon_count]
    stay, over, swap, part_tokens, part_cotangent = refs[lon_count : lon_count + 5]
    merged, ordered, terms, whole = refs[lon_count + 5 :]
    head_index = lax.axis_index("head")
    core = lax.rem(head_index, 2)
    heads = bias.shape[0] // 2
    group = heads * HEAD_DIM
    for window in range(WINDOWS):
        for head in range(heads):
            attend(window, heads + head, heads, projected, d_attended, bias, merged, group)
    weight_terms(lon_count, normed, near_grad, merged, group, grads, whole)
    pick = quarter[...]
    for half, part in enumerate((merged_first, merged)):
        ordered[:, half * group : (half + 1) * group] = dot(pick, part[:, :group]).astype(BF16)
        start = 2 * group + half * 3 * group
        ordered[:, start : start + 3 * group] = dot(pick, part[:, group:]).astype(BF16)
    terms[0] = dot(ordered[:, : 2 * group], w_out[...]).astype(BF16)
    terms[1] = dot_rows(ordered[:, 2 * group :], w_qkv[...]).astype(BF16)

    def term(owner):
        return terms[:, pl.ds(pl.multiple_of(owner * PART, 16), PART), :]

    far = lax.rem(head_index + 2, QUARTERS)
    stay[...] = term(head_index)
    over[...] = term(far)
    swap[0] = term(head_index + 1 - 2 * core)
    swap[1] = term(far + 1 - 2 * core)
    mine = quarter[pl.ds(pl.multiple_of(head_index * PART, 16), PART), :]
    part_tokens[...] = dot(mine, near_tokens[...]).astype(BF16)
    part_cotangent[...] = dot(mine, near_grad[...]).astype(BF16)


def cores_kernel(over, swapped, total):
    total[...] = (over[...].astype(F32) + swapped[1].astype(F32)).astype(BF16)


def regroup_kernel(*refs):
    arrived, blocks = refs[:-1], refs[-1]
    total = arrived[0][...].astype(F32)
    for other in arrived[1:]:
        total = total + other[...].astype(F32)
    blocks[...] = total.astype(BF16)


def finish_kernel(group, flip, first, second, grad_qkv, grad_out):
    for half, arrived in enumerate((first, second)):
        total = jnp.sum(arrived[...].astype(F32), axis=0)
        grad_qkv[:, half * 3 * group : (half + 1) * 3 * group] = total[:, : 3 * group]
        out = total[:, 3 * group :]
        if flip:
            grad_out[half * group : (half + 1) * group, :] = out.T
        else:
            grad_out[:, half * group : (half + 1) * group] = out


def norm_kernel(part_tokens, part_cotangent, gain, pick, stay, swapped, crossed, *outs):
    layer = part_tokens[...].astype(F32)
    attn = stay[0].astype(F32) + swapped[0, 0].astype(F32) + crossed[0].astype(F32)
    d_normed = stay[1].astype(F32) + swapped[0, 1].astype(F32) + crossed[1].astype(F32)
    scaled, inverse = scaled_rows(part_tokens[...])
    grad = d_normed * gain[...]
    mean_grad = jnp.mean(grad, axis=-1, keepdims=True)
    mean_mixed = jnp.mean(grad * scaled, axis=-1, keepdims=True)
    change = (grad - mean_grad - scaled * mean_mixed) * inverse
    for at, value in enumerate((layer + attn, part_cotangent[...].astype(F32) + change)):
        rows = dot(pick[...], value.astype(BF16)).astype(BF16)
        for start, out in zip(OUT_STARTS, outs):
            out[at] = rows[start : start + out.shape[1]]


def join_kernel(pick, own, z_rows, x_rows, d_rows, joined, rows):
    for start, piece in zip(OUT_STARTS, (own, z_rows, x_rows, d_rows)):
        rows[:, start : start + piece.shape[1], :] = piece[...]
    for at in range(2):
        joined[at] = dot_columns(pick[...], rows[at]).astype(BF16)


def spread_kernel(pick, mine, far, near, across, layer_out, grad_tokens, gathered):
    head_index = lax.axis_index("head")
    sibling = 1 - 2 * lax.rem(head_index, 2)
    over = lax.rem(head_index + 2, QUARTERS)
    owners = (head_index, over, head_index + sibling, over + sibling)
    for owner, piece in zip(owners, (mine, far, near, across)):
        at = pl.ds(pl.multiple_of(owner * PART, 16), PART)
        gathered[:, at, :] = piece[...]
    layer_out[...] = dot(pick[...], gathered[0]).astype(BF16)
    grad_tokens[...] = dot(pick[...], gathered[1]).astype(BF16)


def shaped(*shape, dtype=BF16):
    return jax.ShapeDtypeStruct(shape, dtype)


def rotated(value, axis, step):
    count = lax.axis_size(axis)
    return lax.ppermute(value, axis, [(i, (i + step) % count) for i in range(count)])


def moved(value, lat_step, lon_step):
    lon_count, lat_count = lax.axis_size("lon"), lax.axis_size("lat")
    pairs = []
    for lon in range(lon_count):
        for lat in range(lat_count):
            target = (lon + lon_step) % lon_count * lat_count + (lat + lat_step) % lat_count
            pairs.append((lon * lat_count + lat, target))
    return lax.ppermute(value, ("lon", "lat"), pairs)


def body(tokens, norm_gain, w_qkv, w_out, bias_table, cotangent):
    level_count, lat_cells, lon_cells, width = tokens.shape
    heads = bias_table.shape[1]
    group = w_out.shape[0]
    lon_count, lat_count = lax.axis_size("lon"), lax.axis_size("lat")
    flat_tokens = tokens.reshape(CELLS, width)
    flat_grad = cotangent.reshape(CELLS, width)
    gain = norm_gain.reshape(1, width)
    rims = call(
        pack_kernel,
        [shaped(RIM_Z, width), shaped(RIM_X, width), shaped(RIM_D, width)],
        cost=cost(2 * RIM * CELLS * width, 4 * CELLS * width),
        name="pack_rims",
    )(one_hot(rim_source(), CELLS), flat_tokens, flat_grad)
    arrived = [moved(rims[0], -1, 0), moved(rims[1], 0, -1), moved(rims[2], -1, -1)]
    rim_here = jnp.concatenate(arrived, axis=0)
    pairs = [(i, i ^ 1) for i in range(QUARTERS)]
    rim_there = lax.ppermute(rim_here, "head", pairs)
    table = jnp.pad(bias_table.T, ((0, 0), (0, 1024 - bias_table.shape[0])))
    bias = call(
        bias_kernel,
        shaped(heads, WINDOW, WINDOW, dtype=F32),
        [pltpu.VMEM((heads * 48, 768), BF16), pltpu.VMEM((heads, 576, WINDOW), BF16)],
        cost=cost(2 * 192 * 768 * 144 * 12 * 2, 1000000),
        name="window_bias",
    )(table, bias_columns(), bias_rows(), pole_mask())
    lon_rows = width // lon_count
    half_group = group // 2
    row_scratch = pltpu.VMEM((width, 4 * half_group), BF16)
    first = call(
        functools.partial(first_kernel, lon_count),
        [shaped(lon_rows, 4 * half_group)] * lon_count
        + [shaped(CELLS, width)] * 3
        + [shaped(CELLS, 3 * half_group), shaped(CELLS, half_group), shaped(CELLS, 4 * half_group)],
        [
            pltpu.VMEM((CELLS + RIM, width), BF16),
            row_scratch,
            pltpu.VMEM((CELLS, 3 * group), BF16),
            pltpu.VMEM((CELLS, group), BF16),
        ],
        cost=cost(3 * CELLS * width * width, 8000000),
        name="layer_first_heads",
    )(
        flat_tokens,
        flat_grad,
        rim_here,
        rim_there,
        gain,
        w_qkv,
        w_out,
        bias,
        one_hot(shifted_source(), CELLS + RIM),
    )
    near_tokens, near_grad, normed, projected, d_attended, merged = first[lon_count:]

    def lon_exchange(grads):
        return [grads[0]] + [rotated(grads[step], "lon", step) for step in range(1, lon_count)]

    def lat_exchange(arrived):
        rows = lon_rows // lat_count
        total = call(
            regroup_kernel,
            shaped(lon_rows, 4 * half_group),
            cost=cost(4 * lon_rows * 4 * half_group, 6 * lon_rows * 4 * half_group),
            name="sum_over_lon",
        )(*arrived)
        moved_rows = lax.all_to_all(total, "lat", 0, 0, tiled=True)
        return moved_rows.reshape(lat_count, rows, 4 * half_group)

    from_lon_first = lon_exchange(first[:lon_count])
    second = call(
        functools.partial(second_kernel, lon_count),
        [shaped(lon_rows, 4 * half_group)] * lon_count
        + [shaped(2, PART, width)] * 2
        + [shaped(2, 2, PART, width)]
        + [shaped(PART, width)] * 2,
        [
            pltpu.VMEM((CELLS, 4 * half_group), BF16),
            pltpu.VMEM((QUARTERS * PART, 4 * group), BF16),
            pltpu.VMEM((2, QUARTERS * PART, width), BF16),
            row_scratch,
        ],
        cost=cost(4 * CELLS * width * width, 8000000),
        name="layer_second_heads",
    )(
        near_tokens,
        near_grad,
        normed,
        projected,
        d_attended,
        merged,
        w_qkv,
        w_out,
        bias,
        quarter_pick(),
    )
    stay, over, swap, part_tokens, part_cotangent = second[lon_count:]
    swapped = lax.ppermute(swap, "head", pairs)
    from_lon_second = lon_exchange(second[:lon_count])
    across = call(
        cores_kernel, shaped(2, PART, width), cost=cost(0, 8 * PART * width), name="sum_over_cores"
    )(over, swapped)
    chips = [(i, i ^ 2) for i in range(QUARTERS)]
    crossed = lax.ppermute(across, "head", chips)
    from_lat_first = lat_exchange(from_lon_first)
    pieces = call(
        norm_kernel,
        [shaped(2, count, width) for count in (OUT_OWN, OUT_Z, OUT_X, OUT_D)],
        cost=cost(2 * 2 * OUT_ROWS * PART * width, 12 * PART * width),
        name="sum_over_heads",
    )(part_tokens, part_cotangent, gain, group_pick(), stay, swapped, crossed)
    home = [pieces[0], moved(pieces[1], 1, 0), moved(pieces[2], 0, 1), moved(pieces[3], 1, 1)]
    mine = call(
        join_kernel,
        shaped(2, PART, width),
        [pltpu.VMEM((2, OUT_ROWS, width), BF16)],
        cost=cost(2 * 2 * OUT_ROWS * PART * width, 8 * OUT_ROWS * width),
        name="join_home",
    )(group_pick(), *home)
    far = lax.ppermute(mine, "head", chips)
    near = lax.ppermute(mine, "head", pairs)
    from_lat_second = lat_exchange(from_lon_second)
    beyond = lax.ppermute(far, "head", pairs)
    layer_out, grad_tokens = call(
        spread_kernel,
        [shaped(CELLS, width)] * 2,
        [pltpu.VMEM((2, QUARTERS * PART, width), BF16)],
        cost=cost(2 * 2 * CELLS * CELLS * width, 8 * CELLS * width),
        name="spread_outputs",
    )(own_pick(), mine, far, near, beyond)
    rows = lon_rows // lat_count
    flip = rows % 128 == 0
    grad_qkv, grad_out = call(
        functools.partial(finish_kernel, half_group, flip),
        [
            shaped(rows, 3 * group, dtype=F32),
            shaped(*((group, rows) if flip else (rows, group)), dtype=F32),
        ],
        cost=cost(4 * rows * 4 * group, 16 * rows * 4 * group),
        name="sum_over_lat",
    )(from_lat_first, from_lat_second)
    return (
        layer_out.reshape(tokens.shape),
        grad_tokens.reshape(tokens.shape),
        grad_qkv,
        grad_out if flip else grad_out.T,
    )


def solution(mesh):
    in_specs = (
        P(None, "lat", "lon", None),
        P(),
        P(None, "head"),
        P("head", None),
        P(None, "head"),
        P(None, "lat", "lon", None),
    )
    out_specs = (
        P(None, "lat", "lon", None),
        P(None, "lat", "lon", None),
        P(("lon", "lat"), "head"),
        P("head", ("lon", "lat")),
    )
    return jax.shard_map(body, mesh=mesh, in_specs=in_specs, out_specs=out_specs, check_vma=False)
```

```python
import functools

import jax
import jax.numpy as jnp
import numpy as np
from jax import lax
from jax.experimental import pallas as pl
from jax.experimental.pallas import tpu as pltpu
from jax.sharding import PartitionSpec as P

HEAD_DIM = 64
LEV = 2
WLAT = 6
WLON = 12
TILE_LON = 24
WINDOW = LEV * WLAT * WLON
WINDOWS = TILE_LON // WLON
CELLS = WINDOWS * WINDOW
QUARTERS = 4
PART = 80
MID_LAT = WLAT // 2
MID_LON = WLON // 2
SPAN_LAT = 2 * WLAT - 1
SPAN_LON = 2 * WLON - 1
EPSILON = 1e-05
NEG_FILL = -1e30
F32 = jnp.float32
BF16 = jnp.bfloat16

RIM_Z, RIM_X, RIM_D = 112, 48, 48
RIM = RIM_Z + RIM_X + RIM_D
OUT_OWN, OUT_Z, OUT_X, OUT_D = 32, 32, 16, 16
OUT_STARTS = (0, 32, 64, 80)
OUT_ROWS = 96


def own_row(level, lat, lon):
    return (level * WLAT + lat) * TILE_LON + lon


def rim_source():
    rows = np.full(RIM, -1)
    z_width = TILE_LON - MID_LON
    for level in range(LEV):
        for lat in range(MID_LAT):
            for lon in range(z_width):
                rows[(level * MID_LAT + lat) * z_width + lon] = own_row(level, lat, lon + MID_LON)
            for lon in range(MID_LON):
                at = (level * MID_LAT + lat) * MID_LON + lon
                rows[RIM_Z + at] = own_row(level, lat + MID_LAT, lon)
                rows[RIM_Z + RIM_X + at] = own_row(level, lat, lon)
    return rows


def window_cells():
    cells = []
    for window in range(WINDOWS):
        for quarter in range(QUARTERS):
            for lat in range(WLAT):
                for half in range(2):
                    for third in range(3):
                        lon = half * MID_LON + (quarter % 2) * 3 + third
                        cells.append((window, quarter // 2, lat, lon))
    return cells


CELL_LIST = window_cells()
CELL_AT = {cell: at for at, cell in enumerate(CELL_LIST)}


def shifted_source():
    z_width = TILE_LON - MID_LON
    rows = []
    for window, level, lat, lon in CELL_LIST:
        column = window * WLON + lon + MID_LON
        if lat < MID_LAT and column < TILE_LON:
            rows.append(own_row(level, lat + MID_LAT, column))
        elif column < TILE_LON:
            rows.append(CELLS + (level * MID_LAT + lat - MID_LAT) * z_width + column - MID_LON)
        else:
            base = CELLS + RIM_Z + (RIM_X if lat >= MID_LAT else 0)
            rows.append(base + (level * MID_LAT + lat % MID_LAT) * MID_LON + column - TILE_LON)
    return np.array(rows)


def quarter_cells(quarter):
    groups = [[], [], [], []]
    for cell in CELL_LIST:
        window, level, lat, lon = cell
        if level != quarter // 2 or lon % MID_LON // 3 != quarter % 2:
            continue
        beyond = window * WLON + lon + MID_LON >= TILE_LON
        groups[2 * beyond + (lat >= MID_LAT)].append(cell)
    return groups


def one_hot(rows, count):
    picked = np.zeros((len(rows), count), np.float32)
    for at, row in enumerate(rows):
        if row >= 0:
            picked[at, row] = 1.0
    return picked.astype(BF16)


def quarter_pick():
    rows = []
    for quarter in range(QUARTERS):
        cells = sum(quarter_cells(quarter), [])
        rows += [CELL_AT[cell] for cell in cells] + [-1] * (PART - len(cells))
    return one_hot(rows, CELLS)


def group_pick():
    rows = []
    start = 0
    for group, padded in zip(quarter_cells(0), (OUT_OWN, OUT_Z, OUT_X, OUT_D)):
        rows += list(range(start, start + len(group))) + [-1] * (padded - len(group))
        start += len(group)
    return one_hot(rows, PART)


def own_pick():
    place = {}
    for quarter in range(QUARTERS):
        for at, (window, level, lat, lon) in enumerate(sum(quarter_cells(quarter), [])):
            column = (window * WLON + lon + MID_LON) % TILE_LON
            row = own_row(level, (lat + MID_LAT) % WLAT, column)
            place[row] = quarter * PART + at
    return one_hot([place[row] for row in range(CELLS)], QUARTERS * PART)


def bias_rows():
    rows = []
    for window, level, lat, lon in CELL_LIST[:WINDOW]:
        rows.append((level * WLAT + lat) * 16 + WLON - 1 - lon)
    single = one_hot(rows, LEV * WLAT * 16)
    return np.concatenate([single] * 3, axis=1)


def bias_columns():
    return np.array(
        [
            [
                SPAN_LAT * SPAN_LON * (LEV - 1 - level)
                + SPAN_LON * (WLAT - 1 - lat)
                + 2 * (WLON - 1)
                - lon
                for _, level, lat, lon in CELL_LIST[:WINDOW]
            ]
        ],
        np.int32,
    )


def pole_mask():
    side = np.array([lat < MID_LAT for _, _, lat, _ in CELL_LIST[:WINDOW]])
    return np.where(side[:, None] == side[None, :], 0.0, NEG_FILL).astype(np.float32)


def dot(left, right):
    return lax.dot_general(left, right, (((1,), (0,)), ((), ())), preferred_element_type=F32)


def dot_rows(left, right):
    return lax.dot_general(left, right, (((1,), (1,)), ((), ())), preferred_element_type=F32)


def dot_columns(left, right):
    return lax.dot_general(left, right, (((0,), (0,)), ((), ())), preferred_element_type=F32)


def call(kernel, outs, scratch=(), cost=None, name=None, after=()):
    def run(*args):
        def body(*refs):
            kernel(*refs[: len(args)], *refs[len(args) + len(after) :])

        return pl.pallas_call(
            body,
            out_shape=outs,
            in_specs=[pl.BlockSpec(memory_space=pltpu.VMEM)] * len(args)
            + [pl.BlockSpec(memory_space=pl.ANY)] * len(after),
            scratch_shapes=scratch,
            name=name,
            cost_estimate=cost,
            compiler_params=pltpu.CompilerParams(vmem_limit_bytes=48 * 1024 * 1024),
        )(*args, *after)

    return run


def cost(flops, moved):
    return pl.CostEstimate(flops=flops, bytes_accessed=moved, transcendentals=0)


def pack_kernel(pick, tokens, cotangent, rim_z, rim_x, rim_d):
    core = lax.rem(lax.axis_index("head"), 2)
    source = jnp.where(core == 0, tokens[...], cotangent[...])
    rim = dot(pick[...], source).astype(BF16)
    rim_z[...] = rim[:RIM_Z]
    rim_x[...] = rim[RIM_Z : RIM_Z + RIM_X]
    rim_d[...] = rim[RIM_Z + RIM_X :]


def bias_kernel(table, columns, rows, mask, bias, shifted, parts):
    heads = bias.shape[0]
    width = shifted.shape[1]
    for head in range(heads):
        spread = jnp.broadcast_to(table[head : head + 1, :], (16, table.shape[1]))
        rolled = pltpu.roll(spread, 0, 1, stride=1, stride_axis=0)[:, :width]
        high = rolled.astype(BF16)
        rest = rolled - high.astype(F32)
        middle = rest.astype(BF16)
        low = (rest - middle.astype(F32)).astype(BF16)
        for split, value in enumerate((high, middle, low)):
            shifted[(head * 3 + split) * 16 : (head * 3 + split + 1) * 16, :] = value
    place = lax.broadcasted_iota(jnp.int32, (width, WINDOW), 0)
    count = LEV * WLAT * 16
    for level in range(LEV):
        for lat in range(WLAT):
            offset = SPAN_LAT * SPAN_LON * level + SPAN_LON * lat
            wanted = (place == columns[...] + offset).astype(F32).astype(BF16)
            block = dot(shifted[...], wanted).astype(BF16)
            start = (level * WLAT + lat) * 16
            for head in range(heads):
                for split in range(3):
                    first = (head * 3 + split) * 16
                    parts[head, split * count + start : split * count + start + 16, :] = block[
                        first : first + 16
                    ]
    last = lax.axis_index("lat") == lax.axis_size("lat") - 1
    added = jnp.where(last, mask[...], 0.0)
    for head in range(heads):
        bias[head] = dot(rows[...], parts[head]) + added


def scaled_rows(values):
    floats = values.astype(F32)
    center = floats - jnp.mean(floats, axis=-1, keepdims=True)
    inverse = lax.rsqrt(jnp.mean(center * center, axis=-1, keepdims=True) + EPSILON)
    return center * inverse, inverse


def attend(window, head, projected, d_attended, bias, merged, group):
    cells = slice(window * WINDOW, (window + 1) * WINDOW)
    scale = HEAD_DIM**-0.5
    first = 3 * HEAD_DIM * head
    query = projected[cells, first : first + HEAD_DIM] * jnp.asarray(scale, BF16)
    key = projected[cells, first + HEAD_DIM : first + 2 * HEAD_DIM]
    value = projected[cells, first + 2 * HEAD_DIM : first + 3 * HEAD_DIM]
    grad = d_attended[cells, HEAD_DIM * head : HEAD_DIM * (head + 1)]
    scores = dot_rows(query, key) + bias[head]
    raised = jnp.exp(scores - jnp.max(scores, axis=-1, keepdims=True))
    prob = raised * (1.0 / jnp.sum(raised, axis=-1, keepdims=True))
    half = prob.astype(BF16)
    grad_prob = dot_rows(grad, value)
    row_term = jnp.sum(prob * grad_prob, axis=-1, keepdims=True)
    grad_score = (prob * (grad_prob - row_term)).astype(BF16)
    attended = dot(half, value)
    grad_query = dot(grad_score, key) * scale
    grad_key = dot_columns(grad_score, query)
    grad_value = dot_columns(half, grad)
    merged[cells, HEAD_DIM * head : HEAD_DIM * (head + 1)] = attended.astype(BF16)
    merged[cells, group + first : group + first + 3 * HEAD_DIM] = jnp.concatenate(
        [grad_query, grad_key, grad_value], axis=1
    ).astype(BF16)


def weight_terms(half, normed, near_grad, merged, grads, whole):
    here = lax.axis_index("lon")
    rows = grads[0].shape[0]
    group = merged.shape[1] // 8
    attended = slice(half * group, (half + 1) * group)
    d_qkv = slice((2 + 3 * half) * group, (5 + 3 * half) * group)
    if rows % 128:
        whole[:, : 3 * group] = dot_columns(normed[...], merged[:, d_qkv]).astype(BF16)
        whole[:, 3 * group :] = dot_columns(near_grad[...], merged[:, attended]).astype(BF16)
    for step, grad in enumerate(grads):
        there = lax.rem(here + step, len(grads))
        part = pl.ds(pl.multiple_of(there * rows, rows), rows)
        if rows % 128:
            grad[...] = whole[part, :]
            continue
        grad[:, : 3 * group] = dot_columns(normed[:, part], merged[:, d_qkv]).astype(BF16)
        grad[:, 3 * group :] = dot_columns(near_grad[:, part], merged[:, attended]).astype(BF16)


def layer_kernel(
    tokens,
    cotangent,
    rim_here,
    rim_there,
    gain,
    w_qkv,
    w_out,
    bias,
    shift_pick,
    quarter,
    *refs,
):
    *grads, normed, near_grad, merged, stay, over, swap, part_tokens, part_cotangent = refs[:-7]
    source, near_tokens, projected, d_attended, ordered, terms, whole = refs[-7:]
    head_index = lax.axis_index("head")
    core = lax.rem(head_index, 2)
    heads = bias.shape[0]
    group = heads * HEAD_DIM
    source[CELLS:, :] = jnp.where(core == 0, rim_here[...], rim_there[...])
    source[:CELLS, :] = tokens[...]
    near_tokens[...] = dot(shift_pick[...], source[...]).astype(BF16)
    source[CELLS:, :] = jnp.where(core == 0, rim_there[...], rim_here[...])
    source[:CELLS, :] = cotangent[...]
    near_grad[...] = dot(shift_pick[...], source[...]).astype(BF16)
    scaled, _ = scaled_rows(near_tokens[...])
    normed[...] = (scaled * gain[...]).astype(BF16)
    projected[...] = dot(normed[...], w_qkv[...]).astype(BF16)
    d_attended[...] = dot_rows(near_grad[...], w_out[...]).astype(BF16)
    for window in range(WINDOWS):
        for head in range(heads):
            attend(window, head, projected, d_attended, bias, merged, group)
    weight_terms(0, normed, near_grad, merged, grads, whole)
    ordered[...] = dot(quarter[...], merged[...]).astype(BF16)
    terms[0] = dot(ordered[:, :group], w_out[...]).astype(BF16)
    terms[1] = dot_rows(ordered[:, group:], w_qkv[...]).astype(BF16)

    def term(owner):
        return terms[:, pl.ds(pl.multiple_of(owner * PART, 16), PART), :]

    far = lax.rem(head_index + 2, QUARTERS)
    stay[...] = term(head_index)
    over[...] = term(far)
    swap[0] = term(head_index + 1 - 2 * core)
    swap[1] = term(far + 1 - 2 * core)
    mine = quarter[pl.ds(pl.multiple_of(head_index * PART, 16), PART), :]
    part_tokens[...] = dot(mine, near_tokens[...]).astype(BF16)
    part_cotangent[...] = dot(mine, near_grad[...]).astype(BF16)


def weights_kernel(normed, near_grad, merged, *refs):
    weight_terms(1, normed, near_grad, merged, refs[:-1], refs[-1])


def cores_kernel(over, swapped, total):
    total[...] = (over[...].astype(F32) + swapped[1].astype(F32)).astype(BF16)


def regroup_kernel(lat_count, *refs):
    arrived, blocks = refs[:-lat_count], refs[-lat_count:]
    here = lax.axis_index("lat")
    rows = blocks[0].shape[0]
    for step, block in enumerate(blocks):
        there = lax.rem(here + step, lat_count)
        part = pl.ds(pl.multiple_of(there * rows, rows), rows)
        total = arrived[0][part, :].astype(F32)
        for other in arrived[1:]:
            total = total + other[part, :].astype(F32)
        block[...] = total.astype(block.dtype)


def finish_kernel(group, flip, *refs):
    arrived, (grad_qkv, grad_out) = refs[:-2], refs[-2:]
    count = len(arrived) // 2
    for half in range(2):
        total = arrived[half * count][...]
        for other in arrived[half * count + 1 : (half + 1) * count]:
            total = total + other[...].astype(F32)
        grad_qkv[:, half * 3 * group : (half + 1) * 3 * group] = total[:, : 3 * group]
        out = total[:, 3 * group :]
        if flip:
            grad_out[half * group : (half + 1) * group, :] = out.T
        else:
            grad_out[:, half * group : (half + 1) * group] = out


def norm_kernel(part_tokens, part_cotangent, gain, pick, stay, swapped, crossed, *outs):
    layer = part_tokens[...].astype(F32)
    attn = stay[0].astype(F32) + swapped[0, 0].astype(F32) + crossed[0].astype(F32)
    d_normed = stay[1].astype(F32) + swapped[0, 1].astype(F32) + crossed[1].astype(F32)
    scaled, inverse = scaled_rows(part_tokens[...])
    grad = d_normed * gain[...]
    mean_grad = jnp.mean(grad, axis=-1, keepdims=True)
    mean_mixed = jnp.mean(grad * scaled, axis=-1, keepdims=True)
    change = (grad - mean_grad - scaled * mean_mixed) * inverse
    for at, value in enumerate((layer + attn, part_cotangent[...].astype(F32) + change)):
        rows = dot(pick[...], value.astype(BF16)).astype(BF16)
        for start, out in zip(OUT_STARTS, outs):
            out[at] = rows[start : start + out.shape[1]]


def join_kernel(pick, own, z_rows, x_rows, d_rows, joined, rows):
    for start, piece in zip(OUT_STARTS, (own, z_rows, x_rows, d_rows)):
        rows[:, start : start + piece.shape[1], :] = piece[...]
    for at in range(2):
        joined[at] = dot_columns(pick[...], rows[at]).astype(BF16)


def spread_kernel(pick, mine, far, near, across, layer_out, grad_tokens, gathered):
    head_index = lax.axis_index("head")
    sibling = 1 - 2 * lax.rem(head_index, 2)
    over = lax.rem(head_index + 2, QUARTERS)
    owners = (head_index, over, head_index + sibling, over + sibling)
    for owner, piece in zip(owners, (mine, far, near, across)):
        at = pl.ds(pl.multiple_of(owner * PART, 16), PART)
        gathered[:, at, :] = piece[...]
    layer_out[...] = dot(pick[...], gathered[0]).astype(BF16)
    grad_tokens[...] = dot(pick[...], gathered[1]).astype(BF16)


def shaped(*shape, dtype=BF16):
    return jax.ShapeDtypeStruct(shape, dtype)


def rotated(value, axis, step):
    count = lax.axis_size(axis)
    return lax.ppermute(value, axis, [(i, (i + step) % count) for i in range(count)])


def moved(value, lat_step, lon_step):
    lon_count, lat_count = lax.axis_size("lon"), lax.axis_size("lat")
    pairs = []
    for lon in range(lon_count):
        for lat in range(lat_count):
            target = (lon + lon_step) % lon_count * lat_count + (lat + lat_step) % lat_count
            pairs.append((lon * lat_count + lat, target))
    return lax.ppermute(value, ("lon", "lat"), pairs)


def body(tokens, norm_gain, w_qkv, w_out, bias_table, cotangent):
    level_count, lat_cells, lon_cells, width = tokens.shape
    heads = bias_table.shape[1]
    group = w_out.shape[0]
    lon_count, lat_count = lax.axis_size("lon"), lax.axis_size("lat")
    flat_tokens = tokens.reshape(CELLS, width)
    flat_grad = cotangent.reshape(CELLS, width)
    gain = norm_gain.reshape(1, width)
    rims = call(
        pack_kernel,
        [shaped(RIM_Z, width), shaped(RIM_X, width), shaped(RIM_D, width)],
        cost=cost(2 * RIM * CELLS * width, 4 * CELLS * width),
        name="pack_rims",
    )(one_hot(rim_source(), CELLS), flat_tokens, flat_grad)
    arrived = [moved(rims[0], -1, 0), moved(rims[1], 0, -1), moved(rims[2], -1, -1)]
    rim_here = jnp.concatenate(arrived, axis=0)
    pairs = [(i, i ^ 1) for i in range(QUARTERS)]
    rim_there = lax.ppermute(rim_here, "head", pairs)
    table = jnp.pad(bias_table.T, ((0, 0), (0, 1024 - bias_table.shape[0])))
    bias = call(
        bias_kernel,
        shaped(heads, WINDOW, WINDOW, dtype=F32),
        [pltpu.VMEM((heads * 48, 768), BF16), pltpu.VMEM((heads, 576, WINDOW), BF16)],
        cost=cost(2 * 192 * 768 * 144 * 12 * 2, 1000000),
        name="window_bias",
    )(table, bias_columns(), bias_rows(), pole_mask())
    lon_rows = width // lon_count
    columns = 2 * group
    row_scratch = pltpu.VMEM((width, columns), BF16)
    *first, normed, near_grad, merged, stay, over, swap, part_tokens, part_cotangent = call(
        layer_kernel,
        [shaped(lon_rows, columns)] * lon_count
        + [shaped(CELLS, width), shaped(CELLS, width), shaped(CELLS, 4 * group)]
        + [shaped(2, PART, width)] * 2
        + [shaped(2, 2, PART, width)]
        + [shaped(PART, width)] * 2,
        [
            pltpu.VMEM((CELLS + RIM, width), BF16),
            pltpu.VMEM((CELLS, width), BF16),
            pltpu.VMEM((CELLS, 3 * group), BF16),
            pltpu.VMEM((CELLS, group), BF16),
            pltpu.VMEM((QUARTERS * PART, 4 * group), BF16),
            pltpu.VMEM((2, QUARTERS * PART, width), BF16),
            row_scratch,
        ],
        cost=cost(6 * CELLS * width * width, 8000000),
        name="window_layer",
    )(
        flat_tokens,
        flat_grad,
        rim_here,
        rim_there,
        gain,
        w_qkv,
        w_out,
        bias,
        one_hot(shifted_source(), CELLS + RIM),
        quarter_pick(),
    )

    def lon_exchange(grads):
        return [grads[0]] + [rotated(grads[step], "lon", step) for step in range(1, lon_count)]

    def lat_exchange(arrived, after):
        rows = lon_rows // lat_count
        blocks = call(
            functools.partial(regroup_kernel, lat_count),
            [shaped(rows, columns, dtype=F32)] + [shaped(rows, columns)] * (lat_count - 1),
            cost=cost(4 * lon_rows * columns, 6 * lon_rows * columns),
            name="sum_over_lon",
            after=after,
        )(*arrived)
        arrived = [rotated(blocks[step], "lat", step) for step in range(1, lat_count)]
        return blocks[0], [blocks[0]] + arrived

    swapped = lax.ppermute(swap, "head", pairs)
    from_lon_first = lon_exchange(first)
    across = call(
        cores_kernel, shaped(2, PART, width), cost=cost(0, 8 * PART * width), name="sum_over_cores"
    )(over, swapped)
    chips = [(i, i ^ 2) for i in range(QUARTERS)]
    crossed = lax.ppermute(across, "head", chips)
    pieces = call(
        norm_kernel,
        [shaped(2, count, width) for count in (OUT_OWN, OUT_Z, OUT_X, OUT_D)],
        cost=cost(2 * 2 * OUT_ROWS * PART * width, 12 * PART * width),
        name="sum_over_heads",
    )(part_tokens, part_cotangent, gain, group_pick(), stay, swapped, crossed)
    home = [pieces[0], moved(pieces[1], 1, 0), moved(pieces[2], 0, 1), moved(pieces[3], 1, 1)]
    second = call(
        weights_kernel,
        [shaped(lon_rows, columns)] * lon_count,
        [row_scratch],
        cost=cost(CELLS * width * width, 8000000),
        name="second_weights",
        after=(pieces[0],),
    )(normed, near_grad, merged)
    from_lon_second = lon_exchange(second)
    done_first, from_lat_first = lat_exchange(from_lon_first, (second[0],))
    mine = call(
        join_kernel,
        shaped(2, PART, width),
        [pltpu.VMEM((2, OUT_ROWS, width), BF16)],
        cost=cost(2 * 2 * OUT_ROWS * PART * width, 8 * OUT_ROWS * width),
        name="join_home",
        after=(done_first,),
    )(group_pick(), *home)
    far = lax.ppermute(mine, "head", chips)
    near = lax.ppermute(mine, "head", pairs)
    done_second, from_lat_second = lat_exchange(from_lon_second, (mine,))
    beyond = lax.ppermute(far, "head", pairs)
    layer_out, grad_tokens = call(
        spread_kernel,
        [shaped(CELLS, width)] * 2,
        [pltpu.VMEM((2, QUARTERS * PART, width), BF16)],
        cost=cost(2 * 2 * CELLS * CELLS * width, 8 * CELLS * width),
        name="spread_outputs",
        after=(done_second,),
    )(own_pick(), mine, far, near, beyond)
    rows = lon_rows // lat_count
    flip = rows % 128 == 0
    grad_qkv, grad_out = call(
        functools.partial(finish_kernel, group // 2, flip),
        [
            shaped(rows, 3 * group, dtype=F32),
            shaped(*((group, rows) if flip else (rows, group)), dtype=F32),
        ],
        cost=cost(4 * rows * 4 * group, 16 * rows * 4 * group),
        name="sum_over_lat",
        after=(layer_out,),
    )(*from_lat_first, *from_lat_second)
    return (
        layer_out.reshape(tokens.shape),
        grad_tokens.reshape(tokens.shape),
        grad_qkv,
        grad_out if flip else grad_out.T,
    )


def solution(mesh):
    in_specs = (
        P(None, "lat", "lon", None),
        P(),
        P(None, "head"),
        P("head", None),
        P(None, "head"),
        P(None, "lat", "lon", None),
    )
    out_specs = (
        P(None, "lat", "lon", None),
        P(None, "lat", "lon", None),
        P(("lon", "lat"), "head"),
        P("head", ("lon", "lat")),
    )
    return jax.shard_map(body, mesh=mesh, in_specs=in_specs, out_specs=out_specs, check_vma=False)
```

```python
import functools

import jax
import jax.numpy as jnp
import numpy as np
from jax import lax
from jax.experimental import pallas as pl
from jax.experimental.pallas import tpu as pltpu
from jax.sharding import PartitionSpec as P

HEAD_DIM = 64
LEV = 2
WLAT = 6
WLON = 12
TILE_LON = 24
WINDOW = LEV * WLAT * WLON
WINDOWS = TILE_LON // WLON
CELLS = WINDOWS * WINDOW
QUARTERS = 4
PART = 80
MID_LAT = WLAT // 2
MID_LON = WLON // 2
SPAN_LAT = 2 * WLAT - 1
SPAN_LON = 2 * WLON - 1
EPSILON = 1e-05
NEG_FILL = -1e30
F32 = jnp.float32
BF16 = jnp.bfloat16

RIM_Z, RIM_X, RIM_D = 112, 48, 48
RIM = RIM_Z + RIM_X + RIM_D
OUT_OWN, OUT_Z, OUT_X, OUT_D = 32, 32, 16, 16
OUT_STARTS = (0, 32, 64, 80)
OUT_ROWS = 96


def own_row(level, lat, lon):
    return (level * WLAT + lat) * TILE_LON + lon


def rim_source():
    rows = np.full(RIM, -1)
    z_width = TILE_LON - MID_LON
    for level in range(LEV):
        for lat in range(MID_LAT):
            for lon in range(z_width):
                rows[(level * MID_LAT + lat) * z_width + lon] = own_row(level, lat, lon + MID_LON)
            for lon in range(MID_LON):
                at = (level * MID_LAT + lat) * MID_LON + lon
                rows[RIM_Z + at] = own_row(level, lat + MID_LAT, lon)
                rows[RIM_Z + RIM_X + at] = own_row(level, lat, lon)
    return rows


def window_cells():
    cells = []
    for window in range(WINDOWS):
        for quarter in range(QUARTERS):
            for lat in range(WLAT):
                for half in range(2):
                    for third in range(3):
                        lon = half * MID_LON + (quarter % 2) * 3 + third
                        cells.append((window, quarter // 2, lat, lon))
    return cells


CELL_LIST = window_cells()
CELL_AT = {cell: at for at, cell in enumerate(CELL_LIST)}


def shifted_source():
    z_width = TILE_LON - MID_LON
    rows = []
    for window, level, lat, lon in CELL_LIST:
        column = window * WLON + lon + MID_LON
        if lat < MID_LAT and column < TILE_LON:
            rows.append(own_row(level, lat + MID_LAT, column))
        elif column < TILE_LON:
            rows.append(CELLS + (level * MID_LAT + lat - MID_LAT) * z_width + column - MID_LON)
        else:
            base = CELLS + RIM_Z + (RIM_X if lat >= MID_LAT else 0)
            rows.append(base + (level * MID_LAT + lat % MID_LAT) * MID_LON + column - TILE_LON)
    return np.array(rows)


def quarter_cells(quarter):
    groups = [[], [], [], []]
    for cell in CELL_LIST:
        window, level, lat, lon = cell
        if level != quarter // 2 or lon % MID_LON // 3 != quarter % 2:
            continue
        beyond = window * WLON + lon + MID_LON >= TILE_LON
        groups[2 * beyond + (lat >= MID_LAT)].append(cell)
    return groups


def one_hot(rows, count):
    picked = np.zeros((len(rows), count), np.float32)
    for at, row in enumerate(rows):
        if row >= 0:
            picked[at, row] = 1.0
    return picked.astype(BF16)


def quarter_pick():
    rows = []
    for quarter in range(QUARTERS):
        cells = sum(quarter_cells(quarter), [])
        rows += [CELL_AT[cell] for cell in cells] + [-1] * (PART - len(cells))
    return one_hot(rows, CELLS)


def group_pick():
    rows = []
    start = 0
    for group, padded in zip(quarter_cells(0), (OUT_OWN, OUT_Z, OUT_X, OUT_D)):
        rows += list(range(start, start + len(group))) + [-1] * (padded - len(group))
        start += len(group)
    return one_hot(rows, PART)


def own_pick():
    place = {}
    for quarter in range(QUARTERS):
        for at, (window, level, lat, lon) in enumerate(sum(quarter_cells(quarter), [])):
            column = (window * WLON + lon + MID_LON) % TILE_LON
            row = own_row(level, (lat + MID_LAT) % WLAT, column)
            place[row] = quarter * PART + at
    return one_hot([place[row] for row in range(CELLS)], QUARTERS * PART)


def bias_rows():
    rows = []
    for window, level, lat, lon in CELL_LIST[:WINDOW]:
        rows.append((level * WLAT + lat) * 16 + WLON - 1 - lon)
    single = one_hot(rows, LEV * WLAT * 16)
    return np.concatenate([single] * 3, axis=1)


def bias_columns():
    return np.array(
        [
            [
                SPAN_LAT * SPAN_LON * (LEV - 1 - level)
                + SPAN_LON * (WLAT - 1 - lat)
                + 2 * (WLON - 1)
                - lon
                for _, level, lat, lon in CELL_LIST[:WINDOW]
            ]
        ],
        np.int32,
    )


def pole_mask():
    side = np.array([lat < MID_LAT for _, _, lat, _ in CELL_LIST[:WINDOW]])
    return np.where(side[:, None] == side[None, :], 0.0, NEG_FILL).astype(np.float32)


def dot(left, right):
    return lax.dot_general(left, right, (((1,), (0,)), ((), ())), preferred_element_type=F32)


def dot_rows(left, right):
    return lax.dot_general(left, right, (((1,), (1,)), ((), ())), preferred_element_type=F32)


def dot_columns(left, right):
    return lax.dot_general(left, right, (((0,), (0,)), ((), ())), preferred_element_type=F32)


def call(kernel, outs, scratch=(), cost=None, name=None, after=()):
    def run(*args):
        def body(*refs):
            kernel(*refs[: len(args)], *refs[len(args) + len(after) :])

        return pl.pallas_call(
            body,
            out_shape=outs,
            in_specs=[pl.BlockSpec(memory_space=pltpu.VMEM)] * len(args)
            + [pl.BlockSpec(memory_space=pl.ANY)] * len(after),
            scratch_shapes=scratch,
            name=name,
            cost_estimate=cost,
            compiler_params=pltpu.CompilerParams(vmem_limit_bytes=48 * 1024 * 1024),
        )(*args, *after)

    return run


def cost(flops, moved):
    return pl.CostEstimate(flops=flops, bytes_accessed=moved, transcendentals=0)


def pack_kernel(pick, tokens, cotangent, rim_z, rim_x, rim_d):
    core = lax.rem(lax.axis_index("head"), 2)
    source = jnp.where(core == 0, tokens[...], cotangent[...])
    rim = dot(pick[...], source).astype(BF16)
    rim_z[...] = rim[:RIM_Z]
    rim_x[...] = rim[RIM_Z : RIM_Z + RIM_X]
    rim_d[...] = rim[RIM_Z + RIM_X :]


def bias_kernel(table, columns, rows, mask, bias, shifted, parts):
    heads = bias.shape[0]
    width = shifted.shape[1]
    for head in range(heads):
        spread = jnp.broadcast_to(table[head : head + 1, :], (16, table.shape[1]))
        rolled = pltpu.roll(spread, 0, 1, stride=1, stride_axis=0)[:, :width]
        high = rolled.astype(BF16)
        rest = rolled - high.astype(F32)
        middle = rest.astype(BF16)
        low = (rest - middle.astype(F32)).astype(BF16)
        for split, value in enumerate((high, middle, low)):
            shifted[(head * 3 + split) * 16 : (head * 3 + split + 1) * 16, :] = value
    place = lax.broadcasted_iota(jnp.int32, (width, WINDOW), 0)
    count = LEV * WLAT * 16
    for level in range(LEV):
        for lat in range(WLAT):
            offset = SPAN_LAT * SPAN_LON * level + SPAN_LON * lat
            wanted = (place == columns[...] + offset).astype(F32).astype(BF16)
            block = dot(shifted[...], wanted).astype(BF16)
            start = (level * WLAT + lat) * 16
            for head in range(heads):
                for split in range(3):
                    first = (head * 3 + split) * 16
                    parts[head, split * count + start : split * count + start + 16, :] = block[
                        first : first + 16
                    ]
    last = lax.axis_index("lat") == lax.axis_size("lat") - 1
    added = jnp.where(last, mask[...], 0.0)
    for head in range(heads):
        bias[head] = dot(rows[...], parts[head]) + added


def scaled_rows(values):
    floats = values.astype(F32)
    center = floats - jnp.mean(floats, axis=-1, keepdims=True)
    inverse = lax.rsqrt(jnp.mean(center * center, axis=-1, keepdims=True) + EPSILON)
    return center * inverse, inverse


def attend(window, head, projected, d_attended, bias, merged, group):
    cells = slice(window * WINDOW, (window + 1) * WINDOW)
    scale = HEAD_DIM**-0.5
    first = 3 * HEAD_DIM * head
    query = projected[cells, first : first + HEAD_DIM] * jnp.asarray(scale, BF16)
    key = projected[cells, first + HEAD_DIM : first + 2 * HEAD_DIM]
    value = projected[cells, first + 2 * HEAD_DIM : first + 3 * HEAD_DIM]
    grad = d_attended[cells, HEAD_DIM * head : HEAD_DIM * (head + 1)]
    scores = dot_rows(query, key) + bias[head]
    raised = jnp.exp(scores - jnp.max(scores, axis=-1, keepdims=True))
    prob = raised * (1.0 / jnp.sum(raised, axis=-1, keepdims=True))
    half = prob.astype(BF16)
    grad_prob = dot_rows(grad, value)
    row_term = jnp.sum(prob * grad_prob, axis=-1, keepdims=True)
    grad_score = (prob * (grad_prob - row_term)).astype(BF16)
    attended = dot(half, value)
    grad_query = dot(grad_score, key) * scale
    grad_key = dot_columns(grad_score, query)
    grad_value = dot_columns(half, grad)
    merged[cells, HEAD_DIM * head : HEAD_DIM * (head + 1)] = attended.astype(BF16)
    merged[cells, group + first : group + first + 3 * HEAD_DIM] = jnp.concatenate(
        [grad_query, grad_key, grad_value], axis=1
    ).astype(BF16)


def weight_terms(half, normed, near_grad, merged, whole):
    group = merged.shape[1] // 8
    attended = slice(half * group, (half + 1) * group)
    d_qkv = slice((2 + 3 * half) * group, (5 + 3 * half) * group)
    whole[:, : 3 * group] = dot_columns(normed[...], merged[:, d_qkv]).astype(BF16)
    whole[:, 3 * group :] = dot_columns(near_grad[...], merged[:, attended]).astype(BF16)


def lat_rows(whole, out, lon_count, parity):
    rows = whole.shape[0] // (4 * lon_count)
    for block in range(2 * lon_count):
        start = pl.multiple_of((2 * block + parity) * rows, rows)
        out[block * rows : (block + 1) * rows, :] = whole[pl.ds(start, rows), :]


def layer_kernel(
    tokens,
    cotangent,
    rim_here,
    rim_there,
    gain,
    w_qkv,
    w_out,
    bias,
    shift_pick,
    quarter,
    *refs,
):
    *by_lon, lat_keep, lat_send, stay, over, swap, part_tokens, part_cotangent = refs[:-10]
    source, near_tokens, near_grad, normed, projected, d_attended, merged = refs[-10:-3]
    ordered, terms, whole = refs[-3:]
    head_index = lax.axis_index("head")
    core = lax.rem(head_index, 2)
    heads = bias.shape[0]
    group = heads * HEAD_DIM
    source[CELLS:, :] = jnp.where(core == 0, rim_here[...], rim_there[...])
    source[:CELLS, :] = tokens[...]
    near_tokens[...] = dot(shift_pick[...], source[...]).astype(BF16)
    source[CELLS:, :] = jnp.where(core == 0, rim_there[...], rim_here[...])
    source[:CELLS, :] = cotangent[...]
    near_grad[...] = dot(shift_pick[...], source[...]).astype(BF16)
    scaled, _ = scaled_rows(near_tokens[...])
    normed[...] = (scaled * gain[...]).astype(BF16)
    projected[...] = dot(normed[...], w_qkv[...]).astype(BF16)
    d_attended[...] = dot_rows(near_grad[...], w_out[...]).astype(BF16)
    for window in range(WINDOWS):
        for head in range(heads):
            attend(window, head, projected, d_attended, bias, merged, group)
    weight_terms(0, normed, near_grad, merged, whole)
    lon, lon_count = lax.axis_index("lon"), len(by_lon)
    rows = by_lon[0].shape[0]
    for step, block in enumerate(by_lon):
        start = pl.multiple_of(lax.rem(lon + step, lon_count) * rows, rows)
        block[...] = whole[pl.ds(start, rows), :]
    weight_terms(1, normed, near_grad, merged, whole)
    parity = lax.rem(lax.axis_index("lat"), 2)
    lat_rows(whole, lat_keep, lon_count, parity)
    lat_rows(whole, lat_send, lon_count, 1 - parity)
    ordered[...] = dot(quarter[...], merged[...]).astype(BF16)
    terms[0] = dot(ordered[:, :group], w_out[...]).astype(BF16)
    terms[1] = dot_rows(ordered[:, group:], w_qkv[...]).astype(BF16)

    def term(owner):
        return terms[:, pl.ds(pl.multiple_of(owner * PART, 16), PART), :]

    far = lax.rem(head_index + 2, QUARTERS)
    stay[...] = term(head_index)
    over[...] = term(far)
    swap[0] = term(head_index + 1 - 2 * core)
    swap[1] = term(far + 1 - 2 * core)
    mine = quarter[pl.ds(pl.multiple_of(head_index * PART, 16), PART), :]
    part_tokens[...] = dot(mine, near_tokens[...]).astype(BF16)
    part_cotangent[...] = dot(mine, near_grad[...]).astype(BF16)


def cores_kernel(over, swapped, total):
    total[...] = (over[...].astype(F32) + swapped[1].astype(F32)).astype(BF16)


def total_of(parts):
    total = parts[0].astype(F32)
    for part in parts[1:]:
        total = total + part.astype(F32)
    return total


def second_step_kernel(lon_count, *refs):
    from_lon, (lat_keep, from_lat) = refs[:lon_count], refs[lon_count : lon_count + 2]
    keep_first, send_first, *by_lon = refs[lon_count + 2 :]
    rows = keep_first.shape[0] // 2
    lon, parity = lax.axis_index("lon"), lax.rem(lax.axis_index("lat"), 2)
    for out, wanted in ((keep_first, parity), (send_first, 1 - parity)):
        for block in range(2):
            part = pl.ds(pl.multiple_of((2 * block + wanted) * rows, rows), rows)
            total = total_of([piece[part, :] for piece in from_lon])
            out[block * rows : (block + 1) * rows, :] = total.astype(out.dtype)
    for step, out in enumerate(by_lon):
        start = lax.rem(lon + step, lon_count) * 2 * rows
        part = pl.ds(pl.multiple_of(start, rows), 2 * rows)
        out[...] = total_of([lat_keep[part, :], from_lat[part, :]]).astype(out.dtype)


def third_step_kernel(keep_first, from_lat, *refs):
    from_lon, (keep, send) = refs[:-2], refs[-2:]
    rows = keep.shape[1]
    mine = lax.div(lax.axis_index("lat"), 2)
    for half, parts in enumerate(((keep_first, from_lat), from_lon)):
        for out, block in ((keep, mine), (send, 1 - mine)):
            part = pl.ds(pl.multiple_of(block * rows, rows), rows)
            out[half] = total_of([piece[part, :] for piece in parts]).astype(out.dtype)


def finish_kernel(group, flip, keep, arrived, grad_qkv, grad_out):
    for half in range(2):
        total = keep[half] + arrived[half].astype(F32)
        grad_qkv[:, half * 3 * group : (half + 1) * 3 * group] = total[:, : 3 * group]
        out = total[:, 3 * group :]
        if flip:
            grad_out[half * group : (half + 1) * group, :] = out.T
        else:
            grad_out[:, half * group : (half + 1) * group] = out


def norm_kernel(part_tokens, part_cotangent, gain, pick, stay, swapped, crossed, *outs):
    layer = part_tokens[...].astype(F32)
    attn = stay[0].astype(F32) + swapped[0, 0].astype(F32) + crossed[0].astype(F32)
    d_normed = stay[1].astype(F32) + swapped[0, 1].astype(F32) + crossed[1].astype(F32)
    scaled, inverse = scaled_rows(part_tokens[...])
    grad = d_normed * gain[...]
    mean_grad = jnp.mean(grad, axis=-1, keepdims=True)
    mean_mixed = jnp.mean(grad * scaled, axis=-1, keepdims=True)
    change = (grad - mean_grad - scaled * mean_mixed) * inverse
    for at, value in enumerate((layer + attn, part_cotangent[...].astype(F32) + change)):
        rows = dot(pick[...], value.astype(BF16)).astype(BF16)
        for start, out in zip(OUT_STARTS, outs):
            out[at] = rows[start : start + out.shape[1]]


def join_kernel(pick, own, z_rows, x_rows, d_rows, joined, rows):
    for start, piece in zip(OUT_STARTS, (own, z_rows, x_rows, d_rows)):
        rows[:, start : start + piece.shape[1], :] = piece[...]
    for at in range(2):
        joined[at] = dot_columns(pick[...], rows[at]).astype(BF16)


def spread_kernel(pick, mine, far, near, across, layer_out, grad_tokens, gathered):
    head_index = lax.axis_index("head")
    sibling = 1 - 2 * lax.rem(head_index, 2)
    over = lax.rem(head_index + 2, QUARTERS)
    owners = (head_index, over, head_index + sibling, over + sibling)
    for owner, piece in zip(owners, (mine, far, near, across)):
        at = pl.ds(pl.multiple_of(owner * PART, 16), PART)
        gathered[:, at, :] = piece[...]
    layer_out[...] = dot(pick[...], gathered[0]).astype(BF16)
    grad_tokens[...] = dot(pick[...], gathered[1]).astype(BF16)


def shaped(*shape, dtype=BF16):
    return jax.ShapeDtypeStruct(shape, dtype)


def rotated(value, axis, step):
    count = lax.axis_size(axis)
    return lax.ppermute(value, axis, [(i, (i + step) % count) for i in range(count)])


def moved(value, lat_step, lon_step):
    lon_count, lat_count = lax.axis_size("lon"), lax.axis_size("lat")
    pairs = []
    for lon in range(lon_count):
        for lat in range(lat_count):
            target = (lon + lon_step) % lon_count * lat_count + (lat + lat_step) % lat_count
            pairs.append((lon * lat_count + lat, target))
    return lax.ppermute(value, ("lon", "lat"), pairs)


def body(tokens, norm_gain, w_qkv, w_out, bias_table, cotangent):
    level_count, lat_cells, lon_cells, width = tokens.shape
    heads = bias_table.shape[1]
    group = w_out.shape[0]
    lon_count, lat_count = lax.axis_size("lon"), lax.axis_size("lat")
    flat_tokens = tokens.reshape(CELLS, width)
    flat_grad = cotangent.reshape(CELLS, width)
    gain = norm_gain.reshape(1, width)
    rims = call(
        pack_kernel,
        [shaped(RIM_Z, width), shaped(RIM_X, width), shaped(RIM_D, width)],
        cost=cost(2 * RIM * CELLS * width, 4 * CELLS * width),
        name="pack_rims",
    )(one_hot(rim_source(), CELLS), flat_tokens, flat_grad)
    arrived = [moved(rims[0], -1, 0), moved(rims[1], 0, -1), moved(rims[2], -1, -1)]
    rim_here = jnp.concatenate(arrived, axis=0)
    pairs = [(i, i ^ 1) for i in range(QUARTERS)]
    rim_there = lax.ppermute(rim_here, "head", pairs)
    table = jnp.pad(bias_table.T, ((0, 0), (0, 1024 - bias_table.shape[0])))
    bias = call(
        bias_kernel,
        shaped(heads, WINDOW, WINDOW, dtype=F32),
        [pltpu.VMEM((heads * 48, 768), BF16), pltpu.VMEM((heads, 576, WINDOW), BF16)],
        cost=cost(2 * 192 * 768 * 144 * 12 * 2, 1000000),
        name="window_bias",
    )(table, bias_columns(), bias_rows(), pole_mask())
    lon_rows = width // lon_count
    rows = lon_rows // lat_count
    columns = 2 * group
    *by_lon, lat_keep, lat_send, stay, over, swap, part_tokens, part_cotangent = call(
        layer_kernel,
        [shaped(lon_rows, columns)] * lon_count
        + [shaped(2 * lon_count * rows, columns)] * 2
        + [shaped(2, PART, width)] * 2
        + [shaped(2, 2, PART, width)]
        + [shaped(PART, width)] * 2,
        [
            pltpu.VMEM((CELLS + RIM, width), BF16),
            pltpu.VMEM((CELLS, width), BF16),
            pltpu.VMEM((CELLS, width), BF16),
            pltpu.VMEM((CELLS, width), BF16),
            pltpu.VMEM((CELLS, 3 * group), BF16),
            pltpu.VMEM((CELLS, group), BF16),
            pltpu.VMEM((CELLS, 4 * group), BF16),
            pltpu.VMEM((QUARTERS * PART, 4 * group), BF16),
            pltpu.VMEM((2, QUARTERS * PART, width), BF16),
            pltpu.VMEM((width, columns), BF16),
        ],
        cost=cost(6 * CELLS * width * width, 8000000),
        name="window_layer",
    )(
        flat_tokens,
        flat_grad,
        rim_here,
        rim_there,
        gain,
        w_qkv,
        w_out,
        bias,
        one_hot(shifted_source(), CELLS + RIM),
        quarter_pick(),
    )
    from_lon = [by_lon[0]] + [rotated(by_lon[step], "lon", step) for step in range(1, lon_count)]
    neighbours = [(i, i ^ 1) for i in range(lat_count)]
    from_lat = lax.ppermute(lat_send, "lat", neighbours)
    swapped = lax.ppermute(swap, "head", pairs)
    across = call(
        cores_kernel, shaped(2, PART, width), cost=cost(0, 8 * PART * width), name="sum_over_cores"
    )(over, swapped)
    chips = [(i, i ^ 2) for i in range(QUARTERS)]
    crossed = lax.ppermute(across, "head", chips)
    pieces = call(
        norm_kernel,
        [shaped(2, count, width) for count in (OUT_OWN, OUT_Z, OUT_X, OUT_D)],
        cost=cost(2 * 2 * OUT_ROWS * PART * width, 12 * PART * width),
        name="sum_over_heads",
    )(part_tokens, part_cotangent, gain, group_pick(), stay, swapped, crossed)
    home = [pieces[0], moved(pieces[1], 1, 0), moved(pieces[2], 0, 1), moved(pieces[3], 1, 1)]
    keep_first, send_first, *by_lon = call(
        functools.partial(second_step_kernel, lon_count),
        [shaped(2 * rows, columns, dtype=F32), shaped(2 * rows, columns)]
        + [shaped(2 * rows, columns, dtype=F32)]
        + [shaped(2 * rows, columns)] * (lon_count - 1),
        cost=cost(4 * lon_rows * columns, 6 * lon_rows * columns),
        name="second_step",
        after=(pieces[0],),
    )(*from_lon, lat_keep, from_lat)
    from_lat = lax.ppermute(send_first, "lat", neighbours)
    from_lon = [by_lon[0]] + [rotated(by_lon[step], "lon", step) for step in range(1, lon_count)]
    mine = call(
        join_kernel,
        shaped(2, PART, width),
        [pltpu.VMEM((2, OUT_ROWS, width), BF16)],
        cost=cost(2 * 2 * OUT_ROWS * PART * width, 8 * OUT_ROWS * width),
        name="join_home",
        after=(keep_first,),
    )(group_pick(), *home)
    far = lax.ppermute(mine, "head", chips)
    near = lax.ppermute(mine, "head", pairs)
    keep, send = call(
        third_step_kernel,
        [shaped(2, rows, columns, dtype=F32), shaped(2, rows, columns)],
        cost=cost(4 * rows * columns, 6 * rows * columns),
        name="third_step",
        after=(mine,),
    )(keep_first, from_lat, *from_lon)
    last = lax.ppermute(send, "lat", [(i, i ^ 2) for i in range(lat_count)])
    beyond = lax.ppermute(far, "head", pairs)
    layer_out, grad_tokens = call(
        spread_kernel,
        [shaped(CELLS, width)] * 2,
        [pltpu.VMEM((2, QUARTERS * PART, width), BF16)],
        cost=cost(2 * 2 * CELLS * CELLS * width, 8 * CELLS * width),
        name="spread_outputs",
        after=(keep,),
    )(own_pick(), mine, far, near, beyond)
    flip = rows % 128 == 0
    grad_qkv, grad_out = call(
        functools.partial(finish_kernel, group // 2, flip),
        [
            shaped(rows, 3 * group, dtype=F32),
            shaped(*((group, rows) if flip else (rows, group)), dtype=F32),
        ],
        cost=cost(4 * rows * 4 * group, 16 * rows * 4 * group),
        name="sum_over_lat",
        after=(layer_out,),
    )(keep, last)
    return (
        layer_out.reshape(tokens.shape),
        grad_tokens.reshape(tokens.shape),
        grad_qkv,
        grad_out if flip else grad_out.T,
    )


def solution(mesh):
    in_specs = (
        P(None, "lat", "lon", None),
        P(),
        P(None, "head"),
        P("head", None),
        P(None, "head"),
        P(None, "lat", "lon", None),
    )
    out_specs = (
        P(None, "lat", "lon", None),
        P(None, "lat", "lon", None),
        P(("lon", "lat"), "head"),
        P("head", ("lon", "lat")),
    )
    return jax.shard_map(body, mesh=mesh, in_specs=in_specs, out_specs=out_specs, check_vma=False)
```

```python
import functools

import jax
import jax.numpy as jnp
import numpy as np
from jax import lax
from jax.experimental import pallas as pl
from jax.experimental.pallas import tpu as pltpu
from jax.sharding import PartitionSpec as P

HEAD_DIM = 64
LEV = 2
WLAT = 6
WLON = 12
TILE_LON = 24
WINDOW = LEV * WLAT * WLON
WINDOWS = TILE_LON // WLON
CELLS = WINDOWS * WINDOW
QUARTERS = 4
PART = 80
MID_LAT = WLAT // 2
MID_LON = WLON // 2
SPAN_LAT = 2 * WLAT - 1
SPAN_LON = 2 * WLON - 1
EPSILON = 1e-05
NEG_FILL = -1e30
F32 = jnp.float32
BF16 = jnp.bfloat16

RIM_Z, RIM_X, RIM_D = 112, 48, 48
RIM = RIM_Z + RIM_X + RIM_D
OUT_OWN, OUT_Z, OUT_X, OUT_D = 32, 32, 16, 16
OUT_STARTS = (0, 32, 64, 80)
OUT_ROWS = 96


def own_row(level, lat, lon):
    return (level * WLAT + lat) * TILE_LON + lon


def window_cells():
    cells = []
    for window in range(WINDOWS):
        for quarter in range(QUARTERS):
            for lat in range(WLAT):
                for half in range(2):
                    for third in range(3):
                        lon = half * MID_LON + (quarter % 2) * 3 + third
                        cells.append((window, quarter // 2, lat, lon))
    return cells


CELL_LIST = window_cells()
CELL_AT = {cell: at for at, cell in enumerate(CELL_LIST)}


def shifted_source():
    z_width = TILE_LON - MID_LON
    rows = []
    for window, level, lat, lon in CELL_LIST:
        column = window * WLON + lon + MID_LON
        if lat < MID_LAT and column < TILE_LON:
            rows.append(own_row(level, lat + MID_LAT, column))
        elif column < TILE_LON:
            rows.append(CELLS + (level * MID_LAT + lat - MID_LAT) * z_width + column - MID_LON)
        else:
            base = CELLS + RIM_Z + (RIM_X if lat >= MID_LAT else 0)
            rows.append(base + (level * MID_LAT + lat % MID_LAT) * MID_LON + column - TILE_LON)
    return np.array(rows)


def quarter_cells(quarter):
    groups = [[], [], [], []]
    for cell in CELL_LIST:
        window, level, lat, lon = cell
        if level != quarter // 2 or lon % MID_LON // 3 != quarter % 2:
            continue
        beyond = window * WLON + lon + MID_LON >= TILE_LON
        groups[2 * beyond + (lat >= MID_LAT)].append(cell)
    return groups


def one_hot(rows, count):
    picked = np.zeros((len(rows), count), np.float32)
    for at, row in enumerate(rows):
        if row >= 0:
            picked[at, row] = 1.0
    return picked.astype(BF16)


def quarter_pick():
    rows = []
    for quarter in range(QUARTERS):
        cells = sum(quarter_cells(quarter), [])
        rows += [CELL_AT[cell] for cell in cells] + [-1] * (PART - len(cells))
    return one_hot(rows, CELLS)


def group_pick():
    rows = []
    start = 0
    for group, padded in zip(quarter_cells(0), (OUT_OWN, OUT_Z, OUT_X, OUT_D)):
        rows += list(range(start, start + len(group))) + [-1] * (padded - len(group))
        start += len(group)
    return one_hot(rows, PART)


def own_pick():
    place = {}
    for quarter in range(QUARTERS):
        for at, (window, level, lat, lon) in enumerate(sum(quarter_cells(quarter), [])):
            column = (window * WLON + lon + MID_LON) % TILE_LON
            row = own_row(level, (lat + MID_LAT) % WLAT, column)
            place[row] = quarter * PART + at
    return one_hot([place[row] for row in range(CELLS)], QUARTERS * PART)


def bias_rows():
    rows = []
    for window, level, lat, lon in CELL_LIST[:WINDOW]:
        rows.append((level * WLAT + lat) * 16 + WLON - 1 - lon)
    single = one_hot(rows, LEV * WLAT * 16)
    return np.concatenate([single] * 3, axis=1)


def bias_columns():
    return np.array(
        [
            [
                SPAN_LAT * SPAN_LON * (LEV - 1 - level)
                + SPAN_LON * (WLAT - 1 - lat)
                + 2 * (WLON - 1)
                - lon
                for _, level, lat, lon in CELL_LIST[:WINDOW]
            ]
        ],
        np.int32,
    )


def pole_mask():
    side = np.array([lat < MID_LAT for _, _, lat, _ in CELL_LIST[:WINDOW]])
    return np.where(side[:, None] == side[None, :], 0.0, NEG_FILL).astype(np.float32)


def dot(left, right):
    return lax.dot_general(left, right, (((1,), (0,)), ((), ())), preferred_element_type=F32)


def dot_rows(left, right):
    return lax.dot_general(left, right, (((1,), (1,)), ((), ())), preferred_element_type=F32)


def dot_columns(left, right):
    return lax.dot_general(left, right, (((0,), (0,)), ((), ())), preferred_element_type=F32)


def call(kernel, outs, scratch=(), cost=None, name=None, after=(), far=(), far_outs=0, limit=16):
    def run(*args):
        def body(*refs):
            count = len(args) + len(far)
            kernel(*refs[:count], *refs[count + len(after) :])

        near, outside = pl.BlockSpec(memory_space=pltpu.VMEM), pl.BlockSpec(memory_space=pl.ANY)
        specs = near
        if isinstance(outs, list):
            specs = [outside] * far_outs + [near] * (len(outs) - far_outs)
        return pl.pallas_call(
            body,
            out_shape=outs,
            in_specs=[near] * len(args) + [outside] * (len(far) + len(after)),
            out_specs=specs,
            scratch_shapes=scratch,
            name=name,
            cost_estimate=cost,
            compiler_params=pltpu.CompilerParams(vmem_limit_bytes=limit * 1024 * 1024),
        )(*args, *far, *after)

    return run


def cost(flops, moved):
    return pl.CostEstimate(flops=flops, bytes_accessed=moved, transcendentals=0)


def rim_rows(shape):
    row = lax.broadcasted_iota(jnp.int32, shape, 1)
    level = (row >= WLAT * TILE_LON).astype(jnp.int32)
    row = row - level * WLAT * TILE_LON
    lat = sum((row >= TILE_LON * count).astype(jnp.int32) for count in range(1, WLAT))
    lon = row - lat * TILE_LON
    line = level * MID_LAT + lat
    z_row = line * (TILE_LON - MID_LON) + lon - MID_LON
    d_row = RIM_Z + RIM_X + line * MID_LON + lon
    x_row = RIM_Z + (line - MID_LAT) * MID_LON + lon
    west = lon < MID_LON
    return jnp.where(
        lat < MID_LAT, jnp.where(west, d_row, z_row), jnp.where(west, x_row, -1)
    )


def pack_kernel(tokens, cotangent, rim_z, rim_x, rim_d, source, sems):
    core = lax.rem(lax.axis_index("head"), 2)
    pieces = sems.shape[0]
    rows = CELLS // pieces

    def load(array):
        copies = []
        for piece in range(pieces):
            part = pl.ds(piece * rows, rows)
            copies.append(pltpu.make_async_copy(array.at[part], source.at[part], sems.at[piece]))
        for copy in copies:
            copy.start()
        for copy in copies:
            copy.wait()

    pl.when(core == 0)(lambda: load(tokens))
    pl.when(core != 0)(lambda: load(cotangent))
    wanted = lax.broadcasted_iota(jnp.int32, (RIM, CELLS), 0) == rim_rows((RIM, CELLS))
    rim = dot(wanted.astype(F32).astype(BF16), source[...]).astype(BF16)
    rim_z[...] = rim[:RIM_Z]
    rim_x[...] = rim[RIM_Z : RIM_Z + RIM_X]
    rim_d[...] = rim[RIM_Z + RIM_X :]


def rims_kernel(rim_z, rim_x, rim_d, rim):
    rim[:RIM_Z] = rim_z[...]
    rim[RIM_Z : RIM_Z + RIM_X] = rim_x[...]
    rim[RIM_Z + RIM_X :] = rim_d[...]


def bias_kernel(table, columns, rows, mask, bias, mark, shifted, parts):
    mark[...] = jnp.zeros_like(mark)
    heads = bias.shape[0]
    width = shifted.shape[1]
    for head in range(heads):
        spread = jnp.broadcast_to(table[head : head + 1, :], (16, table.shape[1]))
        rolled = pltpu.roll(spread, 0, 1, stride=1, stride_axis=0)[:, :width]
        high = rolled.astype(BF16)
        rest = rolled - high.astype(F32)
        middle = rest.astype(BF16)
        low = (rest - middle.astype(F32)).astype(BF16)
        for split, value in enumerate((high, middle, low)):
            shifted[(head * 3 + split) * 16 : (head * 3 + split + 1) * 16, :] = value
    place = lax.broadcasted_iota(jnp.int32, (width, WINDOW), 0)
    count = LEV * WLAT * 16
    for level in range(LEV):
        for lat in range(WLAT):
            offset = SPAN_LAT * SPAN_LON * level + SPAN_LON * lat
            wanted = (place == columns[...] + offset).astype(F32).astype(BF16)
            block = dot(shifted[...], wanted).astype(BF16)
            start = (level * WLAT + lat) * 16
            for head in range(heads):
                for split in range(3):
                    first = (head * 3 + split) * 16
                    parts[head, split * count + start : split * count + start + 16, :] = block[
                        first : first + 16
                    ]
    last = lax.axis_index("lat") == lax.axis_size("lat") - 1
    added = jnp.where(last, mask[...], 0.0)
    for head in range(heads):
        bias[head] = dot(rows[...], parts[head]) + added


def scaled_rows(values):
    floats = values.astype(F32)
    center = floats - jnp.mean(floats, axis=-1, keepdims=True)
    inverse = lax.rsqrt(jnp.mean(center * center, axis=-1, keepdims=True) + EPSILON)
    return center * inverse, inverse


def attend(window, head, projected, d_attended, bias, merged, group):
    cells = slice(window * WINDOW, (window + 1) * WINDOW)
    scale = HEAD_DIM**-0.5
    first = 3 * HEAD_DIM * head
    query = projected[cells, first : first + HEAD_DIM] * jnp.asarray(scale, BF16)
    key = projected[cells, first + HEAD_DIM : first + 2 * HEAD_DIM]
    value = projected[cells, first + 2 * HEAD_DIM : first + 3 * HEAD_DIM]
    grad = d_attended[cells, HEAD_DIM * head : HEAD_DIM * (head + 1)]
    scores = dot_rows(query, key) + bias[head]
    raised = jnp.exp(scores - jnp.max(scores, axis=-1, keepdims=True))
    prob = raised * (1.0 / jnp.sum(raised, axis=-1, keepdims=True))
    half = prob.astype(BF16)
    grad_prob = dot_rows(grad, value)
    row_term = jnp.sum(prob * grad_prob, axis=-1, keepdims=True)
    grad_score = (prob * (grad_prob - row_term)).astype(BF16)
    attended = dot(half, value)
    grad_query = dot(grad_score, key) * scale
    grad_key = dot_columns(grad_score, query)
    grad_value = dot_columns(half, grad)
    merged[cells, HEAD_DIM * head : HEAD_DIM * (head + 1)] = attended.astype(BF16)
    merged[cells, group + first : group + first + 3 * HEAD_DIM] = jnp.concatenate(
        [grad_query, grad_key, grad_value], axis=1
    ).astype(BF16)


def weight_terms(half, normed, near_grad, merged, whole):
    group = merged.shape[1] // 8
    attended = slice(half * group, (half + 1) * group)
    d_qkv = slice((2 + 3 * half) * group, (5 + 3 * half) * group)
    whole[:, : 3 * group] = dot_columns(normed[...], merged[:, d_qkv]).astype(BF16)
    whole[:, 3 * group :] = dot_columns(near_grad[...], merged[:, attended]).astype(BF16)


def lat_copies(whole, out, lon_count, parity, sems, first):
    rows = whole.shape[0] // (4 * lon_count)
    copies = []
    for block in range(2 * lon_count):
        start = pl.multiple_of((2 * block + parity) * rows, rows)
        source, target = whole.at[pl.ds(start, rows)], out.at[pl.ds(block * rows, rows)]
        copies.append(pltpu.make_async_copy(source, target, sems.at[first + block]))
    return copies


def layer_kernel(
    tokens,
    cotangent,
    rim_here,
    rim_there,
    gain,
    w_out,
    bias,
    shift_pick,
    quarter,
    w_far,
    *refs,
):
    *by_lon, lat_keep, lat_send, stay, over, swap, part_tokens, part_cotangent = refs[:-14]
    source, near_tokens, near_grad, normed, projected, d_attended, merged = refs[-14:-7]
    ordered, terms, whole_first, whole_second, w_qkv, load_sems, store_sems = refs[-7:]
    pieces = load_sems.shape[0]
    loads = []
    for piece in range(pieces):
        count = w_qkv.shape[0] // pieces
        part = pl.ds(piece * count, count)
        loads.append(
            pltpu.make_async_copy(w_far.at[part], w_qkv.at[part], load_sems.at[piece])
        )
        loads[-1].start()
    head_index = lax.axis_index("head")
    core = lax.rem(head_index, 2)
    heads = bias.shape[0]
    group = heads * HEAD_DIM
    source[CELLS:, :] = jnp.where(core == 0, rim_here[...], rim_there[...])
    source[:CELLS, :] = tokens[...]
    near_tokens[...] = dot(shift_pick[...], source[...]).astype(BF16)
    source[CELLS:, :] = jnp.where(core == 0, rim_there[...], rim_here[...])
    source[:CELLS, :] = cotangent[...]
    near_grad[...] = dot(shift_pick[...], source[...]).astype(BF16)
    scaled, _ = scaled_rows(near_tokens[...])
    normed[...] = (scaled * gain[...]).astype(BF16)
    d_attended[...] = dot_rows(near_grad[...], w_out[...]).astype(BF16)
    for load in loads:
        load.wait()
    projected[...] = dot(normed[...], w_qkv[...]).astype(BF16)
    for window in range(WINDOWS):
        for head in range(heads):
            attend(window, head, projected, d_attended, bias, merged, group)
    weight_terms(0, normed, near_grad, merged, whole_first)
    lon, lon_count = lax.axis_index("lon"), len(by_lon)
    rows = by_lon[0].shape[0]
    stores = []
    for step, block in enumerate(by_lon):
        start = pl.multiple_of(lax.rem(lon + step, lon_count) * rows, rows)
        source_rows = whole_first.at[pl.ds(start, rows)]
        stores.append(pltpu.make_async_copy(source_rows, block, store_sems.at[step]))
    for store in stores:
        store.start()
    weight_terms(1, normed, near_grad, merged, whole_second)
    parity = lax.rem(lax.axis_index("lat"), 2)
    late = lat_copies(whole_second, lat_keep, lon_count, parity, store_sems, lon_count)
    late += lat_copies(whole_second, lat_send, lon_count, 1 - parity, store_sems, 3 * lon_count)
    for store in late:
        store.start()
    ordered[...] = dot(quarter[...], merged[...]).astype(BF16)
    terms[0] = dot(ordered[:, :group], w_out[...]).astype(BF16)
    terms[1] = dot_rows(ordered[:, group:], w_qkv[...]).astype(BF16)

    def term(owner):
        return terms[:, pl.ds(pl.multiple_of(owner * PART, 16), PART), :]

    far = lax.rem(head_index + 2, QUARTERS)
    stay[...] = term(head_index)
    over[...] = term(far)
    swap[0] = term(head_index + 1 - 2 * core)
    swap[1] = term(far + 1 - 2 * core)
    mine = quarter[pl.ds(pl.multiple_of(head_index * PART, 16), PART), :]
    part_tokens[...] = dot(mine, near_tokens[...]).astype(BF16)
    part_cotangent[...] = dot(mine, near_grad[...]).astype(BF16)
    for store in stores + late:
        store.wait()


def cores_kernel(over, swapped, total):
    total[...] = (over[...].astype(F32) + swapped[1].astype(F32)).astype(BF16)


def total_of(parts):
    total = parts[0].astype(F32)
    for part in parts[1:]:
        total = total + part.astype(F32)
    return total


def second_step_kernel(lon_count, *refs):
    from_lon, (lat_keep, from_lat) = refs[:lon_count], refs[lon_count : lon_count + 2]
    keep_first, send_first, *by_lon, mark = refs[lon_count + 2 :]
    mark[...] = jnp.zeros_like(mark)
    rows = keep_first.shape[0] // 2
    lon, parity = lax.axis_index("lon"), lax.rem(lax.axis_index("lat"), 2)
    for out, wanted in ((keep_first, parity), (send_first, 1 - parity)):
        for block in range(2):
            part = pl.ds(pl.multiple_of((2 * block + wanted) * rows, rows), rows)
            total = total_of([piece[part, :] for piece in from_lon])
            out[block * rows : (block + 1) * rows, :] = total.astype(out.dtype)
    for step, out in enumerate(by_lon):
        start = lax.rem(lon + step, lon_count) * 2 * rows
        part = pl.ds(pl.multiple_of(start, rows), 2 * rows)
        out[...] = total_of([lat_keep[part, :], from_lat[part, :]]).astype(out.dtype)


def third_step_kernel(keep_first, from_lat, *refs):
    from_lon, (keep, send, mark) = refs[:-3], refs[-3:]
    mark[...] = jnp.zeros_like(mark)
    rows = keep.shape[1]
    mine = lax.div(lax.axis_index("lat"), 2)
    for half, parts in enumerate(((keep_first, from_lat), from_lon)):
        for out, block in ((keep, mine), (send, 1 - mine)):
            part = pl.ds(pl.multiple_of(block * rows, rows), rows)
            out[half] = total_of([piece[part, :] for piece in parts]).astype(out.dtype)


def finish_kernel(group, flip, keep, arrived, grad_qkv, grad_out, mark):
    mark[...] = jnp.zeros_like(mark)
    for half in range(2):
        total = keep[half] + arrived[half].astype(F32)
        grad_qkv[:, half * 3 * group : (half + 1) * 3 * group] = total[:, : 3 * group]
        out = total[:, 3 * group :]
        if flip:
            grad_out[half * group : (half + 1) * group, :] = out.T
        else:
            grad_out[:, half * group : (half + 1) * group] = out


def norm_kernel(part_tokens, part_cotangent, gain, pick, stay, swapped, crossed, *outs):
    layer = part_tokens[...].astype(F32)
    attn = stay[0].astype(F32) + swapped[0, 0].astype(F32) + crossed[0].astype(F32)
    d_normed = stay[1].astype(F32) + swapped[0, 1].astype(F32) + crossed[1].astype(F32)
    scaled, inverse = scaled_rows(part_tokens[...])
    grad = d_normed * gain[...]
    mean_grad = jnp.mean(grad, axis=-1, keepdims=True)
    mean_mixed = jnp.mean(grad * scaled, axis=-1, keepdims=True)
    change = (grad - mean_grad - scaled * mean_mixed) * inverse
    for at, value in enumerate((layer + attn, part_cotangent[...].astype(F32) + change)):
        rows = dot(pick[...], value.astype(BF16)).astype(BF16)
        for start, out in zip(OUT_STARTS, outs):
            out[at] = rows[start : start + out.shape[1]]


def pass_kernel(arrived, passed):
    passed[...] = arrived[...]


def join_kernel(pick, own, z_rows, x_rows, d_rows, joined, rows):
    for start, piece in zip(OUT_STARTS, (own, z_rows, x_rows, d_rows)):
        rows[:, start : start + piece.shape[1], :] = piece[...]
    for at in range(2):
        joined[at] = dot_columns(pick[...], rows[at]).astype(BF16)


def spread_kernel(pick, mine, far, near, across, layer_out, grad_tokens, gathered):
    head_index = lax.axis_index("head")
    sibling = 1 - 2 * lax.rem(head_index, 2)
    over = lax.rem(head_index + 2, QUARTERS)
    owners = (head_index, over, head_index + sibling, over + sibling)
    for owner, piece in zip(owners, (mine, far, near, across)):
        at = pl.ds(pl.multiple_of(owner * PART, 16), PART)
        gathered[:, at, :] = piece[...]
    layer_out[...] = dot(pick[...], gathered[0]).astype(BF16)
    grad_tokens[...] = dot(pick[...], gathered[1]).astype(BF16)


def shaped(*shape, dtype=BF16):
    return jax.ShapeDtypeStruct(shape, dtype)


def rotated(value, axis, step):
    count = lax.axis_size(axis)
    return lax.ppermute(value, axis, [(i, (i + step) % count) for i in range(count)])


def moved(value, lat_step, lon_step):
    lon_count, lat_count = lax.axis_size("lon"), lax.axis_size("lat")
    pairs = []
    for lon in range(lon_count):
        for lat in range(lat_count):
            target = (lon + lon_step) % lon_count * lat_count + (lat + lat_step) % lat_count
            pairs.append((lon * lat_count + lat, target))
    return lax.ppermute(value, ("lon", "lat"), pairs)


def body(tokens, norm_gain, w_qkv, w_out, bias_table, cotangent):
    level_count, lat_cells, lon_cells, width = tokens.shape
    heads = bias_table.shape[1]
    group = w_out.shape[0]
    lon_count, lat_count = lax.axis_size("lon"), lax.axis_size("lat")
    flat_tokens = tokens.reshape(CELLS, width)
    flat_grad = cotangent.reshape(CELLS, width)
    gain = norm_gain.reshape(1, width)
    mark = shaped(8, 128, dtype=F32)
    rims = call(
        pack_kernel,
        [shaped(RIM_Z, width), shaped(RIM_X, width), shaped(RIM_D, width)],
        [pltpu.VMEM((CELLS, width), BF16), pltpu.SemaphoreType.DMA((6,))],
        cost=cost(2 * RIM * CELLS * width, 4 * CELLS * width),
        name="pack_rims",
        far=tuple(
            pltpu.with_memory_space_constraint(array, pltpu.HBM)
            for array in (flat_tokens, flat_grad)
        ),
    )()
    arrived = [moved(rims[0], -1, 0), moved(rims[1], 0, -1), moved(rims[2], -1, -1)]
    table = jnp.pad(bias_table.T, ((0, 0), (0, 1024 - bias_table.shape[0])))
    bias, bias_mark = call(
        bias_kernel,
        [shaped(heads, WINDOW, WINDOW, dtype=F32), mark],
        [pltpu.VMEM((heads * 48, 768), BF16), pltpu.VMEM((heads, 576, WINDOW), BF16)],
        cost=cost(2 * 192 * 768 * 144 * 12 * 2, 1000000),
        name="window_bias",
    )(table, bias_columns(), bias_rows(), pole_mask())
    rim_here = call(
        rims_kernel, shaped(RIM, width), name="join_rims", cost=cost(0, 4 * RIM * width), after=(bias_mark,)
    )(*arrived)
    pairs = [(i, i ^ 1) for i in range(QUARTERS)]
    rim_there = lax.ppermute(rim_here, "head", pairs)
    lon_rows = width // lon_count
    rows = lon_rows // lat_count
    columns = 2 * group
    *by_lon, lat_keep, lat_send, stay, over, swap, part_tokens, part_cotangent = call(
        layer_kernel,
        [shaped(lon_rows, columns)] * lon_count
        + [shaped(2 * lon_count * rows, columns)] * 2
        + [shaped(2, PART, width)] * 2
        + [shaped(2, 2, PART, width)]
        + [shaped(PART, width)] * 2,
        [
            pltpu.VMEM((CELLS + RIM, width), BF16),
            pltpu.VMEM((CELLS, width), BF16),
            pltpu.VMEM((CELLS, width), BF16),
            pltpu.VMEM((CELLS, width), BF16),
            pltpu.VMEM((CELLS, 3 * group), BF16),
            pltpu.VMEM((CELLS, group), BF16),
            pltpu.VMEM((CELLS, 4 * group), BF16),
            pltpu.VMEM((QUARTERS * PART, 4 * group), BF16),
            pltpu.VMEM((2, QUARTERS * PART, width), BF16),
            pltpu.VMEM((width, columns), BF16),
            pltpu.VMEM((width, columns), BF16),
            pltpu.VMEM((width, 3 * group), BF16),
            pltpu.SemaphoreType.DMA((4,)),
            pltpu.SemaphoreType.DMA((5 * lon_count,)),
        ],
        cost=cost(6 * CELLS * width * width, 8000000),
        name="window_layer",
        far=(w_qkv,),
        far_outs=lon_count + 2,
        limit=32,
    )(
        flat_tokens,
        flat_grad,
        rim_here,
        rim_there,
        gain,
        w_out,
        bias,
        one_hot(shifted_source(), CELLS + RIM),
        quarter_pick(),
    )
    from_lon = [by_lon[0]] + [rotated(by_lon[step], "lon", step) for step in range(1, lon_count)]
    neighbours = [(i, i ^ 1) for i in range(lat_count)]
    from_lat = lax.ppermute(lat_send, "lat", neighbours)
    swapped = lax.ppermute(swap, "head", pairs)
    across = call(
        cores_kernel, shaped(2, PART, width), cost=cost(0, 8 * PART * width), name="sum_over_cores"
    )(over, swapped)
    chips = [(i, i ^ 2) for i in range(QUARTERS)]
    crossed = lax.ppermute(across, "head", chips)
    keep_first, send_first, *by_lon, second_mark = call(
        functools.partial(second_step_kernel, lon_count),
        [shaped(2 * rows, columns, dtype=F32), shaped(2 * rows, columns)]
        + [shaped(2 * rows, columns, dtype=F32)]
        + [shaped(2 * rows, columns)] * (lon_count - 1)
        + [mark],
        cost=cost(4 * lon_rows * columns, 6 * lon_rows * columns),
        name="second_step",
    )(*from_lon, lat_keep, from_lat)
    from_lat = lax.ppermute(send_first, "lat", neighbours)
    from_lon = [by_lon[0]] + [rotated(by_lon[step], "lon", step) for step in range(1, lon_count)]
    pieces = call(
        norm_kernel,
        [shaped(2, count, width) for count in (OUT_OWN, OUT_Z, OUT_X, OUT_D)],
        cost=cost(2 * 2 * OUT_ROWS * PART * width, 12 * PART * width),
        name="sum_over_heads",
        after=(second_mark,),
    )(part_tokens, part_cotangent, gain, group_pick(), stay, swapped, crossed)
    home = [pieces[0], moved(pieces[1], 1, 0), moved(pieces[2], 0, 1), moved(pieces[3], 1, 1)]
    keep, send, third_mark = call(
        third_step_kernel,
        [shaped(2, rows, columns, dtype=F32), shaped(2, rows, columns), mark],
        cost=cost(4 * rows * columns, 6 * rows * columns),
        name="third_step",
    )(keep_first, from_lat, *from_lon)
    last = lax.ppermute(send, "lat", [(i, i ^ 2) for i in range(lat_count)])
    mine = call(
        join_kernel,
        shaped(2, PART, width),
        [pltpu.VMEM((2, OUT_ROWS, width), BF16)],
        cost=cost(2 * 2 * OUT_ROWS * PART * width, 8 * OUT_ROWS * width),
        name="join_home",
        after=(third_mark,),
    )(group_pick(), *home)
    far = lax.ppermute(mine, "head", chips)
    near = lax.ppermute(mine, "head", pairs)
    flip = rows % 128 == 0
    grad_qkv, grad_out, finish_mark = call(
        functools.partial(finish_kernel, group // 2, flip),
        [
            shaped(rows, 3 * group, dtype=F32),
            shaped(*((group, rows) if flip else (rows, group)), dtype=F32),
            mark,
        ],
        cost=cost(4 * rows * 4 * group, 16 * rows * 4 * group),
        name="sum_over_lat",
    )(keep, last)
    passed = call(
        pass_kernel, shaped(2, PART, width), name="pass_on", after=(finish_mark,), cost=cost(0, 8 * PART * width)
    )(far)
    beyond = lax.ppermute(passed, "head", pairs)
    layer_out, grad_tokens = call(
        spread_kernel,
        [shaped(CELLS, width)] * 2,
        [pltpu.VMEM((2, QUARTERS * PART, width), BF16)],
        cost=cost(2 * 2 * CELLS * CELLS * width, 8 * CELLS * width),
        name="spread_outputs",
    )(own_pick(), mine, far, near, beyond)
    return (
        layer_out.reshape(tokens.shape),
        grad_tokens.reshape(tokens.shape),
        grad_qkv,
        grad_out if flip else grad_out.T,
    )


def solution(mesh):
    in_specs = (
        P(None, "lat", "lon", None),
        P(),
        P(None, "head"),
        P("head", None),
        P(None, "head"),
        P(None, "lat", "lon", None),
    )
    out_specs = (
        P(None, "lat", "lon", None),
        P(None, "lat", "lon", None),
        P(("lon", "lat"), "head"),
        P("head", ("lon", "lat")),
    )
    return jax.shard_map(body, mesh=mesh, in_specs=in_specs, out_specs=out_specs, check_vma=False)
```

```python
import functools

import jax
import jax.numpy as jnp
import numpy as np
from jax import lax
from jax.experimental import pallas as pl
from jax.experimental.pallas import tpu as pltpu
from jax.sharding import PartitionSpec as P

HEAD_DIM = 64
LEV = 2
WLAT = 6
WLON = 12
TILE_LON = 24
WINDOW = LEV * WLAT * WLON
WINDOWS = TILE_LON // WLON
CELLS = WINDOWS * WINDOW
QUARTERS = 4
PART = 80
MID_LAT = WLAT // 2
MID_LON = WLON // 2
SPAN_LAT = 2 * WLAT - 1
SPAN_LON = 2 * WLON - 1
EPSILON = 1e-05
NEG_FILL = -1e30
F32 = jnp.float32
BF16 = jnp.bfloat16

RIM_Z, RIM_X, RIM_D = 112, 48, 48
RIM = RIM_Z + RIM_X + RIM_D
OUT_OWN, OUT_Z, OUT_X, OUT_D = 32, 32, 16, 16
OUT_STARTS = (0, 32, 64)
OUT_ROWS = 96


def own_row(level, lat, lon):
    return (level * WLAT + lat) * TILE_LON + lon


def window_cells():
    cells = []
    for window in range(WINDOWS):
        for quarter in range(QUARTERS):
            for lat in range(WLAT):
                for half in range(2):
                    for third in range(3):
                        lon = half * MID_LON + (quarter % 2) * 3 + third
                        cells.append((window, quarter // 2, lat, lon))
    return cells


CELL_LIST = window_cells()
CELL_AT = {cell: at for at, cell in enumerate(CELL_LIST)}


def shifted_source():
    z_width = TILE_LON - MID_LON
    rows = []
    for window, level, lat, lon in CELL_LIST:
        column = window * WLON + lon + MID_LON
        if lat < MID_LAT and column < TILE_LON:
            rows.append(own_row(level, lat + MID_LAT, column))
        elif column < TILE_LON:
            rows.append(CELLS + (level * MID_LAT + lat - MID_LAT) * z_width + column - MID_LON)
        else:
            base = CELLS + RIM_Z + (RIM_X if lat >= MID_LAT else 0)
            rows.append(base + (level * MID_LAT + lat % MID_LAT) * MID_LON + column - TILE_LON)
    return np.array(rows)


def quarter_cells(quarter):
    groups = [[], [], [], []]
    for cell in CELL_LIST:
        window, level, lat, lon = cell
        if level != quarter // 2 or lon % MID_LON // 3 != quarter % 2:
            continue
        beyond = window * WLON + lon + MID_LON >= TILE_LON
        groups[2 * beyond + (lat >= MID_LAT)].append(cell)
    return groups


def one_hot(rows, count):
    picked = np.zeros((len(rows), count), np.float32)
    for at, row in enumerate(rows):
        if row >= 0:
            picked[at, row] = 1.0
    return picked.astype(BF16)


def quarter_pick():
    rows = []
    for quarter in range(QUARTERS):
        cells = sum(quarter_cells(quarter), [])
        rows += [CELL_AT[cell] for cell in cells] + [-1] * (PART - len(cells))
    return one_hot(rows, CELLS)


def group_pick():
    rows = []
    start = 0
    for group, padded in zip(quarter_cells(0), (OUT_OWN, OUT_Z, OUT_X, OUT_D)):
        rows += list(range(start, start + len(group))) + [-1] * (padded - len(group))
        start += len(group)
    return one_hot(rows, PART)


def own_pick():
    place = {}
    for quarter in range(QUARTERS):
        for at, (window, level, lat, lon) in enumerate(sum(quarter_cells(quarter), [])):
            column = (window * WLON + lon + MID_LON) % TILE_LON
            row = own_row(level, (lat + MID_LAT) % WLAT, column)
            place[row] = quarter * PART + at
    return one_hot([place[row] for row in range(CELLS)], QUARTERS * PART)


def window_position(shape, dim):
    def count(value, size, parts):
        return sum((value >= size * step).astype(jnp.int32) for step in range(1, parts))

    cell = lax.broadcasted_iota(jnp.int32, shape, dim)
    quarter = count(cell, WINDOW // QUARTERS, QUARTERS)
    cell = cell - quarter * (WINDOW // QUARTERS)
    lat = count(cell, 6, WLAT)
    cell = cell - lat * 6
    half = count(cell, 3, 2)
    level = count(quarter, 2, 2)
    lon = half * MID_LON + (quarter - 2 * level) * 3 + cell - half * 3
    return level, lat, lon


def dot(left, right):
    return lax.dot_general(left, right, (((1,), (0,)), ((), ())), preferred_element_type=F32)


def dot_rows(left, right):
    return lax.dot_general(left, right, (((1,), (1,)), ((), ())), preferred_element_type=F32)


def dot_columns(left, right):
    return lax.dot_general(left, right, (((0,), (0,)), ((), ())), preferred_element_type=F32)


def call(kernel, outs, scratch=(), cost=None, name=None, after=(), far=(), far_outs=0, limit=16):
    def run(*args):
        def body(*refs):
            count = len(args) + len(far)
            kernel(*refs[:count], *refs[count + len(after) :])

        near, outside = pl.BlockSpec(memory_space=pltpu.VMEM), pl.BlockSpec(memory_space=pl.ANY)
        specs = near
        if isinstance(outs, list):
            specs = [outside] * far_outs + [near] * (len(outs) - far_outs)
        return pl.pallas_call(
            body,
            out_shape=outs,
            in_specs=[near] * len(args) + [outside] * (len(far) + len(after)),
            out_specs=specs,
            scratch_shapes=scratch,
            name=name,
            cost_estimate=cost,
            compiler_params=pltpu.CompilerParams(vmem_limit_bytes=limit * 1024 * 1024),
        )(*args, *far, *after)

    return run


def cost(flops, moved):
    return pl.CostEstimate(flops=flops, bytes_accessed=moved, transcendentals=0)


def rim_rows(shape):
    row = lax.broadcasted_iota(jnp.int32, shape, 1)
    level = (row >= WLAT * TILE_LON).astype(jnp.int32)
    row = row - level * WLAT * TILE_LON
    lat = sum((row >= TILE_LON * count).astype(jnp.int32) for count in range(1, WLAT))
    lon = row - lat * TILE_LON
    line = level * MID_LAT + lat
    z_row = line * (TILE_LON - MID_LON) + lon - MID_LON
    d_row = RIM_Z + RIM_X + line * MID_LON + lon
    x_row = RIM_Z + (line - MID_LAT) * MID_LON + lon
    west = lon < MID_LON
    return jnp.where(
        lat < MID_LAT, jnp.where(west, d_row, z_row), jnp.where(west, x_row, -1)
    )


def pack_kernel(tokens, cotangent, rim_z, rim_x, rim_d, source, sems):
    core = lax.rem(lax.axis_index("head"), 2)
    pieces = sems.shape[0]
    rows = CELLS // pieces

    def load(array):
        copies = []
        for piece in range(pieces):
            part = pl.ds(piece * rows, rows)
            copies.append(pltpu.make_async_copy(array.at[part], source.at[part], sems.at[piece]))
        for copy in copies:
            copy.start()
        for copy in copies:
            copy.wait()

    pl.when(core == 0)(lambda: load(tokens))
    pl.when(core != 0)(lambda: load(cotangent))
    wanted = lax.broadcasted_iota(jnp.int32, (RIM, CELLS), 0) == rim_rows((RIM, CELLS))
    rim = dot(wanted.astype(F32).astype(BF16), source[...]).astype(BF16)
    rim_z[...] = rim[:RIM_Z]
    rim_x[...] = rim[RIM_Z : RIM_Z + RIM_X]
    rim_d[...] = rim[RIM_Z + RIM_X :]


def rims_kernel(rim_z, rim_x, rim_d, rim):
    rim[:RIM_Z] = rim_z[...]
    rim[RIM_Z : RIM_Z + RIM_X] = rim_x[...]
    rim[RIM_Z + RIM_X :] = rim_d[...]


def bias_kernel(table, bias, mark, padded, shifted, parts):
    mark[...] = jnp.zeros_like(mark)
    heads = bias.shape[0]
    width = shifted.shape[1]
    padded[...] = jnp.zeros_like(padded)
    padded[:heads, : table.shape[1]] = table[...]
    for head in range(heads):
        spread = jnp.broadcast_to(padded[head : head + 1, :], (16, padded.shape[1]))
        rolled = pltpu.roll(spread, 0, 1, stride=1, stride_axis=0)[:, :width]
        high = rolled.astype(BF16)
        rest = rolled - high.astype(F32)
        middle = rest.astype(BF16)
        low = (rest - middle.astype(F32)).astype(BF16)
        for split, value in enumerate((high, middle, low)):
            shifted[(head * 3 + split) * 16 : (head * 3 + split + 1) * 16, :] = value
    place = lax.broadcasted_iota(jnp.int32, (width, WINDOW), 0)
    count = LEV * WLAT * 16
    level_of, lat_of, lon_of = window_position((1, WINDOW), 1)
    plane = SPAN_LAT * SPAN_LON
    column = plane * (level_of + LEV - 1) + SPAN_LON * (lat_of + WLAT - 1) + lon_of + WLON - 1
    for level in range(LEV):
        for lat in range(WLAT):
            wanted = (place == column - (plane * level + SPAN_LON * lat)).astype(F32).astype(BF16)
            block = dot(shifted[...], wanted).astype(BF16)
            start = (level * WLAT + lat) * 16
            for head in range(heads):
                for split in range(3):
                    first = (head * 3 + split) * 16
                    parts[head, split * count + start : split * count + start + 16, :] = block[
                        first : first + 16
                    ]
    level_in, lat_in, lon_in = window_position((WINDOW, 1), 0)
    lane = lax.broadcasted_iota(jnp.int32, (WINDOW, 3 * count), 1)
    lane = lane - count * ((lane >= count).astype(jnp.int32) + (lane >= 2 * count).astype(jnp.int32))
    rows = (lane == (level_in * WLAT + lat_in) * 16 + lon_in).astype(F32).astype(BF16)
    last = lax.axis_index("lat") == lax.axis_size("lat") - 1
    south_in = (lat_in < MID_LAT).astype(jnp.int32)
    south_of = (lat_of < MID_LAT).astype(jnp.int32)
    added = jnp.where((south_in != south_of) & last, NEG_FILL, 0.0)
    for head in range(heads):
        bias[head] = dot(rows, parts[head]) + added


def scaled_rows(values):
    floats = values.astype(F32)
    center = floats - jnp.mean(floats, axis=-1, keepdims=True)
    inverse = lax.rsqrt(jnp.mean(center * center, axis=-1, keepdims=True) + EPSILON)
    return center * inverse, inverse


def attend(window, projected, d_attended, bias, merged, group):
    cells = slice(window * WINDOW, (window + 1) * WINDOW)
    scale = HEAD_DIM**-0.5
    heads = range(bias.shape[0])

    def part(head, kind):
        first = (3 * head + kind) * HEAD_DIM
        return projected[cells, first : first + HEAD_DIM]

    queries = [part(head, 0) * jnp.asarray(scale, BF16) for head in heads]
    keys = [part(head, 1) for head in heads]
    values = [part(head, 2) for head in heads]
    grads = [d_attended[cells, HEAD_DIM * head : HEAD_DIM * (head + 1)] for head in heads]
    scores = [dot_rows(keys[head], queries[head]) + bias[head] for head in heads]
    grad_probs = [dot_rows(values[head], grads[head]) for head in heads]
    halves, grad_scores = [], []
    for head in heads:
        raised = jnp.exp(scores[head] - jnp.max(scores[head], axis=0, keepdims=True))
        prob = raised * (1.0 / jnp.sum(raised, axis=0, keepdims=True))
        row_term = jnp.sum(prob * grad_probs[head], axis=0, keepdims=True)
        halves.append(prob.astype(BF16))
        grad_scores.append((prob * (grad_probs[head] - row_term)).astype(BF16))
    for head in heads:
        attended = dot_columns(halves[head], values[head])
        grad_value = dot(halves[head], grads[head])
        grad_query = dot_columns(grad_scores[head], keys[head]) * scale
        grad_key = dot(grad_scores[head], queries[head])
        merged[cells, HEAD_DIM * head : HEAD_DIM * (head + 1)] = attended.astype(BF16)
        first = group + 3 * HEAD_DIM * head
        merged[cells, first : first + 3 * HEAD_DIM] = jnp.concatenate(
            [grad_query, grad_key, grad_value], axis=1
        ).astype(BF16)


def lat_copies(whole, columns, out, lon_count, parity, sems, first):
    rows = whole.shape[0] // (4 * lon_count)
    copies = []
    for block in range(2 * lon_count):
        start = pl.multiple_of((2 * block + parity) * rows, rows)
        source, target = whole.at[pl.ds(start, rows), columns], out.at[pl.ds(block * rows, rows)]
        copies.append(pltpu.make_async_copy(source, target, sems.at[first + block]))
    return copies


def layer_kernel(
    tokens,
    cotangent,
    rim_here,
    rim_there,
    gain,
    w_out,
    bias,
    shift_pick,
    quarter,
    w_far,
    *refs,
):
    *by_lon, lat_keep, lat_send, stay, over, swap, part_tokens, part_cotangent = refs[:-13]
    source, near_tokens, near_grad, normed, projected, d_attended, merged = refs[-13:-6]
    ordered, terms, whole, w_qkv, load_sems, store_sems = refs[-6:]
    pieces = load_sems.shape[0]
    loads = []
    for piece in range(pieces):
        count = w_qkv.shape[0] // pieces
        part = pl.ds(piece * count, count)
        loads.append(
            pltpu.make_async_copy(w_far.at[part], w_qkv.at[part], load_sems.at[piece])
        )
        loads[-1].start()
    head_index = lax.axis_index("head")
    core = lax.rem(head_index, 2)
    heads = bias.shape[0]
    group = heads * HEAD_DIM
    source[CELLS:, :] = jnp.where(core == 0, rim_here[...], rim_there[...])
    source[:CELLS, :] = tokens[...]
    near_tokens[...] = dot(shift_pick[...], source[...]).astype(BF16)
    source[CELLS:, :] = jnp.where(core == 0, rim_there[...], rim_here[...])
    source[:CELLS, :] = cotangent[...]
    near_grad[...] = dot(shift_pick[...], source[...]).astype(BF16)
    scaled, _ = scaled_rows(near_tokens[...])
    normed[...] = (scaled * gain[...]).astype(BF16)
    d_attended[...] = dot_rows(near_grad[...], w_out[...]).astype(BF16)
    for load in loads:
        load.wait()
    projected[...] = dot(normed[...], w_qkv[...]).astype(BF16)
    for window in range(WINDOWS):
        attend(window, projected, d_attended, bias, merged, group)
    whole[:, : 3 * group] = dot_columns(normed[...], merged[:, group:]).astype(BF16)
    whole[:, 3 * group :] = dot_columns(near_grad[...], merged[:, :group]).astype(BF16)
    lon, lon_count = lax.axis_index("lon"), len(by_lon)
    rows = by_lon[0].shape[0]
    stores = []
    for step, block in enumerate(by_lon):
        start = pl.multiple_of(lax.rem(lon + step, lon_count) * rows, rows)
        source_rows = whole.at[pl.ds(start, rows), pl.ds(0, 2 * group)]
        stores.append(pltpu.make_async_copy(source_rows, block, store_sems.at[step]))
    parity = lax.rem(lax.axis_index("lat"), 2)
    later = pl.ds(2 * group, 2 * group)
    stores += lat_copies(whole, later, lat_keep, lon_count, parity, store_sems, lon_count)
    stores += lat_copies(whole, later, lat_send, lon_count, 1 - parity, store_sems, 3 * lon_count)
    for store in stores:
        store.start()
    ordered[...] = dot(quarter[...], merged[...]).astype(BF16)
    terms[0] = dot(ordered[:, :group], w_out[...]).astype(BF16)
    terms[1] = dot_rows(ordered[:, group:], w_qkv[...]).astype(BF16)

    def term(owner):
        return terms[:, pl.ds(pl.multiple_of(owner * PART, 16), PART), :]

    far = lax.rem(head_index + 2, QUARTERS)
    stay[...] = term(head_index)
    over[...] = term(far)
    swap[0] = term(head_index + 1 - 2 * core)
    swap[1] = term(far + 1 - 2 * core)
    mine = quarter[pl.ds(pl.multiple_of(head_index * PART, 16), PART), :]
    part_tokens[...] = dot(mine, near_tokens[...]).astype(BF16)
    part_cotangent[...] = dot(mine, near_grad[...]).astype(BF16)
    for store in stores:
        store.wait()


def cores_kernel(over, swapped, total):
    total[...] = (over[...].astype(F32) + swapped[1].astype(F32)).astype(BF16)


def total_of(parts):
    total = parts[0].astype(F32)
    for part in parts[1:]:
        total = total + part.astype(F32)
    return total


def second_step_kernel(lon_count, *refs):
    from_lon, (lat_keep, from_lat) = refs[:lon_count], refs[lon_count : lon_count + 2]
    keep_first, send_first, *by_lon = refs[lon_count + 2 :]
    rows = keep_first.shape[0] // 2
    lon, parity = lax.axis_index("lon"), lax.rem(lax.axis_index("lat"), 2)
    for out, wanted in ((keep_first, parity), (send_first, 1 - parity)):
        for block in range(2):
            part = pl.ds(pl.multiple_of((2 * block + wanted) * rows, rows), rows)
            total = total_of([piece[part, :] for piece in from_lon])
            out[block * rows : (block + 1) * rows, :] = total.astype(out.dtype)
    for step, out in enumerate(by_lon):
        start = lax.rem(lon + step, lon_count) * 2 * rows
        part = pl.ds(pl.multiple_of(start, rows), 2 * rows)
        out[...] = total_of([lat_keep[part, :], from_lat[part, :]]).astype(out.dtype)


def third_step_kernel(keep_first, from_lat, *refs):
    from_lon, (keep, send) = refs[:-2], refs[-2:]
    rows = keep.shape[1]
    mine = lax.div(lax.axis_index("lat"), 2)
    for half, parts in enumerate(((keep_first, from_lat), from_lon)):
        for out, block in ((keep, mine), (send, 1 - mine)):
            part = pl.ds(pl.multiple_of(block * rows, rows), rows)
            out[half] = total_of([piece[part, :] for piece in parts]).astype(out.dtype)


def finish_kernel(group, flip, keep, arrived, grad_qkv, grad_out):
    grad_qkv[:, : 2 * group] = keep[0] + arrived[0].astype(F32)
    total = keep[1] + arrived[1].astype(F32)
    grad_qkv[:, 2 * group :] = total[:, :group]
    out = total[:, group:]
    grad_out[...] = out.T if flip else out


def norm_kernel(part_tokens, part_cotangent, gain, pick, stay, swapped, crossed, *outs):
    layer = part_tokens[...].astype(F32)
    attn = stay[0].astype(F32) + swapped[0, 0].astype(F32) + crossed[0].astype(F32)
    d_normed = stay[1].astype(F32) + swapped[0, 1].astype(F32) + crossed[1].astype(F32)
    scaled, inverse = scaled_rows(part_tokens[...])
    grad = d_normed * gain[...]
    mean_grad = jnp.mean(grad, axis=-1, keepdims=True)
    mean_mixed = jnp.mean(grad * scaled, axis=-1, keepdims=True)
    change = (grad - mean_grad - scaled * mean_mixed) * inverse
    for at, value in enumerate((layer + attn, part_cotangent[...].astype(F32) + change)):
        rows = dot(pick[...], value.astype(BF16)).astype(BF16)
        for start, out in zip(OUT_STARTS, outs):
            out[at] = rows[start : start + out.shape[1]]


def north_kernel(z_rows, x_rows, rows, mark):
    mark[...] = jnp.zeros_like(mark)
    rows[:, :OUT_Z, :] = z_rows[...]
    rows[:, OUT_Z:, :] = x_rows[:, OUT_X:, :]


def join_kernel(pick, own, z_rows, x_rows, joined, layer, grad, mark, rows):
    mark[...] = jnp.zeros_like(mark)
    rows[:, :OUT_OWN, :] = own[...]
    rows[:, OUT_OWN : OUT_OWN + OUT_Z, :] = z_rows[:, :OUT_Z, :]
    rows[:, OUT_OWN + OUT_Z : OUT_ROWS - OUT_D, :] = x_rows[:, :OUT_X, :]
    rows[:, OUT_ROWS - OUT_D :, :] = z_rows[:, OUT_Z:, :]
    for at, single in enumerate((layer, grad)):
        single[...] = dot_columns(pick[...], rows[at]).astype(BF16)
        joined[at] = single[...]


def spread_kernel(pick, mine, near, *refs):
    far, across, outs, (mark, gathered) = refs[:2], refs[2:4], refs[4:6], refs[6:]
    mark[...] = jnp.zeros_like(mark)
    head_index = lax.axis_index("head")
    sibling = 1 - 2 * lax.rem(head_index, 2)
    over = lax.rem(head_index + 2, QUARTERS)

    def place(owner):
        return pl.ds(pl.multiple_of(owner * PART, 16), PART)

    for at, out in enumerate(outs):
        gathered[at, place(head_index), :] = mine[at]
        gathered[at, place(head_index + sibling), :] = near[at]
        gathered[at, place(over), :] = far[at][...]
        gathered[at, place(over + sibling), :] = across[at][...]
        out[...] = dot(pick[...], gathered[at]).astype(BF16)


def shaped(*shape, dtype=BF16):
    return jax.ShapeDtypeStruct(shape, dtype)


def rotated(value, axis, step):
    count = lax.axis_size(axis)
    return lax.ppermute(value, axis, [(i, (i + step) % count) for i in range(count)])


def moved(value, lat_step, lon_step):
    lon_count, lat_count = lax.axis_size("lon"), lax.axis_size("lat")
    pairs = []
    for lon in range(lon_count):
        for lat in range(lat_count):
            target = (lon + lon_step) % lon_count * lat_count + (lat + lat_step) % lat_count
            pairs.append((lon * lat_count + lat, target))
    return lax.ppermute(value, ("lon", "lat"), pairs)


def body(tokens, norm_gain, w_qkv, w_out, bias_table, cotangent):
    level_count, lat_cells, lon_cells, width = tokens.shape
    heads = bias_table.shape[1]
    group = w_out.shape[0]
    lon_count, lat_count = lax.axis_size("lon"), lax.axis_size("lat")
    flat_tokens = tokens.reshape(CELLS, width)
    flat_grad = cotangent.reshape(CELLS, width)
    gain = norm_gain.reshape(1, width)
    mark = shaped(8, 128, dtype=F32)
    rims = call(
        pack_kernel,
        [shaped(RIM_Z, width), shaped(RIM_X, width), shaped(RIM_D, width)],
        [pltpu.VMEM((CELLS, width), BF16), pltpu.SemaphoreType.DMA((6,))],
        cost=cost(2 * RIM * CELLS * width, 4 * CELLS * width),
        name="pack_rims",
        far=tuple(
            pltpu.with_memory_space_constraint(array, pltpu.HBM)
            for array in (flat_tokens, flat_grad)
        ),
    )()
    arrived = [moved(rims[0], -1, 0), moved(rims[1], 0, -1), moved(rims[2], -1, -1)]
    bias, bias_mark = call(
        bias_kernel,
        [shaped(heads, WINDOW, WINDOW, dtype=F32), mark],
        [
            pltpu.VMEM((8, 1024), F32),
            pltpu.VMEM((heads * 48, 768), BF16),
            pltpu.VMEM((heads, 576, WINDOW), BF16),
        ],
        cost=cost(2 * 192 * 768 * 144 * 12 * 2, 1000000),
        name="window_bias",
    )(bias_table.T)
    rim_here = call(
        rims_kernel, shaped(RIM, width), name="join_rims", cost=cost(0, 4 * RIM * width), after=(bias_mark,)
    )(*arrived)
    pairs = [(i, i ^ 1) for i in range(QUARTERS)]
    rim_there = lax.ppermute(rim_here, "head", pairs)
    lon_rows = width // lon_count
    rows = lon_rows // lat_count
    columns = 2 * group
    *by_lon, lat_keep, lat_send, stay, over, swap, part_tokens, part_cotangent = call(
        layer_kernel,
        [shaped(lon_rows, columns)] * lon_count
        + [shaped(2 * lon_count * rows, columns)] * 2
        + [shaped(2, PART, width)] * 2
        + [shaped(2, 2, PART, width)]
        + [shaped(PART, width)] * 2,
        [
            pltpu.VMEM((CELLS + RIM, width), BF16),
            pltpu.VMEM((CELLS, width), BF16),
            pltpu.VMEM((CELLS, width), BF16),
            pltpu.VMEM((CELLS, width), BF16),
            pltpu.VMEM((CELLS, 3 * group), BF16),
            pltpu.VMEM((CELLS, group), BF16),
            pltpu.VMEM((CELLS, 4 * group), BF16),
            pltpu.VMEM((QUARTERS * PART, 4 * group), BF16),
            pltpu.VMEM((2, QUARTERS * PART, width), BF16),
            pltpu.VMEM((width, 4 * group), BF16),
            pltpu.VMEM((width, 3 * group), BF16),
            pltpu.SemaphoreType.DMA((4,)),
            pltpu.SemaphoreType.DMA((5 * lon_count,)),
        ],
        cost=cost(6 * CELLS * width * width, 8000000),
        name="window_layer",
        far=(w_qkv,),
        far_outs=lon_count + 2,
        limit=32,
    )(
        flat_tokens,
        flat_grad,
        rim_here,
        rim_there,
        gain,
        w_out,
        bias,
        one_hot(shifted_source(), CELLS + RIM),
        quarter_pick(),
    )
    from_lon = [by_lon[0]] + [rotated(by_lon[step], "lon", step) for step in range(1, lon_count)]
    neighbours = [(i, i ^ 1) for i in range(lat_count)]
    from_lat = lax.ppermute(lat_send, "lat", neighbours)
    swapped = lax.ppermute(swap, "head", pairs)
    across = call(
        cores_kernel, shaped(2, PART, width), cost=cost(0, 8 * PART * width), name="sum_over_cores"
    )(over, swapped)
    chips = [(i, i ^ 2) for i in range(QUARTERS)]
    crossed = lax.ppermute(across, "head", chips)
    pieces = call(
        norm_kernel,
        [shaped(2, count, width) for count in (OUT_OWN, OUT_Z, OUT_X + OUT_D)],
        cost=cost(2 * 2 * OUT_ROWS * PART * width, 12 * PART * width),
        name="sum_over_heads",
    )(part_tokens, part_cotangent, gain, group_pick(), stay, swapped, crossed)
    from_west = rotated(pieces[2], "lon", 1)
    to_north, north_mark = call(
        north_kernel,
        [shaped(2, OUT_Z + OUT_D, width), mark],
        cost=cost(0, 8 * (OUT_Z + OUT_D) * width),
        name="rows_for_north",
    )(pieces[1], from_west)
    home = [pieces[0], rotated(to_north, "lat", 1), from_west]
    keep_first, send_first, *by_lon = call(
        functools.partial(second_step_kernel, lon_count),
        [shaped(2 * rows, columns, dtype=F32), shaped(2 * rows, columns)]
        + [shaped(2 * rows, columns, dtype=F32)]
        + [shaped(2 * rows, columns)] * (lon_count - 1),
        cost=cost(4 * lon_rows * columns, 6 * lon_rows * columns),
        name="second_step",
        after=(north_mark,),
    )(*from_lon, lat_keep, from_lat)
    from_lat = lax.ppermute(send_first, "lat", neighbours)
    from_lon = [by_lon[0]] + [rotated(by_lon[step], "lon", step) for step in range(1, lon_count)]
    mine, *each, join_mark = call(
        join_kernel,
        [shaped(2, PART, width)] + [shaped(PART, width)] * 2 + [mark],
        [pltpu.VMEM((2, OUT_ROWS, width), BF16)],
        cost=cost(2 * 2 * OUT_ROWS * PART * width, 8 * OUT_ROWS * width),
        name="join_home",
    )(group_pick(), *home)
    keep, send = call(
        third_step_kernel,
        [shaped(2, rows, columns, dtype=F32), shaped(2, rows, columns)],
        cost=cost(4 * rows * columns, 6 * rows * columns),
        name="third_step",
        after=(join_mark,),
    )(keep_first, from_lat, *from_lon)
    last = lax.ppermute(send, "lat", [(i, i ^ 2) for i in range(lat_count)])
    far = [lax.ppermute(single, "head", chips) for single in each]
    near = lax.ppermute(mine, "head", pairs)
    across = [lax.ppermute(single, "head", pairs) for single in far]
    layer_out, grad_tokens, spread_mark = call(
        spread_kernel,
        [shaped(CELLS, width)] * 2 + [mark],
        [pltpu.VMEM((2, QUARTERS * PART, width), BF16)],
        cost=cost(2 * 2 * CELLS * CELLS * width, 8 * CELLS * width),
        name="spread_outputs",
    )(own_pick(), mine, near, *far, *across)
    flip = rows % 128 == 0
    grad_qkv, grad_out = call(
        functools.partial(finish_kernel, group, flip),
        [
            shaped(rows, 3 * group, dtype=F32),
            shaped(*((group, rows) if flip else (rows, group)), dtype=F32),
        ],
        cost=cost(4 * rows * 4 * group, 16 * rows * 4 * group),
        name="sum_over_lat",
        after=(spread_mark,),
    )(keep, last)
    return (
        layer_out.reshape(tokens.shape),
        grad_tokens.reshape(tokens.shape),
        grad_qkv,
        grad_out if flip else grad_out.T,
    )


def solution(mesh):
    in_specs = (
        P(None, "lat", "lon", None),
        P(),
        P(None, "head"),
        P("head", None),
        P(None, "head"),
        P(None, "lat", "lon", None),
    )
    out_specs = (
        P(None, "lat", "lon", None),
        P(None, "lat", "lon", None),
        P(("lon", "lat"), "head"),
        P("head", ("lon", "lat")),
    )
    return jax.shard_map(body, mesh=mesh, in_specs=in_specs, out_specs=out_specs, check_vma=False)
```

```python
import functools

import jax
import jax.numpy as jnp
import numpy as np
from jax import lax
from jax.experimental import pallas as pl
from jax.experimental.pallas import tpu as pltpu
from jax.sharding import PartitionSpec as P

HEAD_DIM = 64
LEV = 2
WLAT = 6
WLON = 12
TILE_LON = 24
WINDOW = LEV * WLAT * WLON
WINDOWS = TILE_LON // WLON
CELLS = WINDOWS * WINDOW
QUARTERS = 4
PART = 80
MID_LAT = WLAT // 2
MID_LON = WLON // 2
SPAN_LAT = 2 * WLAT - 1
SPAN_LON = 2 * WLON - 1
EPSILON = 1e-05
NEG_FILL = -1e30
F32 = jnp.float32
BF16 = jnp.bfloat16

RIM_Z, RIM_X, RIM_D = 112, 48, 48
RIM = RIM_Z + RIM_X + RIM_D
OUT_OWN, OUT_Z, OUT_X, OUT_D = 32, 32, 16, 16
OUT_STARTS = (0, 32, 64)
OUT_ROWS = 96


def own_row(level, lat, lon):
    return (level * WLAT + lat) * TILE_LON + lon


def window_cells():
    cells = []
    for window in range(WINDOWS):
        for quarter in range(QUARTERS):
            for lat in range(WLAT):
                for half in range(2):
                    for third in range(3):
                        lon = half * MID_LON + (quarter % 2) * 3 + third
                        cells.append((window, quarter // 2, lat, lon))
    return cells


CELL_LIST = window_cells()
CELL_AT = {cell: at for at, cell in enumerate(CELL_LIST)}


def shifted_source():
    z_width = TILE_LON - MID_LON
    rows = []
    for window, level, lat, lon in CELL_LIST:
        column = window * WLON + lon + MID_LON
        if lat < MID_LAT and column < TILE_LON:
            rows.append(own_row(level, lat + MID_LAT, column))
        elif column < TILE_LON:
            rows.append(CELLS + (level * MID_LAT + lat - MID_LAT) * z_width + column - MID_LON)
        else:
            base = CELLS + RIM_Z + (RIM_X if lat >= MID_LAT else 0)
            rows.append(base + (level * MID_LAT + lat % MID_LAT) * MID_LON + column - TILE_LON)
    return np.array(rows)


def quarter_cells(quarter):
    groups = [[], [], [], []]
    for cell in CELL_LIST:
        window, level, lat, lon = cell
        if level != quarter // 2 or lon % MID_LON // 3 != quarter % 2:
            continue
        beyond = window * WLON + lon + MID_LON >= TILE_LON
        groups[2 * beyond + (lat >= MID_LAT)].append(cell)
    return groups


def one_hot(rows, count):
    picked = np.zeros((len(rows), count), np.float32)
    for at, row in enumerate(rows):
        if row >= 0:
            picked[at, row] = 1.0
    return picked.astype(BF16)


def quarter_pick():
    rows = []
    for quarter in range(QUARTERS):
        cells = sum(quarter_cells(quarter), [])
        rows += [CELL_AT[cell] for cell in cells] + [-1] * (PART - len(cells))
    return one_hot(rows, CELLS)


def group_pick():
    rows = []
    start = 0
    for group, padded in zip(quarter_cells(0), (OUT_OWN, OUT_Z, OUT_X, OUT_D)):
        rows += list(range(start, start + len(group))) + [-1] * (padded - len(group))
        start += len(group)
    return one_hot(rows, PART)


def own_pick():
    place = {}
    for quarter in range(QUARTERS):
        for at, (window, level, lat, lon) in enumerate(sum(quarter_cells(quarter), [])):
            column = (window * WLON + lon + MID_LON) % TILE_LON
            row = own_row(level, (lat + MID_LAT) % WLAT, column)
            place[row] = quarter * PART + at
    return one_hot([place[row] for row in range(CELLS)], QUARTERS * PART)


def window_position(shape, dim):
    def count(value, size, parts):
        return sum((value >= size * step).astype(jnp.int32) for step in range(1, parts))

    cell = lax.broadcasted_iota(jnp.int32, shape, dim)
    quarter = count(cell, WINDOW // QUARTERS, QUARTERS)
    cell = cell - quarter * (WINDOW // QUARTERS)
    lat = count(cell, 6, WLAT)
    cell = cell - lat * 6
    half = count(cell, 3, 2)
    level = count(quarter, 2, 2)
    lon = half * MID_LON + (quarter - 2 * level) * 3 + cell - half * 3
    return level, lat, lon


def dot(left, right):
    return lax.dot_general(left, right, (((1,), (0,)), ((), ())), preferred_element_type=F32)


def dot_rows(left, right):
    return lax.dot_general(left, right, (((1,), (1,)), ((), ())), preferred_element_type=F32)


def dot_columns(left, right):
    return lax.dot_general(left, right, (((0,), (0,)), ((), ())), preferred_element_type=F32)


def call(kernel, outs, scratch=(), cost=None, name=None, after=(), far=(), far_outs=0, limit=16):
    def run(*args):
        def body(*refs):
            count = len(args) + len(far)
            kernel(*refs[:count], *refs[count + len(after) :])

        near, outside = pl.BlockSpec(memory_space=pltpu.VMEM), pl.BlockSpec(memory_space=pl.ANY)
        specs = near
        if isinstance(outs, list):
            specs = [outside] * far_outs + [near] * (len(outs) - far_outs)
        return pl.pallas_call(
            body,
            out_shape=outs,
            in_specs=[near] * len(args) + [outside] * (len(far) + len(after)),
            out_specs=specs,
            scratch_shapes=scratch,
            name=name,
            cost_estimate=cost,
            compiler_params=pltpu.CompilerParams(vmem_limit_bytes=limit * 1024 * 1024),
        )(*args, *far, *after)

    return run


def cost(flops, moved):
    return pl.CostEstimate(flops=flops, bytes_accessed=moved, transcendentals=0)


def rim_rows(shape):
    row = lax.broadcasted_iota(jnp.int32, shape, 1)
    level = (row >= WLAT * TILE_LON).astype(jnp.int32)
    row = row - level * WLAT * TILE_LON
    lat = sum((row >= TILE_LON * count).astype(jnp.int32) for count in range(1, WLAT))
    lon = row - lat * TILE_LON
    line = level * MID_LAT + lat
    z_row = line * (TILE_LON - MID_LON) + lon - MID_LON
    d_row = RIM_Z + RIM_X + line * MID_LON + lon
    x_row = RIM_Z + (line - MID_LAT) * MID_LON + lon
    west = lon < MID_LON
    return jnp.where(
        lat < MID_LAT, jnp.where(west, d_row, z_row), jnp.where(west, x_row, -1)
    )


def pack_kernel(tokens, cotangent, rim_z, rim_x, rim_d, source, sems):
    core = lax.rem(lax.axis_index("head"), 2)
    pieces = sems.shape[0]
    rows = CELLS // pieces

    def load(array):
        copies = []
        for piece in range(pieces):
            part = pl.ds(piece * rows, rows)
            copies.append(pltpu.make_async_copy(array.at[part], source.at[part], sems.at[piece]))
        for copy in copies:
            copy.start()
        for copy in copies:
            copy.wait()

    pl.when(core == 0)(lambda: load(tokens))
    pl.when(core != 0)(lambda: load(cotangent))
    wanted = lax.broadcasted_iota(jnp.int32, (RIM, CELLS), 0) == rim_rows((RIM, CELLS))
    rim = dot(wanted.astype(F32).astype(BF16), source[...]).astype(BF16)
    rim_z[...] = rim[:RIM_Z]
    rim_x[...] = rim[RIM_Z : RIM_Z + RIM_X]
    rim_d[...] = rim[RIM_Z + RIM_X :]


def rims_kernel(rim_z, rim_x, rim_d, rim):
    rim[:RIM_Z] = rim_z[...]
    rim[RIM_Z : RIM_Z + RIM_X] = rim_x[...]
    rim[RIM_Z + RIM_X :] = rim_d[...]


def bias_kernel(table, bias, mark, padded, shifted, parts):
    mark[...] = jnp.zeros_like(mark)
    heads = bias.shape[0]
    width = shifted.shape[1]
    padded[...] = jnp.zeros_like(padded)
    padded[:heads, : table.shape[1]] = table[...]
    for head in range(heads):
        spread = jnp.broadcast_to(padded[head : head + 1, :], (16, padded.shape[1]))
        rolled = pltpu.roll(spread, 0, 1, stride=1, stride_axis=0)[:, :width]
        high = rolled.astype(BF16)
        rest = rolled - high.astype(F32)
        middle = rest.astype(BF16)
        low = (rest - middle.astype(F32)).astype(BF16)
        for split, value in enumerate((high, middle, low)):
            shifted[(head * 3 + split) * 16 : (head * 3 + split + 1) * 16, :] = value
    place = lax.broadcasted_iota(jnp.int32, (width, WINDOW), 0)
    count = LEV * WLAT * 16
    level_of, lat_of, lon_of = window_position((1, WINDOW), 1)
    plane = SPAN_LAT * SPAN_LON
    column = plane * (level_of + LEV - 1) + SPAN_LON * (lat_of + WLAT - 1) + lon_of + WLON - 1
    for level in range(LEV):
        for lat in range(WLAT):
            wanted = (place == column - (plane * level + SPAN_LON * lat)).astype(F32).astype(BF16)
            block = dot(shifted[...], wanted).astype(BF16)
            start = (level * WLAT + lat) * 16
            for head in range(heads):
                for split in range(3):
                    first = (head * 3 + split) * 16
                    parts[head, split * count + start : split * count + start + 16, :] = block[
                        first : first + 16
                    ]
    level_in, lat_in, lon_in = window_position((WINDOW, 1), 0)
    lane = lax.broadcasted_iota(jnp.int32, (WINDOW, 3 * count), 1)
    lane = lane - count * ((lane >= count).astype(jnp.int32) + (lane >= 2 * count).astype(jnp.int32))
    rows = (lane == (level_in * WLAT + lat_in) * 16 + lon_in).astype(F32).astype(BF16)
    last = lax.axis_index("lat") == lax.axis_size("lat") - 1
    south_in = (lat_in < MID_LAT).astype(jnp.int32)
    south_of = (lat_of < MID_LAT).astype(jnp.int32)
    added = jnp.where((south_in != south_of) & last, NEG_FILL, 0.0)
    for head in range(heads):
        bias[head] = dot(rows, parts[head]) + added


def scaled_rows(values):
    floats = values.astype(F32)
    center = floats - jnp.mean(floats, axis=-1, keepdims=True)
    inverse = lax.rsqrt(jnp.mean(center * center, axis=-1, keepdims=True) + EPSILON)
    return center * inverse, inverse


def attend(window, projected, d_attended, bias, merged, group):
    cells = slice(window * WINDOW, (window + 1) * WINDOW)
    scale = HEAD_DIM**-0.5
    heads = range(bias.shape[0])

    def part(head, kind):
        first = (3 * head + kind) * HEAD_DIM
        return projected[cells, first : first + HEAD_DIM]

    queries = [part(head, 0) * jnp.asarray(scale, BF16) for head in heads]
    keys = [part(head, 1) for head in heads]
    values = [part(head, 2) for head in heads]
    grads = [d_attended[cells, HEAD_DIM * head : HEAD_DIM * (head + 1)] for head in heads]
    scores = [dot_rows(keys[head], queries[head]) + bias[head] for head in heads]
    grad_probs = [dot_rows(values[head], grads[head]) for head in heads]
    halves, grad_scores = [], []
    for head in heads:
        raised = jnp.exp(scores[head] - jnp.max(scores[head], axis=0, keepdims=True))
        prob = raised * (1.0 / jnp.sum(raised, axis=0, keepdims=True))
        row_term = jnp.sum(prob * grad_probs[head], axis=0, keepdims=True)
        halves.append(prob.astype(BF16))
        grad_scores.append((prob * (grad_probs[head] - row_term)).astype(BF16))
    for head in heads:
        attended = dot_columns(halves[head], values[head])
        grad_value = dot(halves[head], grads[head])
        grad_query = dot_columns(grad_scores[head], keys[head]) * scale
        grad_key = dot(grad_scores[head], queries[head])
        merged[cells, HEAD_DIM * head : HEAD_DIM * (head + 1)] = attended.astype(BF16)
        first = group + 3 * HEAD_DIM * head
        merged[cells, first : first + 3 * HEAD_DIM] = jnp.concatenate(
            [grad_query, grad_key, grad_value], axis=1
        ).astype(BF16)


def lat_copies(whole, columns, out, lon_count, parity, sems, first):
    rows = whole.shape[0] // (4 * lon_count)
    copies = []
    for block in range(2 * lon_count):
        start = pl.multiple_of((2 * block + parity) * rows, rows)
        source, target = whole.at[pl.ds(start, rows), columns], out.at[pl.ds(block * rows, rows)]
        copies.append(pltpu.make_async_copy(source, target, sems.at[first + block]))
    return copies


def layer_kernel(
    tokens,
    cotangent,
    rim_here,
    rim_there,
    gain,
    w_out,
    bias,
    shift_pick,
    quarter,
    w_far,
    *refs,
):
    *by_lon, lat_keep, lat_send, stay, over, swap, part_tokens, part_cotangent = refs[:-13]
    source, near_tokens, near_grad, normed, projected, d_attended, merged = refs[-13:-6]
    ordered, terms, whole, w_qkv, load_sems, store_sems = refs[-6:]
    pieces = load_sems.shape[0]
    loads = []
    for piece in range(pieces):
        count = w_qkv.shape[0] // pieces
        part = pl.ds(piece * count, count)
        loads.append(
            pltpu.make_async_copy(w_far.at[part], w_qkv.at[part], load_sems.at[piece])
        )
        loads[-1].start()
    head_index = lax.axis_index("head")
    core = lax.rem(head_index, 2)
    heads = bias.shape[0]
    group = heads * HEAD_DIM
    source[CELLS:, :] = jnp.where(core == 0, rim_here[...], rim_there[...])
    source[:CELLS, :] = tokens[...]
    near_tokens[...] = dot(shift_pick[...], source[...]).astype(BF16)
    source[CELLS:, :] = jnp.where(core == 0, rim_there[...], rim_here[...])
    source[:CELLS, :] = cotangent[...]
    near_grad[...] = dot(shift_pick[...], source[...]).astype(BF16)
    scaled, _ = scaled_rows(near_tokens[...])
    normed[...] = (scaled * gain[...]).astype(BF16)
    d_attended[...] = dot_rows(near_grad[...], w_out[...]).astype(BF16)
    for load in loads:
        load.wait()
    projected[...] = dot(normed[...], w_qkv[...]).astype(BF16)
    for window in range(WINDOWS):
        attend(window, projected, d_attended, bias, merged, group)
    whole[:, : 3 * group] = dot_columns(normed[...], merged[:, group:]).astype(BF16)
    whole[:, 3 * group :] = dot_columns(near_grad[...], merged[:, :group]).astype(BF16)
    lon, lon_count = lax.axis_index("lon"), len(by_lon)
    rows = by_lon[0].shape[0]
    stores = []
    for step, block in enumerate(by_lon):
        start = pl.multiple_of(lax.rem(lon + step, lon_count) * rows, rows)
        source_rows = whole.at[pl.ds(start, rows), pl.ds(0, 2 * group)]
        stores.append(pltpu.make_async_copy(source_rows, block, store_sems.at[step]))
    parity = lax.rem(lax.axis_index("lat"), 2)
    later = pl.ds(2 * group, 2 * group)
    stores += lat_copies(whole, later, lat_keep, lon_count, parity, store_sems, lon_count)
    stores += lat_copies(whole, later, lat_send, lon_count, 1 - parity, store_sems, 3 * lon_count)
    for store in stores:
        store.start()
    ordered[...] = dot(quarter[...], merged[...]).astype(BF16)
    terms[0] = dot(ordered[:, :group], w_out[...]).astype(BF16)
    terms[1] = dot_rows(ordered[:, group:], w_qkv[...]).astype(BF16)

    def term(owner):
        return terms[:, pl.ds(pl.multiple_of(owner * PART, 16), PART), :]

    far = lax.rem(head_index + 2, QUARTERS)
    stay[...] = term(head_index)
    over[...] = term(far)
    swap[0] = term(head_index + 1 - 2 * core)
    swap[1] = term(far + 1 - 2 * core)
    mine = quarter[pl.ds(pl.multiple_of(head_index * PART, 16), PART), :]
    part_tokens[...] = dot(mine, near_tokens[...]).astype(BF16)
    part_cotangent[...] = dot(mine, near_grad[...]).astype(BF16)
    for store in stores:
        store.wait()


def cores_kernel(over, swapped, total):
    total[...] = (over[...].astype(F32) + swapped[1].astype(F32)).astype(BF16)


def total_of(parts):
    total = parts[0].astype(F32)
    for part in parts[1:]:
        total = total + part.astype(F32)
    return total


def second_step_kernel(lon_count, *refs):
    from_lon, (lat_keep, from_lat) = refs[:lon_count], refs[lon_count : lon_count + 2]
    keep_first, send_first, *by_lon, mark = refs[lon_count + 2 :]
    mark[...] = jnp.zeros_like(mark)
    rows = keep_first.shape[0] // 2
    lon, parity = lax.axis_index("lon"), lax.rem(lax.axis_index("lat"), 2)
    for out, wanted in ((keep_first, parity), (send_first, 1 - parity)):
        for block in range(2):
            part = pl.ds(pl.multiple_of((2 * block + wanted) * rows, rows), rows)
            total = total_of([piece[part, :] for piece in from_lon])
            out[block * rows : (block + 1) * rows, :] = total.astype(out.dtype)
    for step, out in enumerate(by_lon):
        start = lax.rem(lon + step, lon_count) * 2 * rows
        part = pl.ds(pl.multiple_of(start, rows), 2 * rows)
        out[...] = total_of([lat_keep[part, :], from_lat[part, :]]).astype(out.dtype)


def third_step_kernel(keep_first, from_lat, *refs):
    from_lon, (keep, send, mark) = refs[:-3], refs[-3:]
    mark[...] = jnp.zeros_like(mark)
    rows = keep.shape[1]
    mine = lax.div(lax.axis_index("lat"), 2)
    for half, parts in enumerate(((keep_first, from_lat), from_lon)):
        for out, block in ((keep, mine), (send, 1 - mine)):
            part = pl.ds(pl.multiple_of(block * rows, rows), rows)
            out[half] = total_of([piece[part, :] for piece in parts]).astype(out.dtype)


def finish_kernel(group, flip, keep, arrived, grad_qkv, grad_out):
    grad_qkv[:, : 2 * group] = keep[0] + arrived[0].astype(F32)
    total = keep[1] + arrived[1].astype(F32)
    grad_qkv[:, 2 * group :] = total[:, :group]
    out = total[:, group:]
    grad_out[...] = out.T if flip else out


def norm_kernel(part_tokens, part_cotangent, gain, pick, stay, swapped, crossed, *refs):
    *outs, mark = refs
    mark[...] = jnp.zeros_like(mark)
    layer = part_tokens[...].astype(F32)
    attn = stay[0].astype(F32) + swapped[0, 0].astype(F32) + crossed[0].astype(F32)
    d_normed = stay[1].astype(F32) + swapped[0, 1].astype(F32) + crossed[1].astype(F32)
    scaled, inverse = scaled_rows(part_tokens[...])
    grad = d_normed * gain[...]
    mean_grad = jnp.mean(grad, axis=-1, keepdims=True)
    mean_mixed = jnp.mean(grad * scaled, axis=-1, keepdims=True)
    change = (grad - mean_grad - scaled * mean_mixed) * inverse
    for at, value in enumerate((layer + attn, part_cotangent[...].astype(F32) + change)):
        rows = dot(pick[...], value.astype(BF16)).astype(BF16)
        for start, out in zip(OUT_STARTS, outs):
            out[at] = rows[start : start + out.shape[1]]


def north_kernel(z_rows, x_rows, rows, mark):
    mark[...] = jnp.zeros_like(mark)
    rows[:, :OUT_Z, :] = z_rows[...]
    rows[:, OUT_Z:, :] = x_rows[:, OUT_X:, :]


def join_kernel(pick, own, z_rows, x_rows, layer, grad, rows):
    rows[:, :OUT_OWN, :] = own[...]
    rows[:, OUT_OWN : OUT_OWN + OUT_Z, :] = z_rows[:, :OUT_Z, :]
    rows[:, OUT_OWN + OUT_Z : OUT_ROWS - OUT_D, :] = x_rows[:, :OUT_X, :]
    rows[:, OUT_ROWS - OUT_D :, :] = z_rows[:, OUT_Z:, :]
    for at, single in enumerate((layer, grad)):
        single[...] = dot_columns(pick[...], rows[at]).astype(BF16)


def spread_kernel(pick, *refs):
    arrived, outs, (mark, gathered) = refs[:8], refs[8:10], refs[10:]
    mark[...] = jnp.zeros_like(mark)
    head_index = lax.axis_index("head")
    sibling = 1 - 2 * lax.rem(head_index, 2)
    over = lax.rem(head_index + 2, QUARTERS)
    owners = (head_index, head_index + sibling, over, over + sibling)
    for at, out in enumerate(outs):
        for owner, piece in zip(owners, arrived[at::2]):
            gathered[at, pl.ds(pl.multiple_of(owner * PART, 16), PART), :] = piece[...]
        out[...] = dot(pick[...], gathered[at]).astype(BF16)


def shaped(*shape, dtype=BF16):
    return jax.ShapeDtypeStruct(shape, dtype)


def rotated(value, axis, step):
    count = lax.axis_size(axis)
    return lax.ppermute(value, axis, [(i, (i + step) % count) for i in range(count)])


def moved(value, lat_step, lon_step):
    lon_count, lat_count = lax.axis_size("lon"), lax.axis_size("lat")
    pairs = []
    for lon in range(lon_count):
        for lat in range(lat_count):
            target = (lon + lon_step) % lon_count * lat_count + (lat + lat_step) % lat_count
            pairs.append((lon * lat_count + lat, target))
    return lax.ppermute(value, ("lon", "lat"), pairs)


def body(tokens, norm_gain, w_qkv, w_out, bias_table, cotangent):
    level_count, lat_cells, lon_cells, width = tokens.shape
    heads = bias_table.shape[1]
    group = w_out.shape[0]
    lon_count, lat_count = lax.axis_size("lon"), lax.axis_size("lat")
    flat_tokens = tokens.reshape(CELLS, width)
    flat_grad = cotangent.reshape(CELLS, width)
    gain = norm_gain.reshape(1, width)
    mark = shaped(8, 128, dtype=F32)
    rims = call(
        pack_kernel,
        [shaped(RIM_Z, width), shaped(RIM_X, width), shaped(RIM_D, width)],
        [pltpu.VMEM((CELLS, width), BF16), pltpu.SemaphoreType.DMA((6,))],
        cost=cost(2 * RIM * CELLS * width, 4 * CELLS * width),
        name="pack_rims",
        far=tuple(
            pltpu.with_memory_space_constraint(array, pltpu.HBM)
            for array in (flat_tokens, flat_grad)
        ),
    )()
    arrived = [moved(rims[0], -1, 0), moved(rims[1], 0, -1), moved(rims[2], -1, -1)]
    bias, bias_mark = call(
        bias_kernel,
        [shaped(heads, WINDOW, WINDOW, dtype=F32), mark],
        [
            pltpu.VMEM((8, 1024), F32),
            pltpu.VMEM((heads * 48, 768), BF16),
            pltpu.VMEM((heads, 576, WINDOW), BF16),
        ],
        cost=cost(2 * 192 * 768 * 144 * 12 * 2, 1000000),
        name="window_bias",
    )(bias_table.T)
    rim_here = call(
        rims_kernel, shaped(RIM, width), name="join_rims", cost=cost(0, 4 * RIM * width), after=(bias_mark,)
    )(*arrived)
    pairs = [(i, i ^ 1) for i in range(QUARTERS)]
    rim_there = lax.ppermute(rim_here, "head", pairs)
    lon_rows = width // lon_count
    rows = lon_rows // lat_count
    columns = 2 * group
    *by_lon, lat_keep, lat_send, stay, over, swap, part_tokens, part_cotangent = call(
        layer_kernel,
        [shaped(lon_rows, columns)] * lon_count
        + [shaped(2 * lon_count * rows, columns)] * 2
        + [shaped(2, PART, width)] * 2
        + [shaped(2, 2, PART, width)]
        + [shaped(PART, width)] * 2,
        [
            pltpu.VMEM((CELLS + RIM, width), BF16),
            pltpu.VMEM((CELLS, width), BF16),
            pltpu.VMEM((CELLS, width), BF16),
            pltpu.VMEM((CELLS, width), BF16),
            pltpu.VMEM((CELLS, 3 * group), BF16),
            pltpu.VMEM((CELLS, group), BF16),
            pltpu.VMEM((CELLS, 4 * group), BF16),
            pltpu.VMEM((QUARTERS * PART, 4 * group), BF16),
            pltpu.VMEM((2, QUARTERS * PART, width), BF16),
            pltpu.VMEM((width, 4 * group), BF16),
            pltpu.VMEM((width, 3 * group), BF16),
            pltpu.SemaphoreType.DMA((4,)),
            pltpu.SemaphoreType.DMA((5 * lon_count,)),
        ],
        cost=cost(6 * CELLS * width * width, 8000000),
        name="window_layer",
        far=(w_qkv,),
        far_outs=lon_count + 2,
        limit=32,
    )(
        flat_tokens,
        flat_grad,
        rim_here,
        rim_there,
        gain,
        w_out,
        bias,
        one_hot(shifted_source(), CELLS + RIM),
        quarter_pick(),
    )
    from_lon = [by_lon[0]] + [rotated(by_lon[step], "lon", step) for step in range(1, lon_count)]
    neighbours = [(i, i ^ 1) for i in range(lat_count)]
    from_lat = lax.ppermute(lat_send, "lat", neighbours)
    swapped = lax.ppermute(swap, "head", pairs)
    across = call(
        cores_kernel, shaped(2, PART, width), cost=cost(0, 8 * PART * width), name="sum_over_cores"
    )(over, swapped)
    chips = [(i, i ^ 2) for i in range(QUARTERS)]
    crossed = lax.ppermute(across, "head", chips)
    *pieces, norm_mark = call(
        norm_kernel,
        [shaped(2, count, width) for count in (OUT_OWN, OUT_Z, OUT_X + OUT_D)] + [mark],
        cost=cost(2 * 2 * OUT_ROWS * PART * width, 12 * PART * width),
        name="sum_over_heads",
    )(part_tokens, part_cotangent, gain, group_pick(), stay, swapped, crossed)
    keep_first, send_first, *by_lon, second_mark = call(
        functools.partial(second_step_kernel, lon_count),
        [shaped(2 * rows, columns, dtype=F32), shaped(2 * rows, columns)]
        + [shaped(2 * rows, columns, dtype=F32)]
        + [shaped(2 * rows, columns)] * (lon_count - 1)
        + [mark],
        cost=cost(4 * lon_rows * columns, 6 * lon_rows * columns),
        name="second_step",
        after=(norm_mark,),
    )(*from_lon, lat_keep, from_lat)
    from_lat = lax.ppermute(send_first, "lat", neighbours)
    from_lon = [by_lon[0]] + [rotated(by_lon[step], "lon", step) for step in range(1, lon_count)]
    from_west = rotated(pieces[2], "lon", 1)
    to_north, north_mark = call(
        north_kernel,
        [shaped(2, OUT_Z + OUT_D, width), mark],
        cost=cost(0, 8 * (OUT_Z + OUT_D) * width),
        name="rows_for_north",
        after=(second_mark,),
    )(pieces[1], from_west)
    home = [pieces[0], rotated(to_north, "lat", 1), from_west]
    keep, send, third_mark = call(
        third_step_kernel,
        [shaped(2, rows, columns, dtype=F32), shaped(2, rows, columns), mark],
        cost=cost(4 * rows * columns, 6 * rows * columns),
        name="third_step",
        after=(north_mark,),
    )(keep_first, from_lat, *from_lon)
    last = lax.ppermute(send, "lat", [(i, i ^ 2) for i in range(lat_count)])
    each = call(
        join_kernel,
        [shaped(PART, width)] * 2,
        [pltpu.VMEM((2, OUT_ROWS, width), BF16)],
        cost=cost(2 * 2 * OUT_ROWS * PART * width, 8 * OUT_ROWS * width),
        name="join_home",
        after=(third_mark,),
    )(group_pick(), *home)
    far = [lax.ppermute(single, "head", chips) for single in each]
    near = [lax.ppermute(single, "head", pairs) for single in each]
    across = [lax.ppermute(single, "head", pairs) for single in far]
    layer_out, grad_tokens, spread_mark = call(
        spread_kernel,
        [shaped(CELLS, width)] * 2 + [mark],
        [pltpu.VMEM((2, QUARTERS * PART, width), BF16)],
        cost=cost(2 * 2 * CELLS * CELLS * width, 8 * CELLS * width),
        name="spread_outputs",
    )(own_pick(), *each, *near, *far, *across)
    flip = rows % 128 == 0
    grad_qkv, grad_out = call(
        functools.partial(finish_kernel, group, flip),
        [
            shaped(rows, 3 * group, dtype=F32),
            shaped(*((group, rows) if flip else (rows, group)), dtype=F32),
        ],
        cost=cost(4 * rows * 4 * group, 16 * rows * 4 * group),
        name="sum_over_lat",
        after=(spread_mark,),
    )(keep, last)
    return (
        layer_out.reshape(tokens.shape),
        grad_tokens.reshape(tokens.shape),
        grad_qkv,
        grad_out if flip else grad_out.T,
    )


def solution(mesh):
    in_specs = (
        P(None, "lat", "lon", None),
        P(),
        P(None, "head"),
        P("head", None),
        P(None, "head"),
        P(None, "lat", "lon", None),
    )
    out_specs = (
        P(None, "lat", "lon", None),
        P(None, "lat", "lon", None),
        P(("lon", "lat"), "head"),
        P("head", ("lon", "lat")),
    )
    return jax.shard_map(body, mesh=mesh, in_specs=in_specs, out_specs=out_specs, check_vma=False)
```

```python
import functools

import jax
import jax.numpy as jnp
import numpy as np
from jax import lax
from jax.experimental import pallas as pl
from jax.experimental.pallas import tpu as pltpu
from jax.sharding import PartitionSpec as P

HEAD_DIM = 64
LEV = 2
WLAT = 6
WLON = 12
TILE_LON = 24
WINDOW = LEV * WLAT * WLON
WINDOWS = TILE_LON // WLON
CELLS = WINDOWS * WINDOW
QUARTERS = 4
PART = 72
STRIDE = 80
MID_LAT = WLAT // 2
MID_LON = WLON // 2
SPAN_LAT = 2 * WLAT - 1
SPAN_LON = 2 * WLON - 1
EPSILON = 1e-05
NEG_FILL = -1e30
F32 = jnp.float32
BF16 = jnp.bfloat16

RIM_Z, RIM_X, RIM_D = 112, 48, 48
RIM = RIM_Z + RIM_X + RIM_D
OUT_STARTS = (0, 32, 64)
OUT_SIZES = (32, 32, 32)
OUT_ROWS = 96
NORTH_ROWS = 40


def own_row(level, lat, lon):
    return (level * WLAT + lat) * TILE_LON + lon


def window_cells():
    cells = []
    for window in range(WINDOWS):
        for quarter in range(QUARTERS):
            for lat in range(WLAT):
                for half in range(2):
                    for third in range(3):
                        lon = half * MID_LON + (quarter % 2) * 3 + third
                        cells.append((window, quarter // 2, lat, lon))
    return cells


CELL_LIST = window_cells()
CELL_AT = {cell: at for at, cell in enumerate(CELL_LIST)}


def shifted_source():
    z_width = TILE_LON - MID_LON
    rows = []
    for window, level, lat, lon in CELL_LIST:
        column = window * WLON + lon + MID_LON
        if lat < MID_LAT and column < TILE_LON:
            rows.append(own_row(level, lat + MID_LAT, column))
        elif column < TILE_LON:
            rows.append(CELLS + (level * MID_LAT + lat - MID_LAT) * z_width + column - MID_LON)
        else:
            base = CELLS + RIM_Z + (RIM_X if lat >= MID_LAT else 0)
            rows.append(base + (level * MID_LAT + lat % MID_LAT) * MID_LON + column - TILE_LON)
    return np.array(rows)


def quarter_cells(quarter):
    groups = [[], [], [], []]
    for cell in CELL_LIST:
        window, level, lat, lon = cell
        if level != quarter // 2 or lon % MID_LON // 3 != quarter % 2:
            continue
        beyond = window * WLON + lon + MID_LON >= TILE_LON
        groups[2 * beyond + (lat >= MID_LAT)].append(cell)
    return groups


def one_hot(rows, count):
    picked = np.zeros((len(rows), count), np.float32)
    for at, row in enumerate(rows):
        if row >= 0:
            picked[at, row] = 1.0
    return picked.astype(BF16)


def quarter_pick():
    rows = []
    for quarter in range(QUARTERS):
        cells = sum(quarter_cells(quarter), [])
        rows += [CELL_AT[cell] for cell in cells] + [-1] * (STRIDE - len(cells))
    return one_hot(rows, CELLS)


def group_sizes():
    return [len(group) for group in quarter_cells(0)]


def group_pick():
    stay, north, east, corner = group_sizes()
    rows = list(range(stay)) + [-1] * (OUT_STARTS[1] - stay)
    rows += list(range(stay, stay + north)) + [-1] * (OUT_STARTS[2] - OUT_STARTS[1] - north)
    rows += list(range(stay + north, PART)) + [-1] * (OUT_ROWS - OUT_STARTS[2] - east - corner)
    return one_hot(rows, PART)


def own_pick():
    place = {}
    for quarter in range(QUARTERS):
        for at, (window, level, lat, lon) in enumerate(sum(quarter_cells(quarter), [])):
            column = (window * WLON + lon + MID_LON) % TILE_LON
            row = own_row(level, (lat + MID_LAT) % WLAT, column)
            place[row] = quarter * STRIDE + at
    return one_hot([place[row] for row in range(CELLS)], QUARTERS * STRIDE)


def window_position(shape, dim):
    def count(value, size, parts):
        return sum((value >= size * step).astype(jnp.int32) for step in range(1, parts))

    cell = lax.broadcasted_iota(jnp.int32, shape, dim)
    quarter = count(cell, WINDOW // QUARTERS, QUARTERS)
    cell = cell - quarter * (WINDOW // QUARTERS)
    lat = count(cell, 6, WLAT)
    cell = cell - lat * 6
    half = count(cell, 3, 2)
    level = count(quarter, 2, 2)
    lon = half * MID_LON + (quarter - 2 * level) * 3 + cell - half * 3
    return level, lat, lon


def dot(left, right):
    return lax.dot_general(left, right, (((1,), (0,)), ((), ())), preferred_element_type=F32)


def dot_rows(left, right):
    return lax.dot_general(left, right, (((1,), (1,)), ((), ())), preferred_element_type=F32)


def dot_columns(left, right):
    return lax.dot_general(left, right, (((0,), (0,)), ((), ())), preferred_element_type=F32)


def call(kernel, outs, scratch=(), cost=None, name=None, after=(), far=(), far_outs=0, limit=16):
    def run(*args):
        def body(*refs):
            count = len(args) + len(far)
            kernel(*refs[:count], *refs[count + len(after) :])

        near, outside = pl.BlockSpec(memory_space=pltpu.VMEM), pl.BlockSpec(memory_space=pl.ANY)
        specs = near
        if isinstance(outs, list):
            specs = [outside] * far_outs + [near] * (len(outs) - far_outs)
        return pl.pallas_call(
            body,
            out_shape=outs,
            in_specs=[near] * len(args) + [outside] * (len(far) + len(after)),
            out_specs=specs,
            scratch_shapes=scratch,
            name=name,
            cost_estimate=cost,
            compiler_params=pltpu.CompilerParams(vmem_limit_bytes=limit * 1024 * 1024),
        )(*args, *far, *after)

    return run


def cost(flops, moved):
    return pl.CostEstimate(flops=flops, bytes_accessed=moved, transcendentals=0)


def rim_rows(shape):
    row = lax.broadcasted_iota(jnp.int32, shape, 1)
    level = (row >= WLAT * TILE_LON).astype(jnp.int32)
    row = row - level * WLAT * TILE_LON
    lat = sum((row >= TILE_LON * count).astype(jnp.int32) for count in range(1, WLAT))
    lon = row - lat * TILE_LON
    line = level * MID_LAT + lat
    z_row = line * (TILE_LON - MID_LON) + lon - MID_LON
    d_row = RIM_Z + RIM_X + line * MID_LON + lon
    x_row = RIM_Z + (line - MID_LAT) * MID_LON + lon
    west = lon < MID_LON
    return jnp.where(
        lat < MID_LAT, jnp.where(west, d_row, z_row), jnp.where(west, x_row, -1)
    )


def pack_kernel(tokens, cotangent, rim_z, rim_x, rim_d, source, sems):
    core = lax.rem(lax.axis_index("head"), 2)
    pieces = sems.shape[0]
    rows = CELLS // pieces

    def load(array):
        copies = []
        for piece in range(pieces):
            part = pl.ds(piece * rows, rows)
            copies.append(pltpu.make_async_copy(array.at[part], source.at[part], sems.at[piece]))
        for copy in copies:
            copy.start()
        for copy in copies:
            copy.wait()

    pl.when(core == 0)(lambda: load(tokens))
    pl.when(core != 0)(lambda: load(cotangent))
    wanted = lax.broadcasted_iota(jnp.int32, (RIM, CELLS), 0) == rim_rows((RIM, CELLS))
    rim = dot(wanted.astype(F32).astype(BF16), source[...]).astype(BF16)
    rim_z[...] = rim[:RIM_Z]
    rim_x[...] = rim[RIM_Z : RIM_Z + RIM_X]
    rim_d[...] = rim[RIM_Z + RIM_X :]


def rims_kernel(rim_z, rim_x, rim_d, rim):
    rim[:RIM_Z] = rim_z[...]
    rim[RIM_Z : RIM_Z + RIM_X] = rim_x[...]
    rim[RIM_Z + RIM_X :] = rim_d[...]


def bias_kernel(table, bias, mark, padded, shifted, parts):
    mark[...] = jnp.zeros_like(mark)
    heads = bias.shape[0]
    width = shifted.shape[1]
    padded[...] = jnp.zeros_like(padded)
    padded[:heads, : table.shape[1]] = table[...]
    for head in range(heads):
        spread = jnp.broadcast_to(padded[head : head + 1, :], (16, padded.shape[1]))
        rolled = pltpu.roll(spread, 0, 1, stride=1, stride_axis=0)[:, :width]
        high = rolled.astype(BF16)
        rest = rolled - high.astype(F32)
        middle = rest.astype(BF16)
        low = (rest - middle.astype(F32)).astype(BF16)
        for split, value in enumerate((high, middle, low)):
            shifted[(head * 3 + split) * 16 : (head * 3 + split + 1) * 16, :] = value
    place = lax.broadcasted_iota(jnp.int32, (width, WINDOW), 0)
    count = LEV * WLAT * 16
    level_of, lat_of, lon_of = window_position((1, WINDOW), 1)
    plane = SPAN_LAT * SPAN_LON
    column = plane * (level_of + LEV - 1) + SPAN_LON * (lat_of + WLAT - 1) + lon_of + WLON - 1
    for level in range(LEV):
        for lat in range(WLAT):
            wanted = (place == column - (plane * level + SPAN_LON * lat)).astype(F32).astype(BF16)
            block = dot(shifted[...], wanted).astype(BF16)
            start = (level * WLAT + lat) * 16
            for head in range(heads):
                for split in range(3):
                    first = (head * 3 + split) * 16
                    parts[head, split * count + start : split * count + start + 16, :] = block[
                        first : first + 16
                    ]
    level_in, lat_in, lon_in = window_position((WINDOW, 1), 0)
    lane = lax.broadcasted_iota(jnp.int32, (WINDOW, 3 * count), 1)
    lane = lane - count * ((lane >= count).astype(jnp.int32) + (lane >= 2 * count).astype(jnp.int32))
    rows = (lane == (level_in * WLAT + lat_in) * 16 + lon_in).astype(F32).astype(BF16)
    last = lax.axis_index("lat") == lax.axis_size("lat") - 1
    south_in = (lat_in < MID_LAT).astype(jnp.int32)
    south_of = (lat_of < MID_LAT).astype(jnp.int32)
    added = jnp.where((south_in != south_of) & last, NEG_FILL, 0.0)
    for head in range(heads):
        bias[head] = dot(rows, parts[head]) + added


def scaled_rows(values):
    floats = values.astype(F32)
    center = floats - jnp.mean(floats, axis=-1, keepdims=True)
    inverse = lax.rsqrt(jnp.mean(center * center, axis=-1, keepdims=True) + EPSILON)
    return center * inverse, inverse


def attend(window, projected, d_attended, bias, merged, group):
    cells = slice(window * WINDOW, (window + 1) * WINDOW)
    scale = HEAD_DIM**-0.5
    heads = range(bias.shape[0])

    def part(head, kind):
        first = (3 * head + kind) * HEAD_DIM
        return projected[cells, first : first + HEAD_DIM]

    queries = [part(head, 0) * jnp.asarray(scale, BF16) for head in heads]
    keys = [part(head, 1) for head in heads]
    values = [part(head, 2) for head in heads]
    grads = [d_attended[cells, HEAD_DIM * head : HEAD_DIM * (head + 1)] for head in heads]
    scores = [dot_rows(keys[head], queries[head]) + bias[head] for head in heads]
    grad_probs = [dot_rows(values[head], grads[head]) for head in heads]
    halves, grad_scores = [], []
    for head in heads:
        raised = jnp.exp(scores[head] - jnp.max(scores[head], axis=0, keepdims=True))
        prob = raised * (1.0 / jnp.sum(raised, axis=0, keepdims=True))
        row_term = jnp.sum(prob * grad_probs[head], axis=0, keepdims=True)
        halves.append(prob.astype(BF16))
        grad_scores.append((prob * (grad_probs[head] - row_term)).astype(BF16))
    for head in heads:
        attended = dot_columns(halves[head], values[head])
        grad_value = dot(halves[head], grads[head])
        grad_query = dot_columns(grad_scores[head], keys[head]) * scale
        grad_key = dot(grad_scores[head], queries[head])
        merged[cells, HEAD_DIM * head : HEAD_DIM * (head + 1)] = attended.astype(BF16)
        first = group + 3 * HEAD_DIM * head
        merged[cells, first : first + 3 * HEAD_DIM] = jnp.concatenate(
            [grad_query, grad_key, grad_value], axis=1
        ).astype(BF16)


def lat_copies(whole, columns, out, lon_count, parity, sems, first):
    rows = whole.shape[0] // (4 * lon_count)
    copies = []
    for block in range(2 * lon_count):
        start = pl.multiple_of((2 * block + parity) * rows, rows)
        source, target = whole.at[pl.ds(start, rows), columns], out.at[pl.ds(block * rows, rows)]
        copies.append(pltpu.make_async_copy(source, target, sems.at[first + block]))
    return copies


def layer_kernel(
    tokens,
    cotangent,
    rim_here,
    rim_there,
    gain,
    w_out,
    bias,
    shift_pick,
    quarter,
    w_far,
    *refs,
):
    *by_lon, lat_keep, lat_send, stay, over, swap, part_tokens, part_cotangent = refs[:-13]
    source, near_tokens, near_grad, normed, projected, d_attended, merged = refs[-13:-6]
    ordered, terms, whole, w_qkv, load_sems, store_sems = refs[-6:]
    pieces = load_sems.shape[0]
    loads = []
    for piece in range(pieces):
        count = w_qkv.shape[0] // pieces
        part = pl.ds(piece * count, count)
        loads.append(
            pltpu.make_async_copy(w_far.at[part], w_qkv.at[part], load_sems.at[piece])
        )
        loads[-1].start()
    head_index = lax.axis_index("head")
    core = lax.rem(head_index, 2)
    heads = bias.shape[0]
    group = heads * HEAD_DIM
    source[CELLS:, :] = jnp.where(core == 0, rim_here[...], rim_there[...])
    source[:CELLS, :] = tokens[...]
    near_tokens[...] = dot(shift_pick[...], source[...]).astype(BF16)
    source[CELLS:, :] = jnp.where(core == 0, rim_there[...], rim_here[...])
    source[:CELLS, :] = cotangent[...]
    near_grad[...] = dot(shift_pick[...], source[...]).astype(BF16)
    scaled, _ = scaled_rows(near_tokens[...])
    normed[...] = (scaled * gain[...]).astype(BF16)
    d_attended[...] = dot_rows(near_grad[...], w_out[...]).astype(BF16)
    for load in loads:
        load.wait()
    projected[...] = dot(normed[...], w_qkv[...]).astype(BF16)
    for window in range(WINDOWS):
        attend(window, projected, d_attended, bias, merged, group)
    whole[:, : 3 * group] = dot_columns(normed[...], merged[:, group:]).astype(BF16)
    whole[:, 3 * group :] = dot_columns(near_grad[...], merged[:, :group]).astype(BF16)
    lon, lon_count = lax.axis_index("lon"), len(by_lon)
    rows = by_lon[0].shape[0]
    stores = []
    for step, block in enumerate(by_lon):
        start = pl.multiple_of(lax.rem(lon + step, lon_count) * rows, rows)
        source_rows = whole.at[pl.ds(start, rows), pl.ds(0, 2 * group)]
        stores.append(pltpu.make_async_copy(source_rows, block, store_sems.at[step]))
    parity = lax.rem(lax.axis_index("lat"), 2)
    later = pl.ds(2 * group, 2 * group)
    stores += lat_copies(whole, later, lat_keep, lon_count, parity, store_sems, lon_count)
    stores += lat_copies(whole, later, lat_send, lon_count, 1 - parity, store_sems, 3 * lon_count)
    for store in stores:
        store.start()
    ordered[...] = dot(quarter[...], merged[...]).astype(BF16)
    terms[0] = dot(ordered[:, :group], w_out[...]).astype(BF16)
    terms[1] = dot_rows(ordered[:, group:], w_qkv[...]).astype(BF16)

    def term(owner):
        return terms[:, pl.ds(pl.multiple_of(owner * STRIDE, 16), PART), :]

    far = lax.rem(head_index + 2, QUARTERS)
    stay[...] = term(head_index)
    over[...] = term(far)
    swap[0] = term(head_index + 1 - 2 * core)
    swap[1] = term(far + 1 - 2 * core)
    mine = quarter[pl.ds(pl.multiple_of(head_index * STRIDE, 16), PART), :]
    part_tokens[...] = dot(mine, near_tokens[...]).astype(BF16)
    part_cotangent[...] = dot(mine, near_grad[...]).astype(BF16)
    for store in stores:
        store.wait()


def cores_kernel(over, swapped, total):
    total[...] = (over[...].astype(F32) + swapped[1].astype(F32)).astype(BF16)


def total_of(parts):
    total = parts[0].astype(F32)
    for part in parts[1:]:
        total = total + part.astype(F32)
    return total


def second_step_kernel(lon_count, *refs):
    from_lon, (lat_keep, from_lat) = refs[:lon_count], refs[lon_count : lon_count + 2]
    keep_first, send_first, *by_lon, mark = refs[lon_count + 2 :]
    mark[...] = jnp.zeros_like(mark)
    rows = keep_first.shape[0] // 2
    lon, parity = lax.axis_index("lon"), lax.rem(lax.axis_index("lat"), 2)
    for out, wanted in ((keep_first, parity), (send_first, 1 - parity)):
        for block in range(2):
            part = pl.ds(pl.multiple_of((2 * block + wanted) * rows, rows), rows)
            total = total_of([piece[part, :] for piece in from_lon])
            out[block * rows : (block + 1) * rows, :] = total.astype(out.dtype)
    for step, out in enumerate(by_lon):
        start = lax.rem(lon + step, lon_count) * 2 * rows
        part = pl.ds(pl.multiple_of(start, rows), 2 * rows)
        out[...] = total_of([lat_keep[part, :], from_lat[part, :]]).astype(out.dtype)


def third_step_kernel(keep_first, from_lat, *refs):
    from_lon, (keep, send, mark) = refs[:-3], refs[-3:]
    mark[...] = jnp.zeros_like(mark)
    rows = keep.shape[1]
    mine = lax.div(lax.axis_index("lat"), 2)
    for half, parts in enumerate(((keep_first, from_lat), from_lon)):
        for out, block in ((keep, mine), (send, 1 - mine)):
            part = pl.ds(pl.multiple_of(block * rows, rows), rows)
            out[half] = total_of([piece[part, :] for piece in parts]).astype(out.dtype)


def finish_kernel(group, flip, keep, arrived, grad_qkv, grad_out):
    grad_qkv[:, : 2 * group] = keep[0] + arrived[0].astype(F32)
    total = keep[1] + arrived[1].astype(F32)
    grad_qkv[:, 2 * group :] = total[:, :group]
    out = total[:, group:]
    grad_out[...] = out.T if flip else out


def norm_kernel(part_tokens, part_cotangent, gain, pick, stay, swapped, crossed, *refs):
    *outs, mark = refs
    mark[...] = jnp.zeros_like(mark)
    layer = part_tokens[...].astype(F32)
    attn = stay[0].astype(F32) + swapped[0, 0].astype(F32) + crossed[0].astype(F32)
    d_normed = stay[1].astype(F32) + swapped[0, 1].astype(F32) + crossed[1].astype(F32)
    scaled, inverse = scaled_rows(part_tokens[...])
    grad = d_normed * gain[...]
    mean_grad = jnp.mean(grad, axis=-1, keepdims=True)
    mean_mixed = jnp.mean(grad * scaled, axis=-1, keepdims=True)
    change = (grad - mean_grad - scaled * mean_mixed) * inverse
    for at, value in enumerate((layer + attn, part_cotangent[...].astype(F32) + change)):
        rows = dot(pick[...], value.astype(BF16)).astype(BF16)
        for start, out in zip(OUT_STARTS, outs):
            out[at] = rows[start : start + out.shape[1]]


def taken(count, source, spans):
    row = lax.broadcasted_iota(jnp.int32, (count, source.shape[0]), 0)
    column = lax.broadcasted_iota(jnp.int32, (count, source.shape[0]), 1)
    wanted = jnp.zeros((count, source.shape[0]), F32)
    for start, first, rows in spans:
        inside = (row >= start) & (row < start + rows)
        wanted = jnp.where(inside & (column == row + (first - start)), 1.0, wanted)
    return dot(wanted.astype(BF16), source)


def north_kernel(z_rows, x_rows, rows, mark):
    mark[...] = jnp.zeros_like(mark)
    _, north, east, corner = group_sizes()
    for at in range(2):
        total = taken(NORTH_ROWS, z_rows[at], [(0, 0, north)])
        total = total + taken(NORTH_ROWS, x_rows[at], [(north, east, corner)])
        rows[at] = total.astype(BF16)


def join_kernel(own, z_rows, x_rows, layer, grad):
    stay, north, east, corner = group_sizes()
    for at, joined in enumerate((layer, grad)):
        total = taken(PART, own[at], [(0, 0, stay)])
        spans = [(stay, 0, north), (stay + north + east, north, corner)]
        total = total + taken(PART, z_rows[at], spans)
        total = total + taken(PART, x_rows[at], [(stay + north, 0, east)])
        joined[...] = total.astype(BF16)


def pass_kernel(arrived, passed):
    passed[...] = arrived[...]


def spread_kernel(pick, *refs):
    arrived, outs, (mark, gathered) = refs[:8], refs[8:10], refs[10:]
    mark[...] = jnp.zeros_like(mark)
    head_index = lax.axis_index("head")
    sibling = 1 - 2 * lax.rem(head_index, 2)
    over = lax.rem(head_index + 2, QUARTERS)
    owners = (head_index, head_index + sibling, over, over + sibling)
    for at, out in enumerate(outs):
        for owner, piece in zip(owners, arrived[at::2]):
            start = pl.multiple_of(owner * STRIDE, 16)
            gathered[at, pl.ds(start + STRIDE - 16, 16), :] = jnp.zeros_like(gathered[at, :16, :])
            gathered[at, pl.ds(start, PART), :] = piece[...]
        out[...] = dot(pick[...], gathered[at]).astype(BF16)


def shaped(*shape, dtype=BF16):
    return jax.ShapeDtypeStruct(shape, dtype)


def rotated(value, axis, step):
    count = lax.axis_size(axis)
    return lax.ppermute(value, axis, [(i, (i + step) % count) for i in range(count)])


def moved(value, lat_step, lon_step):
    lon_count, lat_count = lax.axis_size("lon"), lax.axis_size("lat")
    pairs = []
    for lon in range(lon_count):
        for lat in range(lat_count):
            target = (lon + lon_step) % lon_count * lat_count + (lat + lat_step) % lat_count
            pairs.append((lon * lat_count + lat, target))
    return lax.ppermute(value, ("lon", "lat"), pairs)


def body(tokens, norm_gain, w_qkv, w_out, bias_table, cotangent):
    level_count, lat_cells, lon_cells, width = tokens.shape
    heads = bias_table.shape[1]
    group = w_out.shape[0]
    lon_count, lat_count = lax.axis_size("lon"), lax.axis_size("lat")
    flat_tokens = tokens.reshape(CELLS, width)
    flat_grad = cotangent.reshape(CELLS, width)
    gain = norm_gain.reshape(1, width)
    mark = shaped(8, 128, dtype=F32)
    rims = call(
        pack_kernel,
        [shaped(RIM_Z, width), shaped(RIM_X, width), shaped(RIM_D, width)],
        [pltpu.VMEM((CELLS, width), BF16), pltpu.SemaphoreType.DMA((6,))],
        cost=cost(2 * RIM * CELLS * width, 4 * CELLS * width),
        name="pack_rims",
        far=tuple(
            pltpu.with_memory_space_constraint(array, pltpu.HBM)
            for array in (flat_tokens, flat_grad)
        ),
    )()
    arrived = [moved(rims[0], -1, 0), moved(rims[1], 0, -1), moved(rims[2], -1, -1)]
    bias, bias_mark = call(
        bias_kernel,
        [shaped(heads, WINDOW, WINDOW, dtype=F32), mark],
        [
            pltpu.VMEM((8, 1024), F32),
            pltpu.VMEM((heads * 48, 768), BF16),
            pltpu.VMEM((heads, 576, WINDOW), BF16),
        ],
        cost=cost(2 * 192 * 768 * 144 * 12 * 2, 1000000),
        name="window_bias",
    )(bias_table.T)
    rim_here = call(
        rims_kernel, shaped(RIM, width), name="join_rims", cost=cost(0, 4 * RIM * width), after=(bias_mark,)
    )(*arrived)
    pairs = [(i, i ^ 1) for i in range(QUARTERS)]
    rim_there = lax.ppermute(rim_here, "head", pairs)
    lon_rows = width // lon_count
    rows = lon_rows // lat_count
    columns = 2 * group
    *by_lon, lat_keep, lat_send, stay, over, swap, part_tokens, part_cotangent = call(
        layer_kernel,
        [shaped(lon_rows, columns)] * lon_count
        + [shaped(2 * lon_count * rows, columns)] * 2
        + [shaped(2, PART, width)] * 2
        + [shaped(2, 2, PART, width)]
        + [shaped(PART, width)] * 2,
        [
            pltpu.VMEM((CELLS + RIM, width), BF16),
            pltpu.VMEM((CELLS, width), BF16),
            pltpu.VMEM((CELLS, width), BF16),
            pltpu.VMEM((CELLS, width), BF16),
            pltpu.VMEM((CELLS, 3 * group), BF16),
            pltpu.VMEM((CELLS, group), BF16),
            pltpu.VMEM((CELLS, 4 * group), BF16),
            pltpu.VMEM((QUARTERS * STRIDE, 4 * group), BF16),
            pltpu.VMEM((2, QUARTERS * STRIDE, width), BF16),
            pltpu.VMEM((width, 4 * group), BF16),
            pltpu.VMEM((width, 3 * group), BF16),
            pltpu.SemaphoreType.DMA((4,)),
            pltpu.SemaphoreType.DMA((5 * lon_count,)),
        ],
        cost=cost(6 * CELLS * width * width, 8000000),
        name="window_layer",
        far=(w_qkv,),
        far_outs=lon_count + 2,
        limit=32,
    )(
        flat_tokens,
        flat_grad,
        rim_here,
        rim_there,
        gain,
        w_out,
        bias,
        one_hot(shifted_source(), CELLS + RIM),
        quarter_pick(),
    )
    from_lon = [by_lon[0]] + [rotated(by_lon[step], "lon", step) for step in range(1, lon_count)]
    neighbours = [(i, i ^ 1) for i in range(lat_count)]
    from_lat = lax.ppermute(lat_send, "lat", neighbours)
    swapped = lax.ppermute(swap, "head", pairs)
    across = call(
        cores_kernel, shaped(2, PART, width), cost=cost(0, 8 * PART * width), name="sum_over_cores"
    )(over, swapped)
    chips = [(i, i ^ 2) for i in range(QUARTERS)]
    crossed = lax.ppermute(across, "head", chips)
    *pieces, norm_mark = call(
        norm_kernel,
        [shaped(2, count, width) for count in OUT_SIZES] + [mark],
        cost=cost(2 * 2 * OUT_ROWS * PART * width, 12 * PART * width),
        name="sum_over_heads",
    )(part_tokens, part_cotangent, gain, group_pick(), stay, swapped, crossed)
    keep_first, send_first, *by_lon, second_mark = call(
        functools.partial(second_step_kernel, lon_count),
        [shaped(2 * rows, columns, dtype=F32), shaped(2 * rows, columns)]
        + [shaped(2 * rows, columns, dtype=F32)]
        + [shaped(2 * rows, columns)] * (lon_count - 1)
        + [mark],
        cost=cost(4 * lon_rows * columns, 6 * lon_rows * columns),
        name="second_step",
        after=(norm_mark,),
    )(*from_lon, lat_keep, from_lat)
    from_lat = lax.ppermute(send_first, "lat", neighbours)
    from_lon = [by_lon[0]] + [rotated(by_lon[step], "lon", step) for step in range(1, lon_count)]
    from_west = rotated(pieces[2], "lon", 1)
    to_north, north_mark = call(
        north_kernel,
        [shaped(2, NORTH_ROWS, width), mark],
        cost=cost(0, 8 * NORTH_ROWS * width),
        name="rows_for_north",
        after=(second_mark,),
    )(pieces[1], from_west)
    home = [pieces[0], rotated(to_north, "lat", 1), from_west]
    keep, send, third_mark = call(
        third_step_kernel,
        [shaped(2, rows, columns, dtype=F32), shaped(2, rows, columns), mark],
        cost=cost(4 * rows * columns, 6 * rows * columns),
        name="third_step",
        after=(north_mark,),
    )(keep_first, from_lat, *from_lon)
    last = lax.ppermute(send, "lat", [(i, i ^ 2) for i in range(lat_count)])
    each = call(
        join_kernel,
        [shaped(PART, width)] * 2,
        cost=cost(2 * 2 * OUT_ROWS * PART * width, 8 * OUT_ROWS * width),
        name="join_home",
        after=(third_mark,),
    )(*home)
    far = [lax.ppermute(single, "head", chips) for single in each]
    near = [lax.ppermute(single, "head", pairs) for single in each]
    held = call(
        pass_kernel, shaped(PART, width), name="pass_on", after=(last,), cost=cost(0, 4 * PART * width)
    )(far[1])
    across = [lax.ppermute(single, "head", pairs) for single in (far[0], held)]
    layer_out, grad_tokens, spread_mark = call(
        spread_kernel,
        [shaped(CELLS, width)] * 2 + [mark],
        [pltpu.VMEM((2, QUARTERS * STRIDE, width), BF16)],
        cost=cost(2 * 2 * CELLS * CELLS * width, 8 * CELLS * width),
        name="spread_outputs",
    )(own_pick(), *each, *near, *far, *across)
    flip = rows % 128 == 0
    grad_qkv, grad_out = call(
        functools.partial(finish_kernel, group, flip),
        [
            shaped(rows, 3 * group, dtype=F32),
            shaped(*((group, rows) if flip else (rows, group)), dtype=F32),
        ],
        cost=cost(4 * rows * 4 * group, 16 * rows * 4 * group),
        name="sum_over_lat",
        after=(spread_mark,),
    )(keep, last)
    return (
        layer_out.reshape(tokens.shape),
        grad_tokens.reshape(tokens.shape),
        grad_qkv,
        grad_out if flip else grad_out.T,
    )


def solution(mesh):
    in_specs = (
        P(None, "lat", "lon", None),
        P(),
        P(None, "head"),
        P("head", None),
        P(None, "head"),
        P(None, "lat", "lon", None),
    )
    out_specs = (
        P(None, "lat", "lon", None),
        P(None, "lat", "lon", None),
        P(("lon", "lat"), "head"),
        P("head", ("lon", "lat")),
    )
    return jax.shard_map(body, mesh=mesh, in_specs=in_specs, out_specs=out_specs, check_vma=False)
```

```python
import functools

import jax
import jax.numpy as jnp
import numpy as np
from jax import lax
from jax.experimental import pallas as pl
from jax.experimental.pallas import tpu as pltpu
from jax.sharding import PartitionSpec as P

HEAD_DIM = 64
LEV = 2
WLAT = 6
WLON = 12
TILE_LON = 24
WINDOW = LEV * WLAT * WLON
WINDOWS = TILE_LON // WLON
CELLS = WINDOWS * WINDOW
QUARTERS = 4
PART = 72
STRIDE = 80
MID_LAT = WLAT // 2
MID_LON = WLON // 2
SPAN_LAT = 2 * WLAT - 1
SPAN_LON = 2 * WLON - 1
EPSILON = 1e-05
NEG_FILL = -1e30
F32 = jnp.float32
BF16 = jnp.bfloat16

RIM_Z, RIM_X, RIM_D = 112, 48, 48
RIM = RIM_Z + RIM_X + RIM_D
OUT_STARTS = (0, 32, 64)
OUT_SIZES = (32, 32, 32)
OUT_ROWS = 96
NORTH_ROWS = 40


def own_row(level, lat, lon):
    return (level * WLAT + lat) * TILE_LON + lon


def window_cells():
    cells = []
    for window in range(WINDOWS):
        for quarter in range(QUARTERS):
            for lat in range(WLAT):
                for half in range(2):
                    for third in range(3):
                        lon = half * MID_LON + (quarter % 2) * 3 + third
                        cells.append((window, quarter // 2, lat, lon))
    return cells


CELL_LIST = window_cells()
CELL_AT = {cell: at for at, cell in enumerate(CELL_LIST)}


def shifted_source():
    z_width = TILE_LON - MID_LON
    rows = []
    for window, level, lat, lon in CELL_LIST:
        column = window * WLON + lon + MID_LON
        if lat < MID_LAT and column < TILE_LON:
            rows.append(own_row(level, lat + MID_LAT, column))
        elif column < TILE_LON:
            rows.append(CELLS + (level * MID_LAT + lat - MID_LAT) * z_width + column - MID_LON)
        else:
            base = CELLS + RIM_Z + (RIM_X if lat >= MID_LAT else 0)
            rows.append(base + (level * MID_LAT + lat % MID_LAT) * MID_LON + column - TILE_LON)
    return np.array(rows)


def quarter_cells(quarter):
    groups = [[], [], [], []]
    for cell in CELL_LIST:
        window, level, lat, lon = cell
        if level != quarter // 2 or lon % MID_LON // 3 != quarter % 2:
            continue
        beyond = window * WLON + lon + MID_LON >= TILE_LON
        groups[2 * beyond + (lat >= MID_LAT)].append(cell)
    return groups


def one_hot(rows, count):
    picked = np.zeros((len(rows), count), np.float32)
    for at, row in enumerate(rows):
        if row >= 0:
            picked[at, row] = 1.0
    return picked.astype(BF16)


def quarter_pick():
    rows = []
    for quarter in range(QUARTERS):
        cells = sum(quarter_cells(quarter), [])
        rows += [CELL_AT[cell] for cell in cells] + [-1] * (STRIDE - len(cells))
    return one_hot(rows, CELLS)


def group_sizes():
    return [len(group) for group in quarter_cells(0)]


def group_pick():
    stay, north, east, corner = group_sizes()
    rows = list(range(stay)) + [-1] * (OUT_STARTS[1] - stay)
    rows += list(range(stay, stay + north)) + [-1] * (OUT_STARTS[2] - OUT_STARTS[1] - north)
    rows += list(range(stay + north, PART)) + [-1] * (OUT_ROWS - OUT_STARTS[2] - east - corner)
    return one_hot(rows, PART)


def own_pick():
    place = {}
    for quarter in range(QUARTERS):
        for at, (window, level, lat, lon) in enumerate(sum(quarter_cells(quarter), [])):
            column = (window * WLON + lon + MID_LON) % TILE_LON
            row = own_row(level, (lat + MID_LAT) % WLAT, column)
            place[row] = quarter * STRIDE + at
    return one_hot([place[row] for row in range(CELLS)], QUARTERS * STRIDE)


def window_position(shape, dim):
    def count(value, size, parts):
        return sum((value >= size * step).astype(jnp.int32) for step in range(1, parts))

    cell = lax.broadcasted_iota(jnp.int32, shape, dim)
    quarter = count(cell, WINDOW // QUARTERS, QUARTERS)
    cell = cell - quarter * (WINDOW // QUARTERS)
    lat = count(cell, 6, WLAT)
    cell = cell - lat * 6
    half = count(cell, 3, 2)
    level = count(quarter, 2, 2)
    lon = half * MID_LON + (quarter - 2 * level) * 3 + cell - half * 3
    return level, lat, lon


def dot(left, right):
    return lax.dot_general(left, right, (((1,), (0,)), ((), ())), preferred_element_type=F32)


def dot_rows(left, right):
    return lax.dot_general(left, right, (((1,), (1,)), ((), ())), preferred_element_type=F32)


def dot_columns(left, right):
    return lax.dot_general(left, right, (((0,), (0,)), ((), ())), preferred_element_type=F32)


def call(kernel, outs, scratch=(), cost=None, name=None, after=(), far=(), far_outs=0, limit=16):
    def run(*args):
        def body(*refs):
            count = len(args) + len(far)
            kernel(*refs[:count], *refs[count + len(after) :])

        near, outside = pl.BlockSpec(memory_space=pltpu.VMEM), pl.BlockSpec(memory_space=pl.ANY)
        specs = near
        if isinstance(outs, list):
            specs = [outside] * far_outs + [near] * (len(outs) - far_outs)
        return pl.pallas_call(
            body,
            out_shape=outs,
            in_specs=[near] * len(args) + [outside] * (len(far) + len(after)),
            out_specs=specs,
            scratch_shapes=scratch,
            name=name,
            cost_estimate=cost,
            compiler_params=pltpu.CompilerParams(vmem_limit_bytes=limit * 1024 * 1024),
        )(*args, *far, *after)

    return run


def cost(flops, moved):
    return pl.CostEstimate(flops=flops, bytes_accessed=moved, transcendentals=0)


def rim_rows(shape):
    row = lax.broadcasted_iota(jnp.int32, shape, 1)
    level = (row >= WLAT * TILE_LON).astype(jnp.int32)
    row = row - level * WLAT * TILE_LON
    lat = sum((row >= TILE_LON * count).astype(jnp.int32) for count in range(1, WLAT))
    lon = row - lat * TILE_LON
    line = level * MID_LAT + lat
    z_row = line * (TILE_LON - MID_LON) + lon - MID_LON
    d_row = RIM_Z + RIM_X + line * MID_LON + lon
    x_row = RIM_Z + (line - MID_LAT) * MID_LON + lon
    west = lon < MID_LON
    return jnp.where(
        lat < MID_LAT, jnp.where(west, d_row, z_row), jnp.where(west, x_row, -1)
    )


def pack_kernel(tokens, cotangent, rim_z, rim_x, rim_d, source, sems):
    core = lax.rem(lax.axis_index("head"), 2)
    pieces = sems.shape[0]
    rows = CELLS // pieces

    def load(array):
        copies = []
        for piece in range(pieces):
            part = pl.ds(piece * rows, rows)
            copies.append(pltpu.make_async_copy(array.at[part], source.at[part], sems.at[piece]))
        for copy in copies:
            copy.start()
        for copy in copies:
            copy.wait()

    pl.when(core == 0)(lambda: load(tokens))
    pl.when(core != 0)(lambda: load(cotangent))
    wanted = lax.broadcasted_iota(jnp.int32, (RIM, CELLS), 0) == rim_rows((RIM, CELLS))
    rim = dot(wanted.astype(F32).astype(BF16), source[...]).astype(BF16)
    rim_z[...] = rim[:RIM_Z]
    rim_x[...] = rim[RIM_Z : RIM_Z + RIM_X]
    rim_d[...] = rim[RIM_Z + RIM_X :]


def rims_kernel(rim_z, rim_x, rim_d, rim):
    rim[:RIM_Z] = rim_z[...]
    rim[RIM_Z : RIM_Z + RIM_X] = rim_x[...]
    rim[RIM_Z + RIM_X :] = rim_d[...]


def bias_kernel(table, bias, mark, padded, shifted, parts):
    mark[...] = jnp.zeros_like(mark)
    heads = bias.shape[0]
    width = shifted.shape[1]
    padded[...] = jnp.zeros_like(padded)
    padded[:heads, : table.shape[1]] = table[...]
    for head in range(heads):
        spread = jnp.broadcast_to(padded[head : head + 1, :], (16, padded.shape[1]))
        rolled = pltpu.roll(spread, 0, 1, stride=1, stride_axis=0)[:, :width]
        high = rolled.astype(BF16)
        rest = rolled - high.astype(F32)
        middle = rest.astype(BF16)
        low = (rest - middle.astype(F32)).astype(BF16)
        for split, value in enumerate((high, middle, low)):
            shifted[(head * 3 + split) * 16 : (head * 3 + split + 1) * 16, :] = value
    place = lax.broadcasted_iota(jnp.int32, (width, WINDOW), 0)
    count = LEV * WLAT * 16
    level_of, lat_of, lon_of = window_position((1, WINDOW), 1)
    plane = SPAN_LAT * SPAN_LON
    column = plane * (level_of + LEV - 1) + SPAN_LON * (lat_of + WLAT - 1) + lon_of + WLON - 1
    for level in range(LEV):
        for lat in range(WLAT):
            wanted = (place == column - (plane * level + SPAN_LON * lat)).astype(F32).astype(BF16)
            block = dot(shifted[...], wanted).astype(BF16)
            start = (level * WLAT + lat) * 16
            for head in range(heads):
                for split in range(3):
                    first = (head * 3 + split) * 16
                    parts[head, split * count + start : split * count + start + 16, :] = block[
                        first : first + 16
                    ]
    level_in, lat_in, lon_in = window_position((WINDOW, 1), 0)
    lane = lax.broadcasted_iota(jnp.int32, (WINDOW, 3 * count), 1)
    lane = lane - count * ((lane >= count).astype(jnp.int32) + (lane >= 2 * count).astype(jnp.int32))
    rows = (lane == (level_in * WLAT + lat_in) * 16 + lon_in).astype(F32).astype(BF16)
    last = lax.axis_index("lat") == lax.axis_size("lat") - 1
    south_in = (lat_in < MID_LAT).astype(jnp.int32)
    south_of = (lat_of < MID_LAT).astype(jnp.int32)
    added = jnp.where((south_in != south_of) & last, NEG_FILL, 0.0)
    for head in range(heads):
        bias[head] = dot(rows, parts[head]) + added


def scaled_rows(values):
    floats = values.astype(F32)
    center = floats - jnp.mean(floats, axis=-1, keepdims=True)
    inverse = lax.rsqrt(jnp.mean(center * center, axis=-1, keepdims=True) + EPSILON)
    return center * inverse, inverse


def attend(window, projected, d_attended, bias, merged, group):
    cells = slice(window * WINDOW, (window + 1) * WINDOW)
    scale = HEAD_DIM**-0.5
    heads = range(bias.shape[0])

    def part(head, kind):
        first = (3 * head + kind) * HEAD_DIM
        return projected[cells, first : first + HEAD_DIM]

    queries = [part(head, 0) * jnp.asarray(scale, BF16) for head in heads]
    keys = [part(head, 1) for head in heads]
    values = [part(head, 2) for head in heads]
    grads = [d_attended[cells, HEAD_DIM * head : HEAD_DIM * (head + 1)] for head in heads]
    scores = [dot_rows(keys[head], queries[head]) + bias[head] for head in heads]
    grad_probs = [dot_rows(values[head], grads[head]) for head in heads]
    halves, grad_scores = [], []
    for head in heads:
        raised = jnp.exp(scores[head] - jnp.max(scores[head], axis=0, keepdims=True))
        prob = raised * (1.0 / jnp.sum(raised, axis=0, keepdims=True))
        row_term = jnp.sum(prob * grad_probs[head], axis=0, keepdims=True)
        halves.append(prob.astype(BF16))
        grad_scores.append((prob * (grad_probs[head] - row_term)).astype(BF16))
    for head in heads:
        attended = dot_columns(halves[head], values[head])
        grad_value = dot(halves[head], grads[head])
        grad_query = dot_columns(grad_scores[head], keys[head]) * scale
        grad_key = dot(grad_scores[head], queries[head])
        merged[cells, HEAD_DIM * head : HEAD_DIM * (head + 1)] = attended.astype(BF16)
        first = group + 3 * HEAD_DIM * head
        merged[cells, first : first + 3 * HEAD_DIM] = jnp.concatenate(
            [grad_query, grad_key, grad_value], axis=1
        ).astype(BF16)


def lat_copies(whole, columns, out, lon_count, parity, sems, first):
    rows = whole.shape[0] // (4 * lon_count)
    copies = []
    for block in range(2 * lon_count):
        start = pl.multiple_of((2 * block + parity) * rows, rows)
        source, target = whole.at[pl.ds(start, rows), columns], out.at[pl.ds(block * rows, rows)]
        copies.append(pltpu.make_async_copy(source, target, sems.at[first + block]))
    return copies


def layer_kernel(
    tokens,
    cotangent,
    rim_here,
    rim_there,
    gain,
    w_out,
    bias,
    shift_pick,
    quarter,
    w_far,
    *refs,
):
    *by_lon, lat_keep, lat_send, stay, over, swap, part_tokens, part_cotangent = refs[:-13]
    source, near_tokens, near_grad, normed, projected, d_attended, merged = refs[-13:-6]
    ordered, terms, whole, w_qkv, load_sems, store_sems = refs[-6:]
    pieces = load_sems.shape[0]
    loads = []
    for piece in range(pieces):
        count = w_qkv.shape[0] // pieces
        part = pl.ds(piece * count, count)
        loads.append(
            pltpu.make_async_copy(w_far.at[part], w_qkv.at[part], load_sems.at[piece])
        )
        loads[-1].start()
    head_index = lax.axis_index("head")
    core = lax.rem(head_index, 2)
    heads = bias.shape[0]
    group = heads * HEAD_DIM
    source[CELLS:, :] = jnp.where(core == 0, rim_here[...], rim_there[...])
    source[:CELLS, :] = tokens[...]
    near_tokens[...] = dot(shift_pick[...], source[...]).astype(BF16)
    source[CELLS:, :] = jnp.where(core == 0, rim_there[...], rim_here[...])
    source[:CELLS, :] = cotangent[...]
    near_grad[...] = dot(shift_pick[...], source[...]).astype(BF16)
    scaled, _ = scaled_rows(near_tokens[...])
    normed[...] = (scaled * gain[...]).astype(BF16)
    d_attended[...] = dot_rows(near_grad[...], w_out[...]).astype(BF16)
    for load in loads:
        load.wait()
    projected[...] = dot(normed[...], w_qkv[...]).astype(BF16)
    for window in range(WINDOWS):
        attend(window, projected, d_attended, bias, merged, group)
    whole[:, : 3 * group] = dot_columns(normed[...], merged[:, group:]).astype(BF16)
    whole[:, 3 * group :] = dot_columns(near_grad[...], merged[:, :group]).astype(BF16)
    lon, lon_count = lax.axis_index("lon"), len(by_lon)
    rows = by_lon[0].shape[0]
    stores = []
    for step, block in enumerate(by_lon):
        start = pl.multiple_of(lax.rem(lon + step, lon_count) * rows, rows)
        source_rows = whole.at[pl.ds(start, rows), pl.ds(0, 2 * group)]
        stores.append(pltpu.make_async_copy(source_rows, block, store_sems.at[step]))
    parity = lax.rem(lax.axis_index("lat"), 2)
    later = pl.ds(2 * group, 2 * group)
    stores += lat_copies(whole, later, lat_keep, lon_count, parity, store_sems, lon_count)
    stores += lat_copies(whole, later, lat_send, lon_count, 1 - parity, store_sems, 3 * lon_count)
    for store in stores:
        store.start()
    ordered[...] = dot(quarter[...], merged[...]).astype(BF16)
    terms[0] = dot(ordered[:, :group], w_out[...]).astype(BF16)
    terms[1] = dot_rows(ordered[:, group:], w_qkv[...]).astype(BF16)

    def term(owner):
        return terms[:, pl.ds(pl.multiple_of(owner * STRIDE, 16), PART), :]

    far = lax.rem(head_index + 2, QUARTERS)
    stay[...] = term(head_index)
    over[...] = term(far)
    swap[0] = term(head_index + 1 - 2 * core)
    swap[1] = term(far + 1 - 2 * core)
    mine = quarter[pl.ds(pl.multiple_of(head_index * STRIDE, 16), PART), :]
    part_tokens[...] = dot(mine, near_tokens[...]).astype(BF16)
    part_cotangent[...] = dot(mine, near_grad[...]).astype(BF16)
    for store in stores:
        store.wait()


def cores_kernel(over, swapped, total):
    total[...] = (over[...].astype(F32) + swapped[1].astype(F32)).astype(BF16)


def total_of(parts):
    total = parts[0].astype(F32)
    for part in parts[1:]:
        total = total + part.astype(F32)
    return total


def second_step_kernel(lon_count, *refs):
    from_lon, (lat_keep, from_lat) = refs[:lon_count], refs[lon_count : lon_count + 2]
    keep_first, send_first, *by_lon, mark = refs[lon_count + 2 :]
    mark[...] = jnp.zeros_like(mark)
    rows = keep_first.shape[0] // 2
    lon, parity = lax.axis_index("lon"), lax.rem(lax.axis_index("lat"), 2)
    for out, wanted in ((keep_first, parity), (send_first, 1 - parity)):
        for block in range(2):
            part = pl.ds(pl.multiple_of((2 * block + wanted) * rows, rows), rows)
            total = total_of([piece[part, :] for piece in from_lon])
            out[block * rows : (block + 1) * rows, :] = total.astype(out.dtype)
    for step, out in enumerate(by_lon):
        start = lax.rem(lon + step, lon_count) * 2 * rows
        part = pl.ds(pl.multiple_of(start, rows), 2 * rows)
        out[...] = total_of([lat_keep[part, :], from_lat[part, :]]).astype(out.dtype)


def third_step_kernel(keep_first, from_lat, *refs):
    from_lon, (keep, send, mark) = refs[:-3], refs[-3:]
    mark[...] = jnp.zeros_like(mark)
    rows = keep.shape[1]
    mine = lax.div(lax.axis_index("lat"), 2)
    for half, parts in enumerate(((keep_first, from_lat), from_lon)):
        for out, block in ((keep, mine), (send, 1 - mine)):
            part = pl.ds(pl.multiple_of(block * rows, rows), rows)
            out[half] = total_of([piece[part, :] for piece in parts]).astype(out.dtype)


def finish_kernel(group, flip, keep, arrived, grad_qkv, grad_out):
    grad_qkv[:, : 2 * group] = keep[0] + arrived[0].astype(F32)
    total = keep[1] + arrived[1].astype(F32)
    grad_qkv[:, 2 * group :] = total[:, :group]
    out = total[:, group:]
    grad_out[...] = out.T if flip else out


def norm_kernel(part_tokens, part_cotangent, gain, pick, stay, swapped, crossed, *refs):
    *outs, mark = refs
    mark[...] = jnp.zeros_like(mark)
    layer = part_tokens[...].astype(F32)
    attn = stay[0].astype(F32) + swapped[0, 0].astype(F32) + crossed[0].astype(F32)
    d_normed = stay[1].astype(F32) + swapped[0, 1].astype(F32) + crossed[1].astype(F32)
    scaled, inverse = scaled_rows(part_tokens[...])
    grad = d_normed * gain[...]
    mean_grad = jnp.mean(grad, axis=-1, keepdims=True)
    mean_mixed = jnp.mean(grad * scaled, axis=-1, keepdims=True)
    change = (grad - mean_grad - scaled * mean_mixed) * inverse
    for at, value in enumerate((layer + attn, part_cotangent[...].astype(F32) + change)):
        rows = dot(pick[...], value.astype(BF16)).astype(BF16)
        for start, out in zip(OUT_STARTS, outs):
            out[at] = rows[start : start + out.shape[1]]


def taken(count, source, spans):
    row = lax.broadcasted_iota(jnp.int32, (count, source.shape[0]), 0)
    column = lax.broadcasted_iota(jnp.int32, (count, source.shape[0]), 1)
    wanted = jnp.zeros((count, source.shape[0]), F32)
    for start, first, rows in spans:
        inside = (row >= start) & (row < start + rows)
        wanted = jnp.where(inside & (column == row + (first - start)), 1.0, wanted)
    return dot(wanted.astype(BF16), source)


def north_kernel(z_rows, x_rows, rows, mark):
    mark[...] = jnp.zeros_like(mark)
    _, north, east, corner = group_sizes()
    for at in range(2):
        total = taken(NORTH_ROWS, z_rows[at], [(0, 0, north)])
        total = total + taken(NORTH_ROWS, x_rows[at], [(north, east, corner)])
        rows[at] = total.astype(BF16)


def join_kernel(own, z_rows, x_rows, layer, grad):
    stay, north, east, corner = group_sizes()
    for at, joined in enumerate((layer, grad)):
        total = taken(PART, own[at], [(0, 0, stay)])
        spans = [(stay, 0, north), (stay + north + east, north, corner)]
        total = total + taken(PART, z_rows[at], spans)
        total = total + taken(PART, x_rows[at], [(stay + north, 0, east)])
        joined[...] = total.astype(BF16)


def spread_kernel(pick, *refs):
    arrived, outs, (mark, gathered) = refs[:8], refs[8:10], refs[10:]
    mark[...] = jnp.zeros_like(mark)
    head_index = lax.axis_index("head")
    sibling = 1 - 2 * lax.rem(head_index, 2)
    over = lax.rem(head_index + 2, QUARTERS)
    owners = (head_index, head_index + sibling, over, over + sibling)
    for at, out in enumerate(outs):
        for owner, piece in zip(owners, arrived[at::2]):
            start = pl.multiple_of(owner * STRIDE, 16)
            gathered[at, pl.ds(start + STRIDE - 16, 16), :] = jnp.zeros_like(gathered[at, :16, :])
            gathered[at, pl.ds(start, PART), :] = piece[...]
        out[...] = dot(pick[...], gathered[at]).astype(BF16)


def shaped(*shape, dtype=BF16):
    return jax.ShapeDtypeStruct(shape, dtype)


def rotated(value, axis, step):
    count = lax.axis_size(axis)
    return lax.ppermute(value, axis, [(i, (i + step) % count) for i in range(count)])


def moved(value, lat_step, lon_step):
    lon_count, lat_count = lax.axis_size("lon"), lax.axis_size("lat")
    pairs = []
    for lon in range(lon_count):
        for lat in range(lat_count):
            target = (lon + lon_step) % lon_count * lat_count + (lat + lat_step) % lat_count
            pairs.append((lon * lat_count + lat, target))
    return lax.ppermute(value, ("lon", "lat"), pairs)


def body(tokens, norm_gain, w_qkv, w_out, bias_table, cotangent):
    level_count, lat_cells, lon_cells, width = tokens.shape
    heads = bias_table.shape[1]
    group = w_out.shape[0]
    lon_count, lat_count = lax.axis_size("lon"), lax.axis_size("lat")
    flat_tokens = tokens.reshape(CELLS, width)
    flat_grad = cotangent.reshape(CELLS, width)
    gain = norm_gain.reshape(1, width)
    mark = shaped(8, 128, dtype=F32)
    rims = call(
        pack_kernel,
        [shaped(RIM_Z, width), shaped(RIM_X, width), shaped(RIM_D, width)],
        [pltpu.VMEM((CELLS, width), BF16), pltpu.SemaphoreType.DMA((6,))],
        cost=cost(2 * RIM * CELLS * width, 4 * CELLS * width),
        name="pack_rims",
        far=tuple(
            pltpu.with_memory_space_constraint(array, pltpu.HBM)
            for array in (flat_tokens, flat_grad)
        ),
    )()
    arrived = [moved(rims[0], -1, 0), moved(rims[1], 0, -1), moved(rims[2], -1, -1)]
    bias, bias_mark = call(
        bias_kernel,
        [shaped(heads, WINDOW, WINDOW, dtype=F32), mark],
        [
            pltpu.VMEM((8, 1024), F32),
            pltpu.VMEM((heads * 48, 768), BF16),
            pltpu.VMEM((heads, 576, WINDOW), BF16),
        ],
        cost=cost(2 * 192 * 768 * 144 * 12 * 2, 1000000),
        name="window_bias",
    )(bias_table.T)
    rim_here = call(
        rims_kernel, shaped(RIM, width), name="join_rims", cost=cost(0, 4 * RIM * width), after=(bias_mark,)
    )(*arrived)
    pairs = [(i, i ^ 1) for i in range(QUARTERS)]
    rim_there = lax.ppermute(rim_here, "head", pairs)
    lon_rows = width // lon_count
    rows = lon_rows // lat_count
    columns = 2 * group
    *by_lon, lat_keep, lat_send, stay, over, swap, part_tokens, part_cotangent = call(
        layer_kernel,
        [shaped(lon_rows, columns)] * lon_count
        + [shaped(2 * lon_count * rows, columns)] * 2
        + [shaped(2, PART, width)] * 2
        + [shaped(2, 2, PART, width)]
        + [shaped(PART, width)] * 2,
        [
            pltpu.VMEM((CELLS + RIM, width), BF16),
            pltpu.VMEM((CELLS, width), BF16),
            pltpu.VMEM((CELLS, width), BF16),
            pltpu.VMEM((CELLS, width), BF16),
            pltpu.VMEM((CELLS, 3 * group), BF16),
            pltpu.VMEM((CELLS, group), BF16),
            pltpu.VMEM((CELLS, 4 * group), BF16),
            pltpu.VMEM((QUARTERS * STRIDE, 4 * group), BF16),
            pltpu.VMEM((2, QUARTERS * STRIDE, width), BF16),
            pltpu.VMEM((width, 4 * group), BF16),
            pltpu.VMEM((width, 3 * group), BF16),
            pltpu.SemaphoreType.DMA((4,)),
            pltpu.SemaphoreType.DMA((5 * lon_count,)),
        ],
        cost=cost(6 * CELLS * width * width, 8000000),
        name="window_layer",
        far=(w_qkv,),
        far_outs=lon_count + 2,
        limit=32,
    )(
        flat_tokens,
        flat_grad,
        rim_here,
        rim_there,
        gain,
        w_out,
        bias,
        one_hot(shifted_source(), CELLS + RIM),
        quarter_pick(),
    )
    from_lon = [by_lon[0]] + [rotated(by_lon[step], "lon", step) for step in range(1, lon_count)]
    neighbours = [(i, i ^ 1) for i in range(lat_count)]
    from_lat = lax.ppermute(lat_send, "lat", neighbours)
    swapped = lax.ppermute(swap, "head", pairs)
    across = call(
        cores_kernel, shaped(2, PART, width), cost=cost(0, 8 * PART * width), name="sum_over_cores"
    )(over, swapped)
    chips = [(i, i ^ 2) for i in range(QUARTERS)]
    crossed = lax.ppermute(across, "head", chips)
    *pieces, norm_mark = call(
        norm_kernel,
        [shaped(2, count, width) for count in OUT_SIZES] + [mark],
        cost=cost(2 * 2 * OUT_ROWS * PART * width, 12 * PART * width),
        name="sum_over_heads",
    )(part_tokens, part_cotangent, gain, group_pick(), stay, swapped, crossed)
    keep_first, send_first, *by_lon, second_mark = call(
        functools.partial(second_step_kernel, lon_count),
        [shaped(2 * rows, columns, dtype=F32), shaped(2 * rows, columns)]
        + [shaped(2 * rows, columns, dtype=F32)]
        + [shaped(2 * rows, columns)] * (lon_count - 1)
        + [mark],
        cost=cost(4 * lon_rows * columns, 6 * lon_rows * columns),
        name="second_step",
        after=(norm_mark,),
    )(*from_lon, lat_keep, from_lat)
    from_lat = lax.ppermute(send_first, "lat", neighbours)
    from_lon = [by_lon[0]] + [rotated(by_lon[step], "lon", step) for step in range(1, lon_count)]
    from_west = rotated(pieces[2], "lon", 1)
    to_north, north_mark = call(
        north_kernel,
        [shaped(2, NORTH_ROWS, width), mark],
        cost=cost(0, 8 * NORTH_ROWS * width),
        name="rows_for_north",
        after=(second_mark,),
    )(pieces[1], from_west)
    home = [pieces[0], rotated(to_north, "lat", 1), from_west]
    keep, send, third_mark = call(
        third_step_kernel,
        [shaped(2, rows, columns, dtype=F32), shaped(2, rows, columns), mark],
        cost=cost(4 * rows * columns, 6 * rows * columns),
        name="third_step",
        after=(north_mark,),
    )(keep_first, from_lat, *from_lon)
    last = lax.ppermute(send, "lat", [(i, i ^ 2) for i in range(lat_count)])
    each = call(
        join_kernel,
        [shaped(PART, width)] * 2,
        cost=cost(2 * 2 * OUT_ROWS * PART * width, 8 * OUT_ROWS * width),
        name="join_home",
        after=(third_mark,),
    )(*home)
    far = [lax.ppermute(single, "head", chips) for single in each]
    near = [lax.ppermute(single, "head", pairs) for single in each]
    across = [lax.ppermute(single, "head", pairs) for single in far]
    layer_out, grad_tokens, spread_mark = call(
        spread_kernel,
        [shaped(CELLS, width)] * 2 + [mark],
        [pltpu.VMEM((2, QUARTERS * STRIDE, width), BF16)],
        cost=cost(2 * 2 * CELLS * CELLS * width, 8 * CELLS * width),
        name="spread_outputs",
    )(own_pick(), *each, *near, *far, *across)
    flip = rows % 128 == 0
    grad_qkv, grad_out = call(
        functools.partial(finish_kernel, group, flip),
        [
            shaped(rows, 3 * group, dtype=F32),
            shaped(*((group, rows) if flip else (rows, group)), dtype=F32),
        ],
        cost=cost(4 * rows * 4 * group, 16 * rows * 4 * group),
        name="sum_over_lat",
        after=(spread_mark,),
    )(keep, last)
    return (
        layer_out.reshape(tokens.shape),
        grad_tokens.reshape(tokens.shape),
        grad_qkv,
        grad_out if flip else grad_out.T,
    )


def solution(mesh):
    in_specs = (
        P(None, "lat", "lon", None),
        P(),
        P(None, "head"),
        P("head", None),
        P(None, "head"),
        P(None, "lat", "lon", None),
    )
    out_specs = (
        P(None, "lat", "lon", None),
        P(None, "lat", "lon", None),
        P(("lon", "lat"), "head"),
        P("head", ("lon", "lat")),
    )
    return jax.shard_map(body, mesh=mesh, in_specs=in_specs, out_specs=out_specs, check_vma=False)
```

```python
import functools

import jax
import jax.numpy as jnp
import numpy as np
from jax import lax
from jax.experimental import pallas as pl
from jax.experimental.pallas import tpu as pltpu
from jax.sharding import PartitionSpec as P

HEAD_DIM = 64
LEV = 2
WLAT = 6
WLON = 12
TILE_LON = 24
WINDOW = LEV * WLAT * WLON
WINDOWS = TILE_LON // WLON
CELLS = WINDOWS * WINDOW
QUARTERS = 4
PART = 72
STRIDE = 80
MID_LAT = WLAT // 2
MID_LON = WLON // 2
SPAN_LAT = 2 * WLAT - 1
SPAN_LON = 2 * WLON - 1
EPSILON = 1e-05
NEG_FILL = -1e30
F32 = jnp.float32
BF16 = jnp.bfloat16

RIM_Z, RIM_X, RIM_D = 112, 48, 48
RIM = RIM_Z + RIM_X + RIM_D
OUT_STARTS = (0, 32, 64)
OUT_SIZES = (32, 32, 32)
OUT_ROWS = 112
PIECES = 3
SLOT = 32
NORTH_ROWS = 40


def own_row(level, lat, lon):
    return (level * WLAT + lat) * TILE_LON + lon


def window_cells():
    cells = []
    for window in range(WINDOWS):
        for quarter in range(QUARTERS):
            for lat in range(WLAT):
                for half in range(2):
                    for third in range(3):
                        lon = half * MID_LON + (quarter % 2) * 3 + third
                        cells.append((window, quarter // 2, lat, lon))
    return cells


CELL_LIST = window_cells()
CELL_AT = {cell: at for at, cell in enumerate(CELL_LIST)}


def shifted_source():
    z_width = TILE_LON - MID_LON
    rows = []
    for window, level, lat, lon in CELL_LIST:
        column = window * WLON + lon + MID_LON
        if lat < MID_LAT and column < TILE_LON:
            rows.append(own_row(level, lat + MID_LAT, column))
        elif column < TILE_LON:
            rows.append(CELLS + (level * MID_LAT + lat - MID_LAT) * z_width + column - MID_LON)
        else:
            base = CELLS + RIM_Z + (RIM_X if lat >= MID_LAT else 0)
            rows.append(base + (level * MID_LAT + lat % MID_LAT) * MID_LON + column - TILE_LON)
    return np.array(rows)


def quarter_cells(quarter):
    groups = [[], [], [], []]
    for cell in CELL_LIST:
        window, level, lat, lon = cell
        if level != quarter // 2 or lon % MID_LON // 3 != quarter % 2:
            continue
        beyond = window * WLON + lon + MID_LON >= TILE_LON
        groups[2 * beyond + (lat >= MID_LAT)].append(cell)
    return groups


def one_hot(rows, count):
    picked = np.zeros((len(rows), count), np.float32)
    for at, row in enumerate(rows):
        if row >= 0:
            picked[at, row] = 1.0
    return picked.astype(BF16)


def quarter_pick():
    rows = []
    for quarter in range(QUARTERS):
        cells = sum(quarter_cells(quarter), [])
        rows += [CELL_AT[cell] for cell in cells] + [-1] * (STRIDE - len(cells))
    return one_hot(rows, CELLS)


def group_sizes():
    return [len(group) for group in quarter_cells(0)]


def group_pick():
    stay, north, east, corner = group_sizes()
    rows = list(range(stay)) + [-1] * (OUT_STARTS[1] - stay)
    rows += list(range(stay, stay + north)) + [-1] * (OUT_STARTS[2] - OUT_STARTS[1] - north)
    rows += list(range(stay + north, PART)) + [-1] * (OUT_ROWS - OUT_STARTS[2] - east - corner)
    return one_hot(rows, PART)


def own_pick():
    place = {}
    for quarter in range(QUARTERS):
        for at, (window, level, lat, lon) in enumerate(sum(quarter_cells(quarter), [])):
            column = (window * WLON + lon + MID_LON) % TILE_LON
            row = own_row(level, (lat + MID_LAT) % WLAT, column)
            place[row] = (quarter * PIECES + at // (PART // PIECES)) * SLOT + at % (PART // PIECES)
    return one_hot([place[row] for row in range(CELLS)], QUARTERS * PIECES * SLOT)


def window_position(shape, dim):
    def count(value, size, parts):
        return sum((value >= size * step).astype(jnp.int32) for step in range(1, parts))

    cell = lax.broadcasted_iota(jnp.int32, shape, dim)
    quarter = count(cell, WINDOW // QUARTERS, QUARTERS)
    cell = cell - quarter * (WINDOW // QUARTERS)
    lat = count(cell, 6, WLAT)
    cell = cell - lat * 6
    half = count(cell, 3, 2)
    level = count(quarter, 2, 2)
    lon = half * MID_LON + (quarter - 2 * level) * 3 + cell - half * 3
    return level, lat, lon


def dot(left, right):
    return lax.dot_general(left, right, (((1,), (0,)), ((), ())), preferred_element_type=F32)


def dot_rows(left, right):
    return lax.dot_general(left, right, (((1,), (1,)), ((), ())), preferred_element_type=F32)


def dot_columns(left, right):
    return lax.dot_general(left, right, (((0,), (0,)), ((), ())), preferred_element_type=F32)


def call(kernel, outs, scratch=(), cost=None, name=None, after=(), far=(), far_outs=0, limit=16):
    def run(*args):
        def body(*refs):
            count = len(args) + len(far)
            kernel(*refs[:count], *refs[count + len(after) :])

        near, outside = pl.BlockSpec(memory_space=pltpu.VMEM), pl.BlockSpec(memory_space=pl.ANY)
        specs = near
        if isinstance(outs, list):
            specs = [outside] * far_outs + [near] * (len(outs) - far_outs)
        return pl.pallas_call(
            body,
            out_shape=outs,
            in_specs=[near] * len(args) + [outside] * (len(far) + len(after)),
            out_specs=specs,
            scratch_shapes=scratch,
            name=name,
            cost_estimate=cost,
            compiler_params=pltpu.CompilerParams(vmem_limit_bytes=limit * 1024 * 1024),
        )(*args, *far, *after)

    return run


def cost(flops, moved):
    return pl.CostEstimate(flops=flops, bytes_accessed=moved, transcendentals=0)


def rim_rows(shape):
    row = lax.broadcasted_iota(jnp.int32, shape, 1)
    level = (row >= WLAT * TILE_LON).astype(jnp.int32)
    row = row - level * WLAT * TILE_LON
    lat = sum((row >= TILE_LON * count).astype(jnp.int32) for count in range(1, WLAT))
    lon = row - lat * TILE_LON
    line = level * MID_LAT + lat
    z_row = line * (TILE_LON - MID_LON) + lon - MID_LON
    d_row = RIM_Z + RIM_X + line * MID_LON + lon
    x_row = RIM_Z + (line - MID_LAT) * MID_LON + lon
    west = lon < MID_LON
    return jnp.where(
        lat < MID_LAT, jnp.where(west, d_row, z_row), jnp.where(west, x_row, -1)
    )


def pack_kernel(tokens, cotangent, rim_z, rim_x, rim_d, source, sems):
    core = lax.rem(lax.axis_index("head"), 2)
    pieces = sems.shape[0]
    rows = CELLS // pieces

    def load(array):
        copies = []
        for piece in range(pieces):
            part = pl.ds(piece * rows, rows)
            copies.append(pltpu.make_async_copy(array.at[part], source.at[part], sems.at[piece]))
        for copy in copies:
            copy.start()
        for copy in copies:
            copy.wait()

    pl.when(core == 0)(lambda: load(tokens))
    pl.when(core != 0)(lambda: load(cotangent))
    wanted = lax.broadcasted_iota(jnp.int32, (RIM, CELLS), 0) == rim_rows((RIM, CELLS))
    rim = dot(wanted.astype(F32).astype(BF16), source[...]).astype(BF16)
    rim_z[...] = rim[:RIM_Z]
    rim_x[...] = rim[RIM_Z : RIM_Z + RIM_X]
    rim_d[...] = rim[RIM_Z + RIM_X :]


def hold_kernel(rim, held):
    held[...] = rim[...]


def rims_kernel(x_rim, d_rim, rim):
    rim[:RIM_X] = x_rim[...]
    rim[RIM_X:] = d_rim[...]


def bias_kernel(table, bias, mark, padded, shifted, parts):
    mark[...] = jnp.zeros_like(mark)
    heads = bias.shape[0]
    width = shifted.shape[1]
    padded[...] = jnp.zeros_like(padded)
    padded[:heads, : table.shape[1]] = table[...]
    for head in range(heads):
        spread = jnp.broadcast_to(padded[head : head + 1, :], (16, padded.shape[1]))
        rolled = pltpu.roll(spread, 0, 1, stride=1, stride_axis=0)[:, :width]
        high = rolled.astype(BF16)
        rest = rolled - high.astype(F32)
        middle = rest.astype(BF16)
        low = (rest - middle.astype(F32)).astype(BF16)
        for split, value in enumerate((high, middle, low)):
            shifted[(head * 3 + split) * 16 : (head * 3 + split + 1) * 16, :] = value
    place = lax.broadcasted_iota(jnp.int32, (width, WINDOW), 0)
    count = LEV * WLAT * 16
    level_of, lat_of, lon_of = window_position((1, WINDOW), 1)
    plane = SPAN_LAT * SPAN_LON
    column = plane * (level_of + LEV - 1) + SPAN_LON * (lat_of + WLAT - 1) + lon_of + WLON - 1
    for level in range(LEV):
        for lat in range(WLAT):
            wanted = (place == column - (plane * level + SPAN_LON * lat)).astype(F32).astype(BF16)
            block = dot(shifted[...], wanted).astype(BF16)
            start = (level * WLAT + lat) * 16
            for head in range(heads):
                for split in range(3):
                    first = (head * 3 + split) * 16
                    parts[head, split * count + start : split * count + start + 16, :] = block[
                        first : first + 16
                    ]
    level_in, lat_in, lon_in = window_position((WINDOW, 1), 0)
    lane = lax.broadcasted_iota(jnp.int32, (WINDOW, 3 * count), 1)
    lane = lane - count * ((lane >= count).astype(jnp.int32) + (lane >= 2 * count).astype(jnp.int32))
    rows = (lane == (level_in * WLAT + lat_in) * 16 + lon_in).astype(F32).astype(BF16)
    last = lax.axis_index("lat") == lax.axis_size("lat") - 1
    south_in = (lat_in < MID_LAT).astype(jnp.int32)
    south_of = (lat_of < MID_LAT).astype(jnp.int32)
    added = jnp.where((south_in != south_of) & last, NEG_FILL, 0.0)
    for head in range(heads):
        bias[head] = dot(rows, parts[head]) + added


def scaled_rows(values):
    floats = values.astype(F32)
    center = floats - jnp.mean(floats, axis=-1, keepdims=True)
    inverse = lax.rsqrt(jnp.mean(center * center, axis=-1, keepdims=True) + EPSILON)
    return center * inverse, inverse


def attend(window, projected, d_attended, bias, merged, group):
    cells = slice(window * WINDOW, (window + 1) * WINDOW)
    scale = HEAD_DIM**-0.5
    heads = range(bias.shape[0])

    def part(head, kind):
        first = (3 * head + kind) * HEAD_DIM
        return projected[cells, first : first + HEAD_DIM]

    queries = [part(head, 0) * jnp.asarray(scale, BF16) for head in heads]
    keys = [part(head, 1) for head in heads]
    values = [part(head, 2) for head in heads]
    grads = [d_attended[cells, HEAD_DIM * head : HEAD_DIM * (head + 1)] for head in heads]
    scores = [dot_rows(keys[head], queries[head]) + bias[head] for head in heads]
    grad_probs = [dot_rows(values[head], grads[head]) for head in heads]
    halves, grad_scores = [], []
    for head in heads:
        raised = jnp.exp(scores[head] - jnp.max(scores[head], axis=0, keepdims=True))
        prob = raised * (1.0 / jnp.sum(raised, axis=0, keepdims=True))
        row_term = jnp.sum(prob * grad_probs[head], axis=0, keepdims=True)
        halves.append(prob.astype(BF16))
        grad_scores.append((prob * (grad_probs[head] - row_term)).astype(BF16))
    for head in heads:
        attended = dot_columns(halves[head], values[head])
        grad_value = dot(halves[head], grads[head])
        grad_query = dot_columns(grad_scores[head], keys[head]) * scale
        grad_key = dot(grad_scores[head], queries[head])
        merged[cells, HEAD_DIM * head : HEAD_DIM * (head + 1)] = attended.astype(BF16)
        first = group + 3 * HEAD_DIM * head
        merged[cells, first : first + 3 * HEAD_DIM] = jnp.concatenate(
            [grad_query, grad_key, grad_value], axis=1
        ).astype(BF16)


def lat_copies(whole, columns, out, lon_count, parity, sems, first):
    rows = whole.shape[0] // (4 * lon_count)
    copies = []
    for block in range(2 * lon_count):
        start = pl.multiple_of((2 * block + parity) * rows, rows)
        source, target = whole.at[pl.ds(start, rows), columns], out.at[pl.ds(block * rows, rows)]
        copies.append(pltpu.make_async_copy(source, target, sems.at[first + block]))
    return copies


def layer_kernel(
    tokens,
    cotangent,
    z_here,
    xd_here,
    z_there,
    xd_there,
    gain,
    w_out,
    bias,
    shift_pick,
    quarter,
    w_far,
    *refs,
):
    *by_lon, lat_keep, lat_send, stay, over, swap, part_tokens, part_cotangent = refs[:-13]
    source, near_tokens, near_grad, normed, projected, d_attended, merged = refs[-13:-6]
    ordered, terms, whole, w_qkv, load_sems, store_sems = refs[-6:]
    pieces = load_sems.shape[0]
    loads = []
    for piece in range(pieces):
        count = w_qkv.shape[0] // pieces
        part = pl.ds(piece * count, count)
        loads.append(
            pltpu.make_async_copy(w_far.at[part], w_qkv.at[part], load_sems.at[piece])
        )
        loads[-1].start()
    head_index = lax.axis_index("head")
    core = lax.rem(head_index, 2)
    heads = bias.shape[0]
    group = heads * HEAD_DIM
    split = CELLS + RIM_Z
    source[CELLS:split, :] = jnp.where(core == 0, z_here[...], z_there[...])
    source[split:, :] = jnp.where(core == 0, xd_here[...], xd_there[...])
    source[:CELLS, :] = tokens[...]
    near_tokens[...] = dot(shift_pick[...], source[...]).astype(BF16)
    source[CELLS:split, :] = jnp.where(core == 0, z_there[...], z_here[...])
    source[split:, :] = jnp.where(core == 0, xd_there[...], xd_here[...])
    source[:CELLS, :] = cotangent[...]
    near_grad[...] = dot(shift_pick[...], source[...]).astype(BF16)
    scaled, _ = scaled_rows(near_tokens[...])
    normed[...] = (scaled * gain[...]).astype(BF16)
    d_attended[...] = dot_rows(near_grad[...], w_out[...]).astype(BF16)
    for load in loads:
        load.wait()
    projected[...] = dot(normed[...], w_qkv[...]).astype(BF16)
    for window in range(WINDOWS):
        attend(window, projected, d_attended, bias, merged, group)
    whole[:, : 3 * group] = dot_columns(normed[...], merged[:, group:]).astype(BF16)
    whole[:, 3 * group :] = dot_columns(near_grad[...], merged[:, :group]).astype(BF16)
    lon, lon_count = lax.axis_index("lon"), len(by_lon)
    rows = by_lon[0].shape[0]
    stores = []
    for step, block in enumerate(by_lon):
        start = pl.multiple_of(lax.rem(lon + step, lon_count) * rows, rows)
        source_rows = whole.at[pl.ds(start, rows), pl.ds(0, 2 * group)]
        stores.append(pltpu.make_async_copy(source_rows, block, store_sems.at[step]))
    parity = lax.rem(lax.axis_index("lat"), 2)
    later = pl.ds(2 * group, 2 * group)
    stores += lat_copies(whole, later, lat_keep, lon_count, parity, store_sems, lon_count)
    stores += lat_copies(whole, later, lat_send, lon_count, 1 - parity, store_sems, 3 * lon_count)
    for store in stores:
        store.start()
    ordered[...] = dot(quarter[...], merged[...]).astype(BF16)
    terms[0] = dot(ordered[:, :group], w_out[...]).astype(BF16)
    terms[1] = dot_rows(ordered[:, group:], w_qkv[...]).astype(BF16)

    def term(owner):
        return terms[:, pl.ds(pl.multiple_of(owner * STRIDE, 16), PART), :]

    far = lax.rem(head_index + 2, QUARTERS)
    stay[...] = term(head_index)
    over[...] = term(far)
    swap[0] = term(head_index + 1 - 2 * core)
    swap[1] = term(far + 1 - 2 * core)
    mine = quarter[pl.ds(pl.multiple_of(head_index * STRIDE, 16), PART), :]
    part_tokens[...] = dot(mine, near_tokens[...]).astype(BF16)
    part_cotangent[...] = dot(mine, near_grad[...]).astype(BF16)
    for store in stores:
        store.wait()


def cores_kernel(over, swapped, total):
    total[...] = (over[...].astype(F32) + swapped[1].astype(F32)).astype(BF16)


def total_of(parts):
    total = parts[0].astype(F32)
    for part in parts[1:]:
        total = total + part.astype(F32)
    return total


def second_step_kernel(lon_count, *refs):
    from_lon, (lat_keep, from_lat) = refs[:lon_count], refs[lon_count : lon_count + 2]
    keep_first, send_first, *by_lon, mark = refs[lon_count + 2 :]
    mark[...] = jnp.zeros_like(mark)
    rows = keep_first.shape[0] // 2
    lon, parity = lax.axis_index("lon"), lax.rem(lax.axis_index("lat"), 2)
    for out, wanted in ((keep_first, parity), (send_first, 1 - parity)):
        for block in range(2):
            part = pl.ds(pl.multiple_of((2 * block + wanted) * rows, rows), rows)
            total = total_of([piece[part, :] for piece in from_lon])
            out[block * rows : (block + 1) * rows, :] = total.astype(out.dtype)
    for step, out in enumerate(by_lon):
        start = lax.rem(lon + step, lon_count) * 2 * rows
        part = pl.ds(pl.multiple_of(start, rows), 2 * rows)
        out[...] = total_of([lat_keep[part, :], from_lat[part, :]]).astype(out.dtype)


def third_step_kernel(keep_first, from_lat, *refs):
    from_lon, (keep, send, mark) = refs[:-3], refs[-3:]
    mark[...] = jnp.zeros_like(mark)
    rows = keep.shape[1]
    mine = lax.div(lax.axis_index("lat"), 2)
    for half, parts in enumerate(((keep_first, from_lat), from_lon)):
        for out, block in ((keep, mine), (send, 1 - mine)):
            part = pl.ds(pl.multiple_of(block * rows, rows), rows)
            out[half] = total_of([piece[part, :] for piece in parts]).astype(out.dtype)


def finish_kernel(group, flip, keep, arrived, grad_qkv, grad_out):
    grad_qkv[:, : 2 * group] = keep[0] + arrived[0].astype(F32)
    total = keep[1] + arrived[1].astype(F32)
    grad_qkv[:, 2 * group :] = total[:, :group]
    out = total[:, group:]
    grad_out[...] = out.T if flip else out


def norm_kernel(part_tokens, part_cotangent, gain, pick, stay, swapped, crossed, *refs):
    *outs, mark = refs
    mark[...] = jnp.zeros_like(mark)
    layer = part_tokens[...].astype(F32)
    attn = stay[0].astype(F32) + swapped[0, 0].astype(F32) + crossed[0].astype(F32)
    d_normed = stay[1].astype(F32) + swapped[0, 1].astype(F32) + crossed[1].astype(F32)
    scaled, inverse = scaled_rows(part_tokens[...])
    grad = d_normed * gain[...]
    mean_grad = jnp.mean(grad, axis=-1, keepdims=True)
    mean_mixed = jnp.mean(grad * scaled, axis=-1, keepdims=True)
    change = (grad - mean_grad - scaled * mean_mixed) * inverse
    for at, value in enumerate((layer + attn, part_cotangent[...].astype(F32) + change)):
        rows = dot(pick[...], value.astype(BF16)).astype(BF16)
        for start, out in zip(OUT_STARTS, outs):
            out[at] = rows[start : start + out.shape[1]]


def taken(count, source, spans):
    row = lax.broadcasted_iota(jnp.int32, (count, source.shape[0]), 0)
    column = lax.broadcasted_iota(jnp.int32, (count, source.shape[0]), 1)
    wanted = jnp.zeros((count, source.shape[0]), F32)
    for start, first, rows in spans:
        inside = (row >= start) & (row < start + rows)
        wanted = jnp.where(inside & (column == row + (first - start)), 1.0, wanted)
    return dot(wanted.astype(BF16), source)


def north_kernel(z_rows, x_rows, rows, mark):
    mark[...] = jnp.zeros_like(mark)
    _, north, east, corner = group_sizes()
    for at in range(2):
        total = taken(NORTH_ROWS, z_rows[at], [(0, 0, north)])
        total = total + taken(NORTH_ROWS, x_rows[at], [(north, east, corner)])
        rows[at] = total.astype(BF16)


def join_kernel(own, z_rows, x_rows, *pieces):
    stay, north, east, corner = group_sizes()
    for at in range(2):
        total = taken(PART, own[at], [(0, 0, stay)])
        spans = [(stay, 0, north), (stay + north + east, north, corner)]
        total = total + taken(PART, z_rows[at], spans)
        total = total + taken(PART, x_rows[at], [(stay + north, 0, east)])
        for number, piece in enumerate(pieces):
            rows = piece.shape[1]
            piece[at] = total[number * rows : (number + 1) * rows].astype(BF16)


def spread_kernel(pick, *refs):
    *arrived, layer, grad, mark, gathered = refs
    mark[...] = jnp.zeros_like(mark)
    head_index = lax.axis_index("head")
    sibling = 1 - 2 * lax.rem(head_index, 2)
    over = lax.rem(head_index + 2, QUARTERS)
    owners = (head_index, head_index + sibling, over, over + sibling)
    for at, out in enumerate((layer, grad)):
        for step, owner in enumerate(owners):
            for number in range(PIECES):
                start = pl.multiple_of((owner * PIECES + number) * SLOT, SLOT)
                gathered[at, pl.ds(start + SLOT - 16, 16), :] = jnp.zeros_like(gathered[at, :16, :])
                piece = arrived[step * PIECES + number][at]
                gathered[at, pl.ds(start, PART // PIECES), :] = piece
        out[...] = dot(pick[...], gathered[at]).astype(BF16)


def shaped(*shape, dtype=BF16):
    return jax.ShapeDtypeStruct(shape, dtype)


def rotated(value, axis, step):
    count = lax.axis_size(axis)
    return lax.ppermute(value, axis, [(i, (i + step) % count) for i in range(count)])


def moved(value, lat_step, lon_step):
    lon_count, lat_count = lax.axis_size("lon"), lax.axis_size("lat")
    pairs = []
    for lon in range(lon_count):
        for lat in range(lat_count):
            target = (lon + lon_step) % lon_count * lat_count + (lat + lat_step) % lat_count
            pairs.append((lon * lat_count + lat, target))
    return lax.ppermute(value, ("lon", "lat"), pairs)


def body(tokens, norm_gain, w_qkv, w_out, bias_table, cotangent):
    level_count, lat_cells, lon_cells, width = tokens.shape
    heads = bias_table.shape[1]
    group = w_out.shape[0]
    lon_count, lat_count = lax.axis_size("lon"), lax.axis_size("lat")
    flat_tokens = tokens.reshape(CELLS, width)
    flat_grad = cotangent.reshape(CELLS, width)
    gain = norm_gain.reshape(1, width)
    mark = shaped(8, 128, dtype=F32)
    rims = call(
        pack_kernel,
        [shaped(RIM_Z, width), shaped(RIM_X, width), shaped(RIM_D, width)],
        [pltpu.VMEM((CELLS, width), BF16), pltpu.SemaphoreType.DMA((6,))],
        cost=cost(2 * RIM * CELLS * width, 4 * CELLS * width),
        name="pack_rims",
        far=tuple(
            pltpu.with_memory_space_constraint(array, pltpu.HBM)
            for array in (flat_tokens, flat_grad)
        ),
    )()
    arrived = [moved(rims[0], -1, 0), moved(rims[1], 0, -1), moved(rims[2], -1, -1)]
    bias, bias_mark = call(
        bias_kernel,
        [shaped(heads, WINDOW, WINDOW, dtype=F32), mark],
        [
            pltpu.VMEM((8, 1024), F32),
            pltpu.VMEM((heads * 48, 768), BF16),
            pltpu.VMEM((heads, 576, WINDOW), BF16),
        ],
        cost=cost(2 * 192 * 768 * 144 * 12 * 2, 1000000),
        name="window_bias",
    )(bias_table.T)
    held = call(
        hold_kernel, shaped(RIM_Z, width), name="hold_rim", cost=cost(0, 4 * RIM_Z * width), after=(bias_mark,)
    )(arrived[0])
    joined = call(
        rims_kernel,
        shaped(RIM_X + RIM_D, width),
        name="join_rims",
        cost=cost(0, 4 * (RIM_X + RIM_D) * width),
        after=(bias_mark,),
    )(*arrived[1:])
    rims = [held, joined]
    pairs = [(i, i ^ 1) for i in range(QUARTERS)]
    rims += [lax.ppermute(rim, "head", pairs) for rim in rims]
    lon_rows = width // lon_count
    rows = lon_rows // lat_count
    columns = 2 * group
    *by_lon, lat_keep, lat_send, stay, over, swap, part_tokens, part_cotangent = call(
        layer_kernel,
        [shaped(lon_rows, columns)] * lon_count
        + [shaped(2 * lon_count * rows, columns)] * 2
        + [shaped(2, PART, width)] * 2
        + [shaped(2, 2, PART, width)]
        + [shaped(PART, width)] * 2,
        [
            pltpu.VMEM((CELLS + RIM, width), BF16),
            pltpu.VMEM((CELLS, width), BF16),
            pltpu.VMEM((CELLS, width), BF16),
            pltpu.VMEM((CELLS, width), BF16),
            pltpu.VMEM((CELLS, 3 * group), BF16),
            pltpu.VMEM((CELLS, group), BF16),
            pltpu.VMEM((CELLS, 4 * group), BF16),
            pltpu.VMEM((QUARTERS * STRIDE, 4 * group), BF16),
            pltpu.VMEM((2, QUARTERS * STRIDE, width), BF16),
            pltpu.VMEM((width, 4 * group), BF16),
            pltpu.VMEM((width, 3 * group), BF16),
            pltpu.SemaphoreType.DMA((4,)),
            pltpu.SemaphoreType.DMA((5 * lon_count,)),
        ],
        cost=cost(6 * CELLS * width * width, 8000000),
        name="window_layer",
        far=(w_qkv,),
        far_outs=lon_count + 2,
        limit=32,
    )(
        flat_tokens,
        flat_grad,
        *rims,
        gain,
        w_out,
        bias,
        one_hot(shifted_source(), CELLS + RIM),
        quarter_pick(),
    )
    from_lon = [by_lon[0]] + [rotated(by_lon[step], "lon", step) for step in range(1, lon_count)]
    neighbours = [(i, i ^ 1) for i in range(lat_count)]
    from_lat = lax.ppermute(lat_send, "lat", neighbours)
    swapped = lax.ppermute(swap, "head", pairs)
    across = call(
        cores_kernel, shaped(2, PART, width), cost=cost(0, 8 * PART * width), name="sum_over_cores"
    )(over, swapped)
    chips = [(i, i ^ 2) for i in range(QUARTERS)]
    crossed = lax.ppermute(across, "head", chips)
    *pieces, norm_mark = call(
        norm_kernel,
        [shaped(2, count, width) for count in OUT_SIZES] + [mark],
        cost=cost(2 * 2 * OUT_ROWS * PART * width, 12 * PART * width),
        name="sum_over_heads",
    )(part_tokens, part_cotangent, gain, group_pick(), stay, swapped, crossed)
    keep_first, send_first, *by_lon, second_mark = call(
        functools.partial(second_step_kernel, lon_count),
        [shaped(2 * rows, columns, dtype=F32), shaped(2 * rows, columns)]
        + [shaped(2 * rows, columns, dtype=F32)]
        + [shaped(2 * rows, columns)] * (lon_count - 1)
        + [mark],
        cost=cost(4 * lon_rows * columns, 6 * lon_rows * columns),
        name="second_step",
        after=(norm_mark,),
    )(*from_lon, lat_keep, from_lat)
    from_lat = lax.ppermute(send_first, "lat", neighbours)
    from_lon = [by_lon[0]] + [rotated(by_lon[step], "lon", step) for step in range(1, lon_count)]
    from_west = rotated(pieces[2], "lon", 1)
    to_north, north_mark = call(
        north_kernel,
        [shaped(2, NORTH_ROWS, width), mark],
        cost=cost(0, 8 * NORTH_ROWS * width),
        name="rows_for_north",
        after=(second_mark,),
    )(pieces[1], from_west)
    home = [pieces[0], rotated(to_north, "lat", 1), from_west]
    keep, send, third_mark = call(
        third_step_kernel,
        [shaped(2, rows, columns, dtype=F32), shaped(2, rows, columns), mark],
        cost=cost(4 * rows * columns, 6 * rows * columns),
        name="third_step",
        after=(north_mark,),
    )(keep_first, from_lat, *from_lon)
    last = lax.ppermute(send, "lat", [(i, i ^ 2) for i in range(lat_count)])
    each = call(
        join_kernel,
        [shaped(2, PART // PIECES, width)] * PIECES,
        cost=cost(2 * 2 * OUT_ROWS * PART * width, 8 * OUT_ROWS * width),
        name="join_home",
        after=(third_mark,),
    )(*home)
    far = [lax.ppermute(single, "head", chips) for single in each]
    near = [lax.ppermute(single, "head", pairs) for single in each]
    across = [lax.ppermute(single, "head", pairs) for single in far]
    layer_out, grad_tokens, spread_mark = call(
        spread_kernel,
        [shaped(CELLS, width)] * 2 + [mark],
        [pltpu.VMEM((2, QUARTERS * PIECES * SLOT, width), BF16)],
        cost=cost(2 * 2 * CELLS * CELLS * width, 8 * CELLS * width),
        name="spread_outputs",
    )(own_pick(), *each, *near, *far, *across)
    flip = rows % 128 == 0
    grad_qkv, grad_out = call(
        functools.partial(finish_kernel, group, flip),
        [
            shaped(rows, 3 * group, dtype=F32),
            shaped(*((group, rows) if flip else (rows, group)), dtype=F32),
        ],
        cost=cost(4 * rows * 4 * group, 16 * rows * 4 * group),
        name="sum_over_lat",
        after=(spread_mark,),
    )(keep, last)
    return (
        layer_out.reshape(tokens.shape),
        grad_tokens.reshape(tokens.shape),
        grad_qkv,
        grad_out if flip else grad_out.T,
    )


def solution(mesh):
    in_specs = (
        P(None, "lat", "lon", None),
        P(),
        P(None, "head"),
        P("head", None),
        P(None, "head"),
        P(None, "lat", "lon", None),
    )
    out_specs = (
        P(None, "lat", "lon", None),
        P(None, "lat", "lon", None),
        P(("lon", "lat"), "head"),
        P("head", ("lon", "lat")),
    )
    return jax.shard_map(body, mesh=mesh, in_specs=in_specs, out_specs=out_specs, check_vma=False)
```

```python
import functools

import jax
import jax.numpy as jnp
import numpy as np
from jax import lax
from jax.experimental import pallas as pl
from jax.experimental.pallas import tpu as pltpu
from jax.sharding import PartitionSpec as P

HEAD_DIM = 64
LEV = 2
WLAT = 6
WLON = 12
TILE_LON = 24
WINDOW = LEV * WLAT * WLON
WINDOWS = TILE_LON // WLON
CELLS = WINDOWS * WINDOW
QUARTERS = 4
PART = 72
STRIDE = 80
MID_LAT = WLAT // 2
MID_LON = WLON // 2
SPAN_LAT = 2 * WLAT - 1
SPAN_LON = 2 * WLON - 1
EPSILON = 1e-05
NEG_FILL = -1e30
F32 = jnp.float32
BF16 = jnp.bfloat16

RIM_Z, RIM_X, RIM_D = 112, 48, 48
RIM = RIM_Z + RIM_X + RIM_D
OUT_STARTS = (0, 32, 64)
OUT_SIZES = (32, 32, 32)
OUT_ROWS = 112
PIECES = 3
SLOT = 32
NORTH_ROWS = 40


def own_row(level, lat, lon):
    return (level * WLAT + lat) * TILE_LON + lon


def window_cells():
    cells = []
    for window in range(WINDOWS):
        for quarter in range(QUARTERS):
            for lat in range(WLAT):
                for half in range(2):
                    for third in range(3):
                        lon = half * MID_LON + (quarter % 2) * 3 + third
                        cells.append((window, quarter // 2, lat, lon))
    return cells


CELL_LIST = window_cells()
CELL_AT = {cell: at for at, cell in enumerate(CELL_LIST)}


def shifted_source():
    z_width = TILE_LON - MID_LON
    rows = []
    for window, level, lat, lon in CELL_LIST:
        column = window * WLON + lon + MID_LON
        if lat < MID_LAT and column < TILE_LON:
            rows.append(own_row(level, lat + MID_LAT, column))
        elif column < TILE_LON:
            rows.append(CELLS + (level * MID_LAT + lat - MID_LAT) * z_width + column - MID_LON)
        else:
            base = CELLS + RIM_Z + (RIM_X if lat >= MID_LAT else 0)
            rows.append(base + (level * MID_LAT + lat % MID_LAT) * MID_LON + column - TILE_LON)
    return np.array(rows)


def quarter_cells(quarter):
    groups = [[], [], [], []]
    for cell in CELL_LIST:
        window, level, lat, lon = cell
        if level != quarter // 2 or lon % MID_LON // 3 != quarter % 2:
            continue
        beyond = window * WLON + lon + MID_LON >= TILE_LON
        groups[2 * beyond + (lat >= MID_LAT)].append(cell)
    return groups


def one_hot(rows, count):
    picked = np.zeros((len(rows), count), np.float32)
    for at, row in enumerate(rows):
        if row >= 0:
            picked[at, row] = 1.0
    return picked.astype(BF16)


def quarter_pick():
    rows = []
    for quarter in range(QUARTERS):
        cells = sum(quarter_cells(quarter), [])
        rows += [CELL_AT[cell] for cell in cells] + [-1] * (STRIDE - len(cells))
    return one_hot(rows, CELLS)


def group_sizes():
    return [len(group) for group in quarter_cells(0)]


def group_pick():
    stay, north, east, corner = group_sizes()
    rows = list(range(stay)) + [-1] * (OUT_STARTS[1] - stay)
    rows += list(range(stay, stay + north)) + [-1] * (OUT_STARTS[2] - OUT_STARTS[1] - north)
    rows += list(range(stay + north, PART)) + [-1] * (OUT_ROWS - OUT_STARTS[2] - east - corner)
    return one_hot(rows, PART)


def own_pick():
    place = {}
    for quarter in range(QUARTERS):
        for at, (window, level, lat, lon) in enumerate(sum(quarter_cells(quarter), [])):
            column = (window * WLON + lon + MID_LON) % TILE_LON
            row = own_row(level, (lat + MID_LAT) % WLAT, column)
            place[row] = (quarter * PIECES + at // (PART // PIECES)) * SLOT + at % (PART // PIECES)
    return one_hot([place[row] for row in range(CELLS)], QUARTERS * PIECES * SLOT)


def window_position(shape, dim):
    def count(value, size, parts):
        return sum((value >= size * step).astype(jnp.int32) for step in range(1, parts))

    cell = lax.broadcasted_iota(jnp.int32, shape, dim)
    quarter = count(cell, WINDOW // QUARTERS, QUARTERS)
    cell = cell - quarter * (WINDOW // QUARTERS)
    lat = count(cell, 6, WLAT)
    cell = cell - lat * 6
    half = count(cell, 3, 2)
    level = count(quarter, 2, 2)
    lon = half * MID_LON + (quarter - 2 * level) * 3 + cell - half * 3
    return level, lat, lon


def dot(left, right):
    return lax.dot_general(left, right, (((1,), (0,)), ((), ())), preferred_element_type=F32)


def dot_rows(left, right):
    return lax.dot_general(left, right, (((1,), (1,)), ((), ())), preferred_element_type=F32)


def dot_columns(left, right):
    return lax.dot_general(left, right, (((0,), (0,)), ((), ())), preferred_element_type=F32)


def call(kernel, outs, scratch=(), cost=None, name=None, after=(), far=(), far_outs=0, limit=16):
    def run(*args):
        def body(*refs):
            count = len(args) + len(far)
            kernel(*refs[:count], *refs[count + len(after) :])

        near, outside = pl.BlockSpec(memory_space=pltpu.VMEM), pl.BlockSpec(memory_space=pl.ANY)
        specs = near
        if isinstance(outs, list):
            specs = [outside] * far_outs + [near] * (len(outs) - far_outs)
        return pl.pallas_call(
            body,
            out_shape=outs,
            in_specs=[near] * len(args) + [outside] * (len(far) + len(after)),
            out_specs=specs,
            scratch_shapes=scratch,
            name=name,
            cost_estimate=cost,
            compiler_params=pltpu.CompilerParams(vmem_limit_bytes=limit * 1024 * 1024),
        )(*args, *far, *after)

    return run


def cost(flops, moved):
    return pl.CostEstimate(flops=flops, bytes_accessed=moved, transcendentals=0)


def rim_rows(shape):
    row = lax.broadcasted_iota(jnp.int32, shape, 1)
    level = (row >= WLAT * TILE_LON).astype(jnp.int32)
    row = row - level * WLAT * TILE_LON
    lat = sum((row >= TILE_LON * count).astype(jnp.int32) for count in range(1, WLAT))
    lon = row - lat * TILE_LON
    line = level * MID_LAT + lat
    z_row = line * (TILE_LON - MID_LON) + lon - MID_LON
    d_row = RIM_Z + RIM_X + line * MID_LON + lon
    x_row = RIM_Z + (line - MID_LAT) * MID_LON + lon
    west = lon < MID_LON
    return jnp.where(
        lat < MID_LAT, jnp.where(west, d_row, z_row), jnp.where(west, x_row, -1)
    )


def pack_kernel(tokens, cotangent, rim_z, rim_x, rim_d, source, sems):
    core = lax.rem(lax.axis_index("head"), 2)
    pieces = sems.shape[0]
    rows = CELLS // pieces

    def load(array):
        copies = []
        for piece in range(pieces):
            part = pl.ds(piece * rows, rows)
            copies.append(pltpu.make_async_copy(array.at[part], source.at[part], sems.at[piece]))
        for copy in copies:
            copy.start()
        for copy in copies:
            copy.wait()

    pl.when(core == 0)(lambda: load(tokens))
    pl.when(core != 0)(lambda: load(cotangent))
    wanted = lax.broadcasted_iota(jnp.int32, (RIM, CELLS), 0) == rim_rows((RIM, CELLS))
    rim = dot(wanted.astype(F32).astype(BF16), source[...]).astype(BF16)
    rim_z[...] = rim[:RIM_Z]
    rim_x[...] = rim[RIM_Z : RIM_Z + RIM_X]
    rim_d[...] = rim[RIM_Z + RIM_X :]


def hold_kernel(rim, held):
    held[...] = rim[...]


def rims_kernel(x_rim, d_rim, rim):
    rim[:RIM_X] = x_rim[...]
    rim[RIM_X:] = d_rim[...]


def bias_kernel(table, bias, mark, padded, shifted, parts):
    mark[...] = jnp.zeros_like(mark)
    heads = bias.shape[0]
    width = shifted.shape[1]
    padded[...] = jnp.zeros_like(padded)
    padded[:heads, : table.shape[1]] = table[...]
    for head in range(heads):
        spread = jnp.broadcast_to(padded[head : head + 1, :], (16, padded.shape[1]))
        rolled = pltpu.roll(spread, 0, 1, stride=1, stride_axis=0)[:, :width]
        high = rolled.astype(BF16)
        rest = rolled - high.astype(F32)
        middle = rest.astype(BF16)
        low = (rest - middle.astype(F32)).astype(BF16)
        for split, value in enumerate((high, middle, low)):
            shifted[(head * 3 + split) * 16 : (head * 3 + split + 1) * 16, :] = value
    place = lax.broadcasted_iota(jnp.int32, (width, WINDOW), 0)
    count = LEV * WLAT * 16
    level_of, lat_of, lon_of = window_position((1, WINDOW), 1)
    plane = SPAN_LAT * SPAN_LON
    column = plane * (level_of + LEV - 1) + SPAN_LON * (lat_of + WLAT - 1) + lon_of + WLON - 1
    for level in range(LEV):
        for lat in range(WLAT):
            wanted = (place == column - (plane * level + SPAN_LON * lat)).astype(F32).astype(BF16)
            block = dot(shifted[...], wanted).astype(BF16)
            start = (level * WLAT + lat) * 16
            for head in range(heads):
                for split in range(3):
                    first = (head * 3 + split) * 16
                    parts[head, split * count + start : split * count + start + 16, :] = block[
                        first : first + 16
                    ]
    level_in, lat_in, lon_in = window_position((WINDOW, 1), 0)
    lane = lax.broadcasted_iota(jnp.int32, (WINDOW, 3 * count), 1)
    lane = lane - count * ((lane >= count).astype(jnp.int32) + (lane >= 2 * count).astype(jnp.int32))
    rows = (lane == (level_in * WLAT + lat_in) * 16 + lon_in).astype(F32).astype(BF16)
    last = lax.axis_index("lat") == lax.axis_size("lat") - 1
    south_in = (lat_in < MID_LAT).astype(jnp.int32)
    south_of = (lat_of < MID_LAT).astype(jnp.int32)
    added = jnp.where((south_in != south_of) & last, NEG_FILL, 0.0)
    for head in range(heads):
        bias[head] = dot(rows, parts[head]) + added


def scaled_rows(values):
    floats = values.astype(F32)
    center = floats - jnp.mean(floats, axis=-1, keepdims=True)
    inverse = lax.rsqrt(jnp.mean(center * center, axis=-1, keepdims=True) + EPSILON)
    return center * inverse, inverse


def attend(window, projected, d_attended, bias, merged, group):
    cells = slice(window * WINDOW, (window + 1) * WINDOW)
    scale = HEAD_DIM**-0.5
    heads = range(bias.shape[0])

    def part(head, kind):
        first = (3 * head + kind) * HEAD_DIM
        return projected[cells, first : first + HEAD_DIM]

    queries = [part(head, 0) * jnp.asarray(scale, BF16) for head in heads]
    keys = [part(head, 1) for head in heads]
    values = [part(head, 2) for head in heads]
    grads = [d_attended[cells, HEAD_DIM * head : HEAD_DIM * (head + 1)] for head in heads]
    scores = [dot_rows(keys[head], queries[head]) + bias[head] for head in heads]
    grad_probs = [dot_rows(values[head], grads[head]) for head in heads]
    halves, grad_scores = [], []
    for head in heads:
        raised = jnp.exp(scores[head] - jnp.max(scores[head], axis=0, keepdims=True))
        prob = raised * (1.0 / jnp.sum(raised, axis=0, keepdims=True))
        row_term = jnp.sum(prob * grad_probs[head], axis=0, keepdims=True)
        halves.append(prob.astype(BF16))
        grad_scores.append((prob * (grad_probs[head] - row_term)).astype(BF16))
    for head in heads:
        attended = dot_columns(halves[head], values[head])
        grad_value = dot(halves[head], grads[head])
        grad_query = dot_columns(grad_scores[head], keys[head]) * scale
        grad_key = dot(grad_scores[head], queries[head])
        merged[cells, HEAD_DIM * head : HEAD_DIM * (head + 1)] = attended.astype(BF16)
        first = group + 3 * HEAD_DIM * head
        merged[cells, first : first + 3 * HEAD_DIM] = jnp.concatenate(
            [grad_query, grad_key, grad_value], axis=1
        ).astype(BF16)


def lat_copies(whole, columns, out, lon_count, parity, sems, first):
    rows = whole.shape[0] // (4 * lon_count)
    copies = []
    for block in range(2 * lon_count):
        start = pl.multiple_of((2 * block + parity) * rows, rows)
        source, target = whole.at[pl.ds(start, rows), columns], out.at[pl.ds(block * rows, rows)]
        copies.append(pltpu.make_async_copy(source, target, sems.at[first + block]))
    return copies


def layer_kernel(
    tokens,
    cotangent,
    z_here,
    xd_here,
    z_there,
    xd_there,
    gain,
    w_out,
    bias,
    shift_pick,
    quarter,
    w_far,
    *refs,
):
    *by_lon, lat_keep, lat_send, stay, over, swap, part_tokens, part_cotangent = refs[:-13]
    source, near_tokens, near_grad, normed, projected, d_attended, merged = refs[-13:-6]
    ordered, terms, whole, w_qkv, load_sems, store_sems = refs[-6:]
    pieces = load_sems.shape[0]
    loads = []
    for piece in range(pieces):
        count = w_qkv.shape[0] // pieces
        part = pl.ds(piece * count, count)
        loads.append(
            pltpu.make_async_copy(w_far.at[part], w_qkv.at[part], load_sems.at[piece])
        )
        loads[-1].start()
    head_index = lax.axis_index("head")
    core = lax.rem(head_index, 2)
    heads = bias.shape[0]
    group = heads * HEAD_DIM
    split = CELLS + RIM_Z
    source[CELLS:split, :] = jnp.where(core == 0, z_here[...], z_there[...])
    source[split:, :] = jnp.where(core == 0, xd_here[...], xd_there[...])
    source[:CELLS, :] = tokens[...]
    near_tokens[...] = dot(shift_pick[...], source[...]).astype(BF16)
    source[CELLS:split, :] = jnp.where(core == 0, z_there[...], z_here[...])
    source[split:, :] = jnp.where(core == 0, xd_there[...], xd_here[...])
    source[:CELLS, :] = cotangent[...]
    near_grad[...] = dot(shift_pick[...], source[...]).astype(BF16)
    scaled, _ = scaled_rows(near_tokens[...])
    normed[...] = (scaled * gain[...]).astype(BF16)
    d_attended[...] = dot_rows(near_grad[...], w_out[...]).astype(BF16)
    for load in loads:
        load.wait()
    projected[...] = dot(normed[...], w_qkv[...]).astype(BF16)
    for window in range(WINDOWS):
        attend(window, projected, d_attended, bias, merged, group)
    whole[:, : 3 * group] = dot_columns(normed[...], merged[:, group:]).astype(BF16)
    whole[:, 3 * group :] = dot_columns(near_grad[...], merged[:, :group]).astype(BF16)
    lon, lon_count = lax.axis_index("lon"), len(by_lon)
    rows = by_lon[0].shape[0]
    stores = []
    for step, block in enumerate(by_lon):
        start = pl.multiple_of(lax.rem(lon + step, lon_count) * rows, rows)
        source_rows = whole.at[pl.ds(start, rows), pl.ds(0, 2 * group)]
        stores.append(pltpu.make_async_copy(source_rows, block, store_sems.at[step]))
    parity = lax.rem(lax.axis_index("lat"), 2)
    later = pl.ds(2 * group, 2 * group)
    stores += lat_copies(whole, later, lat_keep, lon_count, parity, store_sems, lon_count)
    stores += lat_copies(whole, later, lat_send, lon_count, 1 - parity, store_sems, 3 * lon_count)
    for store in stores:
        store.start()
    ordered[...] = dot(quarter[...], merged[...]).astype(BF16)
    terms[0] = dot(ordered[:, :group], w_out[...]).astype(BF16)
    terms[1] = dot_rows(ordered[:, group:], w_qkv[...]).astype(BF16)

    def term(owner):
        return terms[:, pl.ds(pl.multiple_of(owner * STRIDE, 16), PART), :]

    far = lax.rem(head_index + 2, QUARTERS)
    stay[...] = term(head_index)
    over[...] = term(far)
    swap[0] = term(head_index + 1 - 2 * core)
    swap[1] = term(far + 1 - 2 * core)
    mine = quarter[pl.ds(pl.multiple_of(head_index * STRIDE, 16), PART), :]
    part_tokens[...] = dot(mine, near_tokens[...]).astype(BF16)
    part_cotangent[...] = dot(mine, near_grad[...]).astype(BF16)
    for store in stores:
        store.wait()


def cores_kernel(over, swapped, total):
    total[...] = (over[...].astype(F32) + swapped[1].astype(F32)).astype(BF16)


def total_of(parts):
    total = parts[0].astype(F32)
    for part in parts[1:]:
        total = total + part.astype(F32)
    return total


def second_step_kernel(lon_count, *refs):
    from_lon, (lat_keep, from_lat) = refs[:lon_count], refs[lon_count : lon_count + 2]
    keep_first, send_first, *by_lon, mark = refs[lon_count + 2 :]
    mark[...] = jnp.zeros_like(mark)
    rows = keep_first.shape[0] // 2
    lon, parity = lax.axis_index("lon"), lax.rem(lax.axis_index("lat"), 2)
    for out, wanted in ((keep_first, parity), (send_first, 1 - parity)):
        for block in range(2):
            part = pl.ds(pl.multiple_of((2 * block + wanted) * rows, rows), rows)
            total = total_of([piece[part, :] for piece in from_lon])
            out[block * rows : (block + 1) * rows, :] = total.astype(out.dtype)
    for step, out in enumerate(by_lon):
        start = lax.rem(lon + step, lon_count) * 2 * rows
        part = pl.ds(pl.multiple_of(start, rows), 2 * rows)
        out[...] = total_of([lat_keep[part, :], from_lat[part, :]]).astype(out.dtype)


def third_step_kernel(keep_first, from_lat, *refs):
    from_lon, (keep, send, mark) = refs[:-3], refs[-3:]
    mark[...] = jnp.zeros_like(mark)
    rows = keep.shape[1]
    mine = lax.div(lax.axis_index("lat"), 2)
    for half, parts in enumerate(((keep_first, from_lat), from_lon)):
        for out, block in ((keep, mine), (send, 1 - mine)):
            part = pl.ds(pl.multiple_of(block * rows, rows), rows)
            out[half] = total_of([piece[part, :] for piece in parts]).astype(out.dtype)


def finish_kernel(group, flip, keep, arrived, grad_qkv, grad_out):
    grad_qkv[:, : 2 * group] = keep[0] + arrived[0].astype(F32)
    total = keep[1] + arrived[1].astype(F32)
    grad_qkv[:, 2 * group :] = total[:, :group]
    out = total[:, group:]
    grad_out[...] = out.T if flip else out


def norm_kernel(part_tokens, part_cotangent, gain, pick, stay, swapped, crossed, *refs):
    *outs, mark = refs
    mark[...] = jnp.zeros_like(mark)
    layer = part_tokens[...].astype(F32)
    attn = stay[0].astype(F32) + swapped[0, 0].astype(F32) + crossed[0].astype(F32)
    d_normed = stay[1].astype(F32) + swapped[0, 1].astype(F32) + crossed[1].astype(F32)
    scaled, inverse = scaled_rows(part_tokens[...])
    grad = d_normed * gain[...]
    mean_grad = jnp.mean(grad, axis=-1, keepdims=True)
    mean_mixed = jnp.mean(grad * scaled, axis=-1, keepdims=True)
    change = (grad - mean_grad - scaled * mean_mixed) * inverse
    for at, value in enumerate((layer + attn, part_cotangent[...].astype(F32) + change)):
        rows = dot(pick[...], value.astype(BF16)).astype(BF16)
        for start, out in zip(OUT_STARTS, outs):
            out[at] = rows[start : start + out.shape[1]]


def taken(count, source, spans):
    row = lax.broadcasted_iota(jnp.int32, (count, source.shape[0]), 0)
    column = lax.broadcasted_iota(jnp.int32, (count, source.shape[0]), 1)
    wanted = jnp.zeros((count, source.shape[0]), F32)
    for start, first, rows in spans:
        inside = (row >= start) & (row < start + rows)
        wanted = jnp.where(inside & (column == row + (first - start)), 1.0, wanted)
    return dot(wanted.astype(BF16), source)


def north_kernel(z_rows, x_rows, rows, mark):
    mark[...] = jnp.zeros_like(mark)
    _, north, east, corner = group_sizes()
    for at in range(2):
        total = taken(NORTH_ROWS, z_rows[at], [(0, 0, north)])
        total = total + taken(NORTH_ROWS, x_rows[at], [(north, east, corner)])
        rows[at] = total.astype(BF16)


def join_kernel(own, z_rows, x_rows, *pieces):
    stay, north, east, corner = group_sizes()
    for at in range(2):
        total = taken(PART, own[at], [(0, 0, stay)])
        spans = [(stay, 0, north), (stay + north + east, north, corner)]
        total = total + taken(PART, z_rows[at], spans)
        total = total + taken(PART, x_rows[at], [(stay + north, 0, east)])
        for number, piece in enumerate(pieces):
            rows = piece.shape[1]
            piece[at] = total[number * rows : (number + 1) * rows].astype(BF16)


def spread_kernel(pick, *refs):
    *arrived, layer, grad, mark, gathered, staged, sems = refs
    copies = []
    mark[...] = jnp.zeros_like(mark)
    head_index = lax.axis_index("head")
    sibling = 1 - 2 * lax.rem(head_index, 2)
    over = lax.rem(head_index + 2, QUARTERS)
    owners = (head_index, head_index + sibling, over, over + sibling)
    for at, out in enumerate((layer, grad)):
        for step, owner in enumerate(owners):
            for number in range(PIECES):
                start = pl.multiple_of((owner * PIECES + number) * SLOT, SLOT)
                gathered[at, pl.ds(start + SLOT - 16, 16), :] = jnp.zeros_like(gathered[at, :16, :])
                piece = arrived[step * PIECES + number][at]
                gathered[at, pl.ds(start, PART // PIECES), :] = piece
        staged[at] = dot(pick[...], gathered[at]).astype(BF16)
        for number in range(PIECES):
            rows = CELLS // PIECES
            part = pl.ds(number * rows, rows)
            sem = sems.at[at * PIECES + number]
            copies.append(pltpu.make_async_copy(staged.at[at, part], out.at[part], sem))
            copies[-1].start()
    for copy in copies:
        copy.wait()


def shaped(*shape, dtype=BF16):
    return jax.ShapeDtypeStruct(shape, dtype)


def rotated(value, axis, step):
    count = lax.axis_size(axis)
    return lax.ppermute(value, axis, [(i, (i + step) % count) for i in range(count)])


def moved(value, lat_step, lon_step):
    lon_count, lat_count = lax.axis_size("lon"), lax.axis_size("lat")
    pairs = []
    for lon in range(lon_count):
        for lat in range(lat_count):
            target = (lon + lon_step) % lon_count * lat_count + (lat + lat_step) % lat_count
            pairs.append((lon * lat_count + lat, target))
    return lax.ppermute(value, ("lon", "lat"), pairs)


def body(tokens, norm_gain, w_qkv, w_out, bias_table, cotangent):
    level_count, lat_cells, lon_cells, width = tokens.shape
    heads = bias_table.shape[1]
    group = w_out.shape[0]
    lon_count, lat_count = lax.axis_size("lon"), lax.axis_size("lat")
    flat_tokens = tokens.reshape(CELLS, width)
    flat_grad = cotangent.reshape(CELLS, width)
    gain = norm_gain.reshape(1, width)
    mark = shaped(8, 128, dtype=F32)
    rims = call(
        pack_kernel,
        [shaped(RIM_Z, width), shaped(RIM_X, width), shaped(RIM_D, width)],
        [pltpu.VMEM((CELLS, width), BF16), pltpu.SemaphoreType.DMA((6,))],
        cost=cost(2 * RIM * CELLS * width, 4 * CELLS * width),
        name="pack_rims",
        far=tuple(
            pltpu.with_memory_space_constraint(array, pltpu.HBM)
            for array in (flat_tokens, flat_grad)
        ),
    )()
    arrived = [moved(rims[0], -1, 0), moved(rims[1], 0, -1), moved(rims[2], -1, -1)]
    bias, bias_mark = call(
        bias_kernel,
        [shaped(heads, WINDOW, WINDOW, dtype=F32), mark],
        [
            pltpu.VMEM((8, 1024), F32),
            pltpu.VMEM((heads * 48, 768), BF16),
            pltpu.VMEM((heads, 576, WINDOW), BF16),
        ],
        cost=cost(2 * 192 * 768 * 144 * 12 * 2, 1000000),
        name="window_bias",
    )(bias_table.T)
    held = call(
        hold_kernel, shaped(RIM_Z, width), name="hold_rim", cost=cost(0, 4 * RIM_Z * width), after=(bias_mark,)
    )(arrived[0])
    joined = call(
        rims_kernel,
        shaped(RIM_X + RIM_D, width),
        name="join_rims",
        cost=cost(0, 4 * (RIM_X + RIM_D) * width),
        after=(bias_mark,),
    )(*arrived[1:])
    rims = [held, joined]
    pairs = [(i, i ^ 1) for i in range(QUARTERS)]
    rims += [lax.ppermute(rim, "head", pairs) for rim in rims]
    lon_rows = width // lon_count
    rows = lon_rows // lat_count
    columns = 2 * group
    *by_lon, lat_keep, lat_send, stay, over, swap, part_tokens, part_cotangent = call(
        layer_kernel,
        [shaped(lon_rows, columns)] * lon_count
        + [shaped(2 * lon_count * rows, columns)] * 2
        + [shaped(2, PART, width)] * 2
        + [shaped(2, 2, PART, width)]
        + [shaped(PART, width)] * 2,
        [
            pltpu.VMEM((CELLS + RIM, width), BF16),
            pltpu.VMEM((CELLS, width), BF16),
            pltpu.VMEM((CELLS, width), BF16),
            pltpu.VMEM((CELLS, width), BF16),
            pltpu.VMEM((CELLS, 3 * group), BF16),
            pltpu.VMEM((CELLS, group), BF16),
            pltpu.VMEM((CELLS, 4 * group), BF16),
            pltpu.VMEM((QUARTERS * STRIDE, 4 * group), BF16),
            pltpu.VMEM((2, QUARTERS * STRIDE, width), BF16),
            pltpu.VMEM((width, 4 * group), BF16),
            pltpu.VMEM((width, 3 * group), BF16),
            pltpu.SemaphoreType.DMA((4,)),
            pltpu.SemaphoreType.DMA((5 * lon_count,)),
        ],
        cost=cost(6 * CELLS * width * width, 8000000),
        name="window_layer",
        far=(w_qkv,),
        far_outs=lon_count + 2,
        limit=32,
    )(
        flat_tokens,
        flat_grad,
        *rims,
        gain,
        w_out,
        bias,
        one_hot(shifted_source(), CELLS + RIM),
        quarter_pick(),
    )
    from_lon = [by_lon[0]] + [rotated(by_lon[step], "lon", step) for step in range(1, lon_count)]
    neighbours = [(i, i ^ 1) for i in range(lat_count)]
    from_lat = lax.ppermute(lat_send, "lat", neighbours)
    swapped = lax.ppermute(swap, "head", pairs)
    across = call(
        cores_kernel, shaped(2, PART, width), cost=cost(0, 8 * PART * width), name="sum_over_cores"
    )(over, swapped)
    chips = [(i, i ^ 2) for i in range(QUARTERS)]
    crossed = lax.ppermute(across, "head", chips)
    *pieces, norm_mark = call(
        norm_kernel,
        [shaped(2, count, width) for count in OUT_SIZES] + [mark],
        cost=cost(2 * 2 * OUT_ROWS * PART * width, 12 * PART * width),
        name="sum_over_heads",
    )(part_tokens, part_cotangent, gain, group_pick(), stay, swapped, crossed)
    keep_first, send_first, *by_lon, second_mark = call(
        functools.partial(second_step_kernel, lon_count),
        [shaped(2 * rows, columns, dtype=F32), shaped(2 * rows, columns)]
        + [shaped(2 * rows, columns, dtype=F32)]
        + [shaped(2 * rows, columns)] * (lon_count - 1)
        + [mark],
        cost=cost(4 * lon_rows * columns, 6 * lon_rows * columns),
        name="second_step",
        after=(norm_mark,),
    )(*from_lon, lat_keep, from_lat)
    from_lat = lax.ppermute(send_first, "lat", neighbours)
    from_lon = [by_lon[0]] + [rotated(by_lon[step], "lon", step) for step in range(1, lon_count)]
    from_west = rotated(pieces[2], "lon", 1)
    to_north, north_mark = call(
        north_kernel,
        [shaped(2, NORTH_ROWS, width), mark],
        cost=cost(0, 8 * NORTH_ROWS * width),
        name="rows_for_north",
        after=(second_mark,),
    )(pieces[1], from_west)
    home = [pieces[0], rotated(to_north, "lat", 1), from_west]
    keep, send, third_mark = call(
        third_step_kernel,
        [shaped(2, rows, columns, dtype=F32), shaped(2, rows, columns), mark],
        cost=cost(4 * rows * columns, 6 * rows * columns),
        name="third_step",
        after=(north_mark,),
    )(keep_first, from_lat, *from_lon)
    last = lax.ppermute(send, "lat", [(i, i ^ 2) for i in range(lat_count)])
    each = call(
        join_kernel,
        [shaped(2, PART // PIECES, width)] * PIECES,
        cost=cost(2 * 2 * OUT_ROWS * PART * width, 8 * OUT_ROWS * width),
        name="join_home",
        after=(third_mark,),
    )(*home)
    far = [lax.ppermute(single, "head", chips) for single in each]
    near = [lax.ppermute(single, "head", pairs) for single in each]
    across = [lax.ppermute(single, "head", pairs) for single in far]
    layer_out, grad_tokens, spread_mark = call(
        spread_kernel,
        [shaped(CELLS, width)] * 2 + [mark],
        [
            pltpu.VMEM((2, QUARTERS * PIECES * SLOT, width), BF16),
            pltpu.VMEM((2, CELLS, width), BF16),
            pltpu.SemaphoreType.DMA((2 * PIECES,)),
        ],
        cost=cost(2 * 2 * CELLS * CELLS * width, 8 * CELLS * width),
        name="spread_outputs",
        far_outs=2,
    )(own_pick(), *each, *near, *far, *across)
    flip = rows % 128 == 0
    grad_qkv, grad_out = call(
        functools.partial(finish_kernel, group, flip),
        [
            shaped(rows, 3 * group, dtype=F32),
            shaped(*((group, rows) if flip else (rows, group)), dtype=F32),
        ],
        cost=cost(4 * rows * 4 * group, 16 * rows * 4 * group),
        name="sum_over_lat",
        after=(spread_mark,),
    )(keep, last)
    return (
        layer_out.reshape(tokens.shape),
        grad_tokens.reshape(tokens.shape),
        grad_qkv,
        grad_out if flip else grad_out.T,
    )


def solution(mesh):
    in_specs = (
        P(None, "lat", "lon", None),
        P(),
        P(None, "head"),
        P("head", None),
        P(None, "head"),
        P(None, "lat", "lon", None),
    )
    out_specs = (
        P(None, "lat", "lon", None),
        P(None, "lat", "lon", None),
        P(("lon", "lat"), "head"),
        P("head", ("lon", "lat")),
    )
    return jax.shard_map(body, mesh=mesh, in_specs=in_specs, out_specs=out_specs, check_vma=False)
```

```python
import functools

import jax
import jax.numpy as jnp
import numpy as np
from jax import lax
from jax.experimental import pallas as pl
from jax.experimental.pallas import tpu as pltpu
from jax.sharding import PartitionSpec as P

HEAD_DIM = 64
LEV = 2
WLAT = 6
WLON = 12
TILE_LON = 24
WINDOW = LEV * WLAT * WLON
WINDOWS = TILE_LON // WLON
CELLS = WINDOWS * WINDOW
QUARTERS = 4
PART = 72
STRIDE = 80
MID_LAT = WLAT // 2
MID_LON = WLON // 2
SPAN_LAT = 2 * WLAT - 1
SPAN_LON = 2 * WLON - 1
EPSILON = 1e-05
NEG_FILL = -1e30
F32 = jnp.float32
BF16 = jnp.bfloat16

RIM_Z, RIM_X, RIM_D = 112, 48, 48
RIM = RIM_Z + RIM_X + RIM_D
RIM_SENT = 40
OUT_STARTS = (0, 32, 64)
OUT_SIZES = (32, 32, 32)
OUT_ROWS = 112
PIECES = 3
SLOT = 32
NORTH_ROWS = 40


def own_row(level, lat, lon):
    return (level * WLAT + lat) * TILE_LON + lon


def window_cells():
    cells = []
    for window in range(WINDOWS):
        for quarter in range(QUARTERS):
            for lat in range(WLAT):
                for half in range(2):
                    for third in range(3):
                        lon = half * MID_LON + (quarter % 2) * 3 + third
                        cells.append((window, quarter // 2, lat, lon))
    return cells


CELL_LIST = window_cells()
CELL_AT = {cell: at for at, cell in enumerate(CELL_LIST)}


def shifted_source():
    z_width = TILE_LON - MID_LON
    rows = []
    for window, level, lat, lon in CELL_LIST:
        column = window * WLON + lon + MID_LON
        if lat < MID_LAT and column < TILE_LON:
            rows.append(own_row(level, lat + MID_LAT, column))
        elif column < TILE_LON:
            rows.append(CELLS + (level * MID_LAT + lat - MID_LAT) * z_width + column - MID_LON)
        else:
            base = CELLS + RIM_Z + (RIM_X if lat >= MID_LAT else 0)
            rows.append(base + (level * MID_LAT + lat % MID_LAT) * MID_LON + column - TILE_LON)
    return np.array(rows)


def quarter_cells(quarter):
    groups = [[], [], [], []]
    for cell in CELL_LIST:
        window, level, lat, lon = cell
        if level != quarter // 2 or lon % MID_LON // 3 != quarter % 2:
            continue
        beyond = window * WLON + lon + MID_LON >= TILE_LON
        groups[2 * beyond + (lat >= MID_LAT)].append(cell)
    return groups


def one_hot(rows, count):
    picked = np.zeros((len(rows), count), np.float32)
    for at, row in enumerate(rows):
        if row >= 0:
            picked[at, row] = 1.0
    return picked.astype(BF16)


def quarter_pick():
    rows = []
    for quarter in range(QUARTERS):
        cells = sum(quarter_cells(quarter), [])
        rows += [CELL_AT[cell] for cell in cells] + [-1] * (STRIDE - len(cells))
    return one_hot(rows, CELLS)


def group_sizes():
    return [len(group) for group in quarter_cells(0)]


def group_pick():
    stay, north, east, corner = group_sizes()
    rows = list(range(stay)) + [-1] * (OUT_STARTS[1] - stay)
    rows += list(range(stay, stay + north)) + [-1] * (OUT_STARTS[2] - OUT_STARTS[1] - north)
    rows += list(range(stay + north, PART)) + [-1] * (OUT_ROWS - OUT_STARTS[2] - east - corner)
    return one_hot(rows, PART)


def own_pick():
    place = {}
    for quarter in range(QUARTERS):
        for at, (window, level, lat, lon) in enumerate(sum(quarter_cells(quarter), [])):
            column = (window * WLON + lon + MID_LON) % TILE_LON
            row = own_row(level, (lat + MID_LAT) % WLAT, column)
            place[row] = (quarter * PIECES + at // (PART // PIECES)) * SLOT + at % (PART // PIECES)
    return one_hot([place[row] for row in range(CELLS)], QUARTERS * PIECES * SLOT)


def window_position(shape, dim):
    def count(value, size, parts):
        return sum((value >= size * step).astype(jnp.int32) for step in range(1, parts))

    cell = lax.broadcasted_iota(jnp.int32, shape, dim)
    quarter = count(cell, WINDOW // QUARTERS, QUARTERS)
    cell = cell - quarter * (WINDOW // QUARTERS)
    lat = count(cell, 6, WLAT)
    cell = cell - lat * 6
    half = count(cell, 3, 2)
    level = count(quarter, 2, 2)
    lon = half * MID_LON + (quarter - 2 * level) * 3 + cell - half * 3
    return level, lat, lon


def dot(left, right):
    return lax.dot_general(left, right, (((1,), (0,)), ((), ())), preferred_element_type=F32)


def dot_rows(left, right):
    return lax.dot_general(left, right, (((1,), (1,)), ((), ())), preferred_element_type=F32)


def dot_columns(left, right):
    return lax.dot_general(left, right, (((0,), (0,)), ((), ())), preferred_element_type=F32)


def call(kernel, outs, scratch=(), cost=None, name=None, after=(), far=(), far_outs=0, limit=16):
    def run(*args):
        def body(*refs):
            count = len(args) + len(far)
            kernel(*refs[:count], *refs[count + len(after) :])

        near, outside = pl.BlockSpec(memory_space=pltpu.VMEM), pl.BlockSpec(memory_space=pl.ANY)
        specs = near
        if isinstance(outs, list):
            specs = [outside] * far_outs + [near] * (len(outs) - far_outs)
        return pl.pallas_call(
            body,
            out_shape=outs,
            in_specs=[near] * len(args) + [outside] * (len(far) + len(after)),
            out_specs=specs,
            scratch_shapes=scratch,
            name=name,
            cost_estimate=cost,
            compiler_params=pltpu.CompilerParams(vmem_limit_bytes=limit * 1024 * 1024),
        )(*args, *far, *after)

    return run


def cost(flops, moved):
    return pl.CostEstimate(flops=flops, bytes_accessed=moved, transcendentals=0)


def rim_rows(shape):
    row = lax.broadcasted_iota(jnp.int32, shape, 1)
    level = (row >= WLAT * TILE_LON).astype(jnp.int32)
    row = row - level * WLAT * TILE_LON
    lat = sum((row >= TILE_LON * count).astype(jnp.int32) for count in range(1, WLAT))
    lon = row - lat * TILE_LON
    line = level * MID_LAT + lat
    z_row = line * (TILE_LON - MID_LON) + lon - MID_LON
    d_row = RIM_Z + RIM_X + line * MID_LON + lon
    x_row = RIM_Z + (line - MID_LAT) * MID_LON + lon
    west = lon < MID_LON
    return jnp.where(
        lat < MID_LAT, jnp.where(west, d_row, z_row), jnp.where(west, x_row, -1)
    )


def pack_kernel(tokens, cotangent, rim_z, rim_x, rim_d, source, sems):
    core = lax.rem(lax.axis_index("head"), 2)
    pieces = sems.shape[0]
    rows = CELLS // pieces

    def load(array):
        copies = []
        for piece in range(pieces):
            part = pl.ds(piece * rows, rows)
            copies.append(pltpu.make_async_copy(array.at[part], source.at[part], sems.at[piece]))
        for copy in copies:
            copy.start()
        for copy in copies:
            copy.wait()

    pl.when(core == 0)(lambda: load(tokens))
    pl.when(core != 0)(lambda: load(cotangent))
    wanted = lax.broadcasted_iota(jnp.int32, (RIM, CELLS), 0) == rim_rows((RIM, CELLS))
    rim = dot(wanted.astype(F32).astype(BF16), source[...]).astype(BF16)
    rim_z[...] = rim[:RIM_Z]
    rim_x[...] = rim[RIM_Z : RIM_Z + RIM_SENT]
    rim_d[...] = rim[RIM_Z + RIM_X : RIM_Z + RIM_X + RIM_SENT]


def hold_kernel(rim, held):
    held[...] = rim[...]


def rims_kernel(x_rim, d_rim, rim):
    rim[...] = jnp.zeros_like(rim)
    rim[:RIM_SENT] = x_rim[...]
    rim[RIM_X : RIM_X + RIM_SENT] = d_rim[...]


def bias_kernel(table, bias, mark, padded, shifted, parts):
    mark[...] = jnp.zeros_like(mark)
    heads = bias.shape[0]
    width = shifted.shape[1]
    padded[...] = jnp.zeros_like(padded)
    padded[:heads, : table.shape[1]] = table[...]
    for head in range(heads):
        spread = jnp.broadcast_to(padded[head : head + 1, :], (16, padded.shape[1]))
        rolled = pltpu.roll(spread, 0, 1, stride=1, stride_axis=0)[:, :width]
        high = rolled.astype(BF16)
        rest = rolled - high.astype(F32)
        middle = rest.astype(BF16)
        low = (rest - middle.astype(F32)).astype(BF16)
        for split, value in enumerate((high, middle, low)):
            shifted[(head * 3 + split) * 16 : (head * 3 + split + 1) * 16, :] = value
    place = lax.broadcasted_iota(jnp.int32, (width, WINDOW), 0)
    count = LEV * WLAT * 16
    level_of, lat_of, lon_of = window_position((1, WINDOW), 1)
    plane = SPAN_LAT * SPAN_LON
    column = plane * (level_of + LEV - 1) + SPAN_LON * (lat_of + WLAT - 1) + lon_of + WLON - 1
    for level in range(LEV):
        for lat in range(WLAT):
            wanted = (place == column - (plane * level + SPAN_LON * lat)).astype(F32).astype(BF16)
            block = dot(shifted[...], wanted).astype(BF16)
            start = (level * WLAT + lat) * 16
            for head in range(heads):
                for split in range(3):
                    first = (head * 3 + split) * 16
                    parts[head, split * count + start : split * count + start + 16, :] = block[
                        first : first + 16
                    ]
    level_in, lat_in, lon_in = window_position((WINDOW, 1), 0)
    lane = lax.broadcasted_iota(jnp.int32, (WINDOW, 3 * count), 1)
    lane = lane - count * ((lane >= count).astype(jnp.int32) + (lane >= 2 * count).astype(jnp.int32))
    rows = (lane == (level_in * WLAT + lat_in) * 16 + lon_in).astype(F32).astype(BF16)
    last = lax.axis_index("lat") == lax.axis_size("lat") - 1
    south_in = (lat_in < MID_LAT).astype(jnp.int32)
    south_of = (lat_of < MID_LAT).astype(jnp.int32)
    added = jnp.where((south_in != south_of) & last, NEG_FILL, 0.0)
    for head in range(heads):
        bias[head] = dot(rows, parts[head]) + added


def scaled_rows(values):
    floats = values.astype(F32)
    center = floats - jnp.mean(floats, axis=-1, keepdims=True)
    inverse = lax.rsqrt(jnp.mean(center * center, axis=-1, keepdims=True) + EPSILON)
    return center * inverse, inverse


def attend(window, projected, d_attended, bias, merged, group):
    cells = slice(window * WINDOW, (window + 1) * WINDOW)
    scale = HEAD_DIM**-0.5
    heads = range(bias.shape[0])

    def part(head, kind):
        first = (3 * head + kind) * HEAD_DIM
        return projected[cells, first : first + HEAD_DIM]

    queries = [part(head, 0) * jnp.asarray(scale, BF16) for head in heads]
    keys = [part(head, 1) for head in heads]
    values = [part(head, 2) for head in heads]
    grads = [d_attended[cells, HEAD_DIM * head : HEAD_DIM * (head + 1)] for head in heads]
    scores = [dot_rows(keys[head], queries[head]) + bias[head] for head in heads]
    grad_probs = [dot_rows(values[head], grads[head]) for head in heads]
    halves, grad_scores = [], []
    for head in heads:
        raised = jnp.exp(scores[head] - jnp.max(scores[head], axis=0, keepdims=True))
        prob = raised * (1.0 / jnp.sum(raised, axis=0, keepdims=True))
        row_term = jnp.sum(prob * grad_probs[head], axis=0, keepdims=True)
        halves.append(prob.astype(BF16))
        grad_scores.append((prob * (grad_probs[head] - row_term)).astype(BF16))
    for head in heads:
        attended = dot_columns(halves[head], values[head])
        grad_value = dot(halves[head], grads[head])
        grad_query = dot_columns(grad_scores[head], keys[head]) * scale
        grad_key = dot(grad_scores[head], queries[head])
        merged[cells, HEAD_DIM * head : HEAD_DIM * (head + 1)] = attended.astype(BF16)
        first = group + 3 * HEAD_DIM * head
        merged[cells, first : first + 3 * HEAD_DIM] = jnp.concatenate(
            [grad_query, grad_key, grad_value], axis=1
        ).astype(BF16)


def lat_copies(whole, columns, out, lon_count, parity, sems, first):
    rows = whole.shape[0] // (4 * lon_count)
    copies = []
    for block in range(2 * lon_count):
        start = pl.multiple_of((2 * block + parity) * rows, rows)
        source, target = whole.at[pl.ds(start, rows), columns], out.at[pl.ds(block * rows, rows)]
        copies.append(pltpu.make_async_copy(source, target, sems.at[first + block]))
    return copies


def layer_kernel(
    tokens,
    cotangent,
    z_here,
    xd_here,
    z_there,
    xd_there,
    gain,
    w_out,
    bias,
    shift_pick,
    quarter,
    w_far,
    *refs,
):
    *by_lon, lat_keep, lat_send, stay, over, swap, part_tokens, part_cotangent = refs[:-13]
    source, near_tokens, near_grad, normed, projected, d_attended, merged = refs[-13:-6]
    ordered, terms, whole, w_qkv, load_sems, store_sems = refs[-6:]
    pieces = load_sems.shape[0]
    loads = []
    for piece in range(pieces):
        count = w_qkv.shape[0] // pieces
        part = pl.ds(piece * count, count)
        loads.append(
            pltpu.make_async_copy(w_far.at[part], w_qkv.at[part], load_sems.at[piece])
        )
        loads[-1].start()
    head_index = lax.axis_index("head")
    core = lax.rem(head_index, 2)
    heads = bias.shape[0]
    group = heads * HEAD_DIM
    split = CELLS + RIM_Z
    source[CELLS:split, :] = jnp.where(core == 0, z_here[...], z_there[...])
    source[split:, :] = jnp.where(core == 0, xd_here[...], xd_there[...])
    source[:CELLS, :] = tokens[...]
    near_tokens[...] = dot(shift_pick[...], source[...]).astype(BF16)
    source[CELLS:split, :] = jnp.where(core == 0, z_there[...], z_here[...])
    source[split:, :] = jnp.where(core == 0, xd_there[...], xd_here[...])
    source[:CELLS, :] = cotangent[...]
    near_grad[...] = dot(shift_pick[...], source[...]).astype(BF16)
    scaled, _ = scaled_rows(near_tokens[...])
    normed[...] = (scaled * gain[...]).astype(BF16)
    d_attended[...] = dot_rows(near_grad[...], w_out[...]).astype(BF16)
    for load in loads:
        load.wait()
    projected[...] = dot(normed[...], w_qkv[...]).astype(BF16)
    for window in range(WINDOWS):
        attend(window, projected, d_attended, bias, merged, group)
    whole[:, : 3 * group] = dot_columns(normed[...], merged[:, group:]).astype(BF16)
    whole[:, 3 * group :] = dot_columns(near_grad[...], merged[:, :group]).astype(BF16)
    lon, lon_count = lax.axis_index("lon"), len(by_lon)
    rows = by_lon[0].shape[0]
    stores = []
    for step, block in enumerate(by_lon):
        start = pl.multiple_of(lax.rem(lon + step, lon_count) * rows, rows)
        source_rows = whole.at[pl.ds(start, rows), pl.ds(0, 2 * group)]
        stores.append(pltpu.make_async_copy(source_rows, block, store_sems.at[step]))
    parity = lax.rem(lax.axis_index("lat"), 2)
    later = pl.ds(2 * group, 2 * group)
    stores += lat_copies(whole, later, lat_keep, lon_count, parity, store_sems, lon_count)
    stores += lat_copies(whole, later, lat_send, lon_count, 1 - parity, store_sems, 3 * lon_count)
    for store in stores:
        store.start()
    ordered[...] = dot(quarter[...], merged[...]).astype(BF16)
    terms[0] = dot(ordered[:, :group], w_out[...]).astype(BF16)
    terms[1] = dot_rows(ordered[:, group:], w_qkv[...]).astype(BF16)

    def term(owner):
        return terms[:, pl.ds(pl.multiple_of(owner * STRIDE, 16), PART), :]

    far = lax.rem(head_index + 2, QUARTERS)
    stay[...] = term(head_index)
    over[...] = term(far)
    swap[0] = term(head_index + 1 - 2 * core)
    swap[1] = term(far + 1 - 2 * core)
    mine = quarter[pl.ds(pl.multiple_of(head_index * STRIDE, 16), PART), :]
    part_tokens[...] = dot(mine, near_tokens[...]).astype(BF16)
    part_cotangent[...] = dot(mine, near_grad[...]).astype(BF16)
    for store in stores:
        store.wait()


def cores_kernel(over, swapped, total):
    total[...] = (over[...].astype(F32) + swapped[1].astype(F32)).astype(BF16)


def total_of(parts):
    total = parts[0].astype(F32)
    for part in parts[1:]:
        total = total + part.astype(F32)
    return total


def second_step_kernel(lon_count, *refs):
    from_lon, (lat_keep, from_lat) = refs[:lon_count], refs[lon_count : lon_count + 2]
    keep_first, send_first, *by_lon, mark = refs[lon_count + 2 :]
    mark[...] = jnp.zeros_like(mark)
    rows = keep_first.shape[0] // 2
    lon, parity = lax.axis_index("lon"), lax.rem(lax.axis_index("lat"), 2)
    for out, wanted in ((keep_first, parity), (send_first, 1 - parity)):
        for block in range(2):
            part = pl.ds(pl.multiple_of((2 * block + wanted) * rows, rows), rows)
            total = total_of([piece[part, :] for piece in from_lon])
            out[block * rows : (block + 1) * rows, :] = total.astype(out.dtype)
    for step, out in enumerate(by_lon):
        start = lax.rem(lon + step, lon_count) * 2 * rows
        part = pl.ds(pl.multiple_of(start, rows), 2 * rows)
        out[...] = total_of([lat_keep[part, :], from_lat[part, :]]).astype(out.dtype)


def third_step_kernel(keep_first, from_lat, *refs):
    from_lon, (keep, send, mark) = refs[:-3], refs[-3:]
    mark[...] = jnp.zeros_like(mark)
    rows = keep.shape[1]
    mine = lax.div(lax.axis_index("lat"), 2)
    for half, parts in enumerate(((keep_first, from_lat), from_lon)):
        for out, block in ((keep, mine), (send, 1 - mine)):
            part = pl.ds(pl.multiple_of(block * rows, rows), rows)
            out[half] = total_of([piece[part, :] for piece in parts]).astype(out.dtype)


def finish_kernel(group, flip, keep, arrived, grad_qkv, grad_out):
    grad_qkv[:, : 2 * group] = keep[0] + arrived[0].astype(F32)
    total = keep[1] + arrived[1].astype(F32)
    grad_qkv[:, 2 * group :] = total[:, :group]
    out = total[:, group:]
    grad_out[...] = out.T if flip else out


def norm_kernel(part_tokens, part_cotangent, gain, pick, stay, swapped, crossed, *refs):
    *outs, mark = refs
    mark[...] = jnp.zeros_like(mark)
    layer = part_tokens[...].astype(F32)
    attn = stay[0].astype(F32) + swapped[0, 0].astype(F32) + crossed[0].astype(F32)
    d_normed = stay[1].astype(F32) + swapped[0, 1].astype(F32) + crossed[1].astype(F32)
    scaled, inverse = scaled_rows(part_tokens[...])
    grad = d_normed * gain[...]
    mean_grad = jnp.mean(grad, axis=-1, keepdims=True)
    mean_mixed = jnp.mean(grad * scaled, axis=-1, keepdims=True)
    change = (grad - mean_grad - scaled * mean_mixed) * inverse
    for at, value in enumerate((layer + attn, part_cotangent[...].astype(F32) + change)):
        rows = dot(pick[...], value.astype(BF16)).astype(BF16)
        for start, out in zip(OUT_STARTS, outs):
            out[at] = rows[start : start + out.shape[1]]


def taken(count, source, spans):
    row = lax.broadcasted_iota(jnp.int32, (count, source.shape[0]), 0)
    column = lax.broadcasted_iota(jnp.int32, (count, source.shape[0]), 1)
    wanted = jnp.zeros((count, source.shape[0]), F32)
    for start, first, rows in spans:
        inside = (row >= start) & (row < start + rows)
        wanted = jnp.where(inside & (column == row + (first - start)), 1.0, wanted)
    return dot(wanted.astype(BF16), source)


def north_kernel(z_rows, x_rows, rows, mark):
    mark[...] = jnp.zeros_like(mark)
    _, north, east, corner = group_sizes()
    for at in range(2):
        total = taken(NORTH_ROWS, z_rows[at], [(0, 0, north)])
        total = total + taken(NORTH_ROWS, x_rows[at], [(north, east, corner)])
        rows[at] = total.astype(BF16)


def join_kernel(own, z_rows, x_rows, *pieces):
    stay, north, east, corner = group_sizes()
    for at in range(2):
        total = taken(PART, own[at], [(0, 0, stay)])
        spans = [(stay, 0, north), (stay + north + east, north, corner)]
        total = total + taken(PART, z_rows[at], spans)
        total = total + taken(PART, x_rows[at], [(stay + north, 0, east)])
        for number, piece in enumerate(pieces):
            rows = piece.shape[1]
            piece[at] = total[number * rows : (number + 1) * rows].astype(BF16)


def spread_kernel(pick, *refs):
    *arrived, layer, grad, mark, gathered = refs
    mark[...] = jnp.zeros_like(mark)
    head_index = lax.axis_index("head")
    sibling = 1 - 2 * lax.rem(head_index, 2)
    over = lax.rem(head_index + 2, QUARTERS)
    owners = (head_index, head_index + sibling, over, over + sibling)
    for at, out in enumerate((layer, grad)):
        for step, owner in enumerate(owners):
            for number in range(PIECES):
                start = pl.multiple_of((owner * PIECES + number) * SLOT, SLOT)
                gathered[at, pl.ds(start + SLOT - 16, 16), :] = jnp.zeros_like(gathered[at, :16, :])
                piece = arrived[step * PIECES + number][at]
                gathered[at, pl.ds(start, PART // PIECES), :] = piece
        out[...] = dot(pick[...], gathered[at]).astype(BF16)


def shaped(*shape, dtype=BF16):
    return jax.ShapeDtypeStruct(shape, dtype)


def rotated(value, axis, step):
    count = lax.axis_size(axis)
    return lax.ppermute(value, axis, [(i, (i + step) % count) for i in range(count)])


def moved(value, lat_step, lon_step):
    lon_count, lat_count = lax.axis_size("lon"), lax.axis_size("lat")
    pairs = []
    for lon in range(lon_count):
        for lat in range(lat_count):
            target = (lon + lon_step) % lon_count * lat_count + (lat + lat_step) % lat_count
            pairs.append((lon * lat_count + lat, target))
    return lax.ppermute(value, ("lon", "lat"), pairs)


def body(tokens, norm_gain, w_qkv, w_out, bias_table, cotangent):
    level_count, lat_cells, lon_cells, width = tokens.shape
    heads = bias_table.shape[1]
    group = w_out.shape[0]
    lon_count, lat_count = lax.axis_size("lon"), lax.axis_size("lat")
    flat_tokens = tokens.reshape(CELLS, width)
    flat_grad = cotangent.reshape(CELLS, width)
    gain = norm_gain.reshape(1, width)
    mark = shaped(8, 128, dtype=F32)
    rims = call(
        pack_kernel,
        [shaped(RIM_Z, width)] + [shaped(RIM_SENT, width)] * 2,
        [pltpu.VMEM((CELLS, width), BF16), pltpu.SemaphoreType.DMA((6,))],
        cost=cost(2 * RIM * CELLS * width, 4 * CELLS * width),
        name="pack_rims",
        far=tuple(
            pltpu.with_memory_space_constraint(array, pltpu.HBM)
            for array in (flat_tokens, flat_grad)
        ),
    )()
    arrived = [moved(rims[0], -1, 0), moved(rims[1], 0, -1), moved(rims[2], -1, -1)]
    bias, bias_mark = call(
        bias_kernel,
        [shaped(heads, WINDOW, WINDOW, dtype=F32), mark],
        [
            pltpu.VMEM((8, 1024), F32),
            pltpu.VMEM((heads * 48, 768), BF16),
            pltpu.VMEM((heads, 576, WINDOW), BF16),
        ],
        cost=cost(2 * 192 * 768 * 144 * 12 * 2, 1000000),
        name="window_bias",
    )(bias_table.T)
    held = call(
        hold_kernel, shaped(RIM_Z, width), name="hold_rim", cost=cost(0, 4 * RIM_Z * width), after=(bias_mark,)
    )(arrived[0])
    joined = call(
        rims_kernel,
        shaped(RIM_X + RIM_D, width),
        name="join_rims",
        cost=cost(0, 4 * (RIM_X + RIM_D) * width),
        after=(bias_mark,),
    )(*arrived[1:])
    rims = [held, joined]
    pairs = [(i, i ^ 1) for i in range(QUARTERS)]
    rims += [lax.ppermute(rim, "head", pairs) for rim in rims]
    lon_rows = width // lon_count
    rows = lon_rows // lat_count
    columns = 2 * group
    *by_lon, lat_keep, lat_send, stay, over, swap, part_tokens, part_cotangent = call(
        layer_kernel,
        [shaped(lon_rows, columns)] * lon_count
        + [shaped(2 * lon_count * rows, columns)] * 2
        + [shaped(2, PART, width)] * 2
        + [shaped(2, 2, PART, width)]
        + [shaped(PART, width)] * 2,
        [
            pltpu.VMEM((CELLS + RIM, width), BF16),
            pltpu.VMEM((CELLS, width), BF16),
            pltpu.VMEM((CELLS, width), BF16),
            pltpu.VMEM((CELLS, width), BF16),
            pltpu.VMEM((CELLS, 3 * group), BF16),
            pltpu.VMEM((CELLS, group), BF16),
            pltpu.VMEM((CELLS, 4 * group), BF16),
            pltpu.VMEM((QUARTERS * STRIDE, 4 * group), BF16),
            pltpu.VMEM((2, QUARTERS * STRIDE, width), BF16),
            pltpu.VMEM((width, 4 * group), BF16),
            pltpu.VMEM((width, 3 * group), BF16),
            pltpu.SemaphoreType.DMA((4,)),
            pltpu.SemaphoreType.DMA((5 * lon_count,)),
        ],
        cost=cost(6 * CELLS * width * width, 8000000),
        name="window_layer",
        far=(w_qkv,),
        far_outs=lon_count + 2,
        limit=32,
    )(
        flat_tokens,
        flat_grad,
        *rims,
        gain,
        w_out,
        bias,
        one_hot(shifted_source(), CELLS + RIM),
        quarter_pick(),
    )
    from_lon = [by_lon[0]] + [rotated(by_lon[step], "lon", step) for step in range(1, lon_count)]
    neighbours = [(i, i ^ 1) for i in range(lat_count)]
    from_lat = lax.ppermute(lat_send, "lat", neighbours)
    swapped = lax.ppermute(swap, "head", pairs)
    across = call(
        cores_kernel, shaped(2, PART, width), cost=cost(0, 8 * PART * width), name="sum_over_cores"
    )(over, swapped)
    chips = [(i, i ^ 2) for i in range(QUARTERS)]
    crossed = lax.ppermute(across, "head", chips)
    *pieces, norm_mark = call(
        norm_kernel,
        [shaped(2, count, width) for count in OUT_SIZES] + [mark],
        cost=cost(2 * 2 * OUT_ROWS * PART * width, 12 * PART * width),
        name="sum_over_heads",
    )(part_tokens, part_cotangent, gain, group_pick(), stay, swapped, crossed)
    keep_first, send_first, *by_lon, second_mark = call(
        functools.partial(second_step_kernel, lon_count),
        [shaped(2 * rows, columns, dtype=F32), shaped(2 * rows, columns)]
        + [shaped(2 * rows, columns, dtype=F32)]
        + [shaped(2 * rows, columns)] * (lon_count - 1)
        + [mark],
        cost=cost(4 * lon_rows * columns, 6 * lon_rows * columns),
        name="second_step",
        after=(norm_mark,),
    )(*from_lon, lat_keep, from_lat)
    from_lat = lax.ppermute(send_first, "lat", neighbours)
    from_lon = [by_lon[0]] + [rotated(by_lon[step], "lon", step) for step in range(1, lon_count)]
    from_west = rotated(pieces[2], "lon", 1)
    to_north, north_mark = call(
        north_kernel,
        [shaped(2, NORTH_ROWS, width), mark],
        cost=cost(0, 8 * NORTH_ROWS * width),
        name="rows_for_north",
        after=(second_mark,),
    )(pieces[1], from_west)
    home = [pieces[0], rotated(to_north, "lat", 1), from_west]
    keep, send, third_mark = call(
        third_step_kernel,
        [shaped(2, rows, columns, dtype=F32), shaped(2, rows, columns), mark],
        cost=cost(4 * rows * columns, 6 * rows * columns),
        name="third_step",
        after=(north_mark,),
    )(keep_first, from_lat, *from_lon)
    last = lax.ppermute(send, "lat", [(i, i ^ 2) for i in range(lat_count)])
    each = call(
        join_kernel,
        [shaped(2, PART // PIECES, width)] * PIECES,
        cost=cost(2 * 2 * OUT_ROWS * PART * width, 8 * OUT_ROWS * width),
        name="join_home",
        after=(third_mark,),
    )(*home)
    far = [lax.ppermute(single, "head", chips) for single in each]
    near = [lax.ppermute(single, "head", pairs) for single in each]
    across = [lax.ppermute(single, "head", pairs) for single in far]
    layer_out, grad_tokens, spread_mark = call(
        spread_kernel,
        [shaped(CELLS, width)] * 2 + [mark],
        [pltpu.VMEM((2, QUARTERS * PIECES * SLOT, width), BF16)],
        cost=cost(2 * 2 * CELLS * CELLS * width, 8 * CELLS * width),
        name="spread_outputs",
    )(own_pick(), *each, *near, *far, *across)
    flip = rows % 128 == 0
    grad_qkv, grad_out = call(
        functools.partial(finish_kernel, group, flip),
        [
            shaped(rows, 3 * group, dtype=F32),
            shaped(*((group, rows) if flip else (rows, group)), dtype=F32),
        ],
        cost=cost(4 * rows * 4 * group, 16 * rows * 4 * group),
        name="sum_over_lat",
        after=(spread_mark,),
    )(keep, last)
    return (
        layer_out.reshape(tokens.shape),
        grad_tokens.reshape(tokens.shape),
        grad_qkv,
        grad_out if flip else grad_out.T,
    )


def solution(mesh):
    in_specs = (
        P(None, "lat", "lon", None),
        P(),
        P(None, "head"),
        P("head", None),
        P(None, "head"),
        P(None, "lat", "lon", None),
    )
    out_specs = (
        P(None, "lat", "lon", None),
        P(None, "lat", "lon", None),
        P(("lon", "lat"), "head"),
        P("head", ("lon", "lat")),
    )
    return jax.shard_map(body, mesh=mesh, in_specs=in_specs, out_specs=out_specs, check_vma=False)
```
